32 devices in a mesh: band: 16 (over z, y, x), grp: 2 (over core).
Axes of the slice: x: 2, y: 2, z: 4, core: 2. Of those that a mesh axis runs over, the one named last changes fastest.
Arguments:
- tokens: bfloat16 [2, 2048, 1024], P('grp', 'band'), may hold values from -6 to 6
- segment_ids: int32 [2, 2048], P('grp', 'band'), may hold values from 0 to 3, as said below
- lead_index: int32 [2, 4], P('grp'), may hold values from 0 to 15
- lead_table: bfloat16 [16, 1024], P(None, ('band', 'grp')), may hold values from -3 to 3
- ln1_gain: bfloat16 [1024], P(('band', 'grp')), may hold values from 0.25 to 1.75
- ln1_bias: bfloat16 [1024], P(('band', 'grp')), may hold values from -1.5 to 1.5
- qkv_weight: bfloat16 [1024, 3072], P(('band', 'grp')), may hold values from -0.25 to 0.25
- q_bias: bfloat16 [1024], P(('band', 'grp')), may hold values from -1.5 to 1.5
- v_bias: bfloat16 [1024], P(('band', 'grp')), may hold values from -1.5 to 1.5
- out_weight: bfloat16 [1024, 1024], P(('band', 'grp')), may hold values from -0.75 to 0.75
- out_bias: bfloat16 [1024], P(('band', 'grp')), may hold values from -1 to 1
- ln2_gain: bfloat16 [1024], P(('band', 'grp')), may hold values from 0.25 to 1.75
- ln2_bias: bfloat16 [1024], P(('band', 'grp')), may hold values from -1.5 to 1.5
- up_weight: bfloat16 [1024, 4096], P(('band', 'grp')), may hold values from -0.1875 to 0.1875
- up_bias: bfloat16 [4096], P(('band', 'grp')), may hold values from -2.5 to 2.5
- down_weight: bfloat16 [4096, 1024], P(('band', 'grp')), may hold values from -0.125 to 0.125
- down_bias: bfloat16 [1024], P(('band', 'grp')), may hold values from -1 to 1
- d_out: bfloat16 [2, 2048, 1024], P('grp', 'band'), may hold values from -6 to 6
Outputs:
- layer_out: bfloat16 [2, 2048, 1024], P('grp', 'band')
- d_tokens: float32 [2, 2048, 1024], P('grp', 'band')
- d_lead_table: float32 [16, 1024], P(None, ('band', 'grp'))
- d_ln1_gain: float32 [1024], P(('band', 'grp'))
- d_ln1_bias: float32 [1024], P(('band', 'grp'))
- d_qkv_weight: float32 [1024, 3072], P(('band', 'grp'))
- d_q_bias: float32 [1024], P(('band', 'grp'))
- d_v_bias: float32 [1024], P(('band', 'grp'))
- d_out_weight: float32 [1024, 1024], P(('band', 'grp'))
- d_out_bias: float32 [1024], P(('band', 'grp'))
- d_ln2_gain: float32 [1024], P(('band', 'grp'))
- d_ln2_bias: float32 [1024], P(('band', 'grp'))
- d_up_weight: float32 [1024, 4096], P(('band', 'grp'))
- d_up_bias: float32 [4096], P(('band', 'grp'))
- d_down_weight: float32 [4096, 1024], P(('band', 'grp'))
- d_down_bias: float32 [1024], P(('band', 'grp'))
The draws below stay inside these ranges and needn't reach their ends.
Inputs may be any that keep to these rules, and one draw needn't show every extreme that they name: `segment_ids`: A group holds either one sample (every id 0) or 4 samples; each of the 4 samples fills one equal run of 32 rows of every device's 128 rows, the runs holding the ids in an order drawn from the seed for each group; every latitude band of a group holds the same ids in the same order; max(1, 0) groups, which ones drawn from the seed, hold one sample.
All inputs are finite; a program needn't handle non-finite values.
Results may differ from the reference program's by a relative error of at most 0.017.
Values may be sent and summed in bfloat16 or wider, within the bound.
No kernel may reach another device: no remote copies, remote signals or barrier semaphores. Data moves between devices by JAX's collectives and lax.ppermute only.
A program may use at most 192 MiB of HBM per device.

```python
import math
import jax
import jax.numpy as jnp
from jax import lax

D = 1024
HEADS = 16
HEAD_DIM = 64
FF = 4096
TOK_DEV = 128
SEGS = 4
LEADS = 16
GROUPS = 2
GROUP_TOK = 2048


def draw_segment_ids(key, part):
    key = jax.random.fold_in(key, 7)
    single_key = jax.random.fold_in(key, 1)
    order_key = jax.random.fold_in(key, 2)
    single_count = max(1, GROUPS // 4)
    order = jax.random.permutation(single_key, GROUPS)
    single = order < single_count
    slot_orders = jax.vmap(lambda one_key: jax.random.permutation(one_key, SEGS))(jax.random.split(order_key, GROUPS)).astype(jnp.int32)
    row_index = jnp.arange(TOK_DEV, dtype=jnp.int32)
    slot_ids = row_index // (TOK_DEV // SEGS)
    placed = jnp.take(slot_orders, slot_ids, axis=1)
    block_ids = jnp.where(single[:, None], 0, placed)
    return jnp.tile(block_ids, (1, GROUP_TOK // TOK_DEV)).astype(jnp.int32)


def plant(values, key, least, high):
    spot = [jax.random.randint(jax.random.fold_in(key, axis), (), 0, length) for axis, length in enumerate(values.shape)]
    longest = values.shape.index(max(values.shape))
    neighbour = spot[:longest] + [(spot[longest] + 1) % values.shape[longest]] + spot[longest + 1:]
    return values.at[tuple(spot)].set(least).at[tuple(neighbour)].set(high)


def block_levels(key, extent, cuts, low, high):
    loudness = 1.0
    for position, shards_of in cuts:
        steps = jax.random.uniform(jax.random.fold_in(jax.random.fold_in(key, 6), position), (shards_of,), jnp.float32, low / len(cuts), high / len(cuts))
        loudness = loudness * jnp.repeat(jnp.exp(steps), extent[position] // shards_of).reshape((-1,) + (1,) * (len(extent) - 1 - position))
    return loudness


def noise(key, shape, width, reach, pieces=(), held_as=jnp.bfloat16):
    level = block_levels(key, shape, pieces, -0.22, 0.18) if pieces else 1.0
    drawn = jax.random.normal(key, shape, jnp.float32) * width * level
    return jnp.minimum(jnp.maximum(drawn, -reach), reach).astype(held_as)


def setup_inputs(seed: int = 0) -> dict:
    streams_of = jax.random.split(jax.random.key(seed), 19)
    tokens = noise(streams_of[0], (GROUPS, GROUP_TOK, D), 1.0, 6.0, ((0, 2), (1, 16)))
    segment_ids = draw_segment_ids(jax.random.fold_in(streams_of[18], 71), 0)
    lead_index = plant(jax.random.randint(streams_of[2], (GROUPS, SEGS), 0, LEADS), jax.random.fold_in(streams_of[2], 1), 0, LEADS - 1).astype(jnp.int32)
    lead_table = noise(streams_of[3], (LEADS, D), 0.5, 3.0, ((1, 32),))
    ln1_gain = jnp.clip(1.0 + 0.15 * jax.random.normal(streams_of[4], (D,), jnp.float32), 0.25, 1.75).astype(jnp.bfloat16)
    ln1_bias = noise(streams_of[5], (D,), 0.3, 1.5, ((0, 32),))
    qkv_weight = noise(streams_of[6], (D, 3 * D), (D // 2) ** -0.5, 0.25, ((0, 32),))
    q_bias = noise(streams_of[7], (D,), 0.3, 1.5, ((0, 32),))
    v_bias = noise(streams_of[8], (D,), 0.3, 1.5, ((0, 32),))
    out_weight = noise(streams_of[9], (D, D), 64 ** -0.5, 0.75, ((0, 32),))
    out_bias = noise(streams_of[10], (D,), 0.2, 1.0, ((0, 32),))
    ln2_gain = jnp.clip(1.0 + 0.15 * jax.random.normal(streams_of[11], (D,), jnp.float32), 0.25, 1.75).astype(jnp.bfloat16)
    ln2_bias = noise(streams_of[12], (D,), 0.3, 1.5, ((0, 32),))
    up_weight = noise(streams_of[13], (D, FF), D ** -0.5, 0.1875, ((0, 32),))
    up_bias = noise(streams_of[14], (FF,), 0.5, 2.5, ((0, 32),))
    down_weight = noise(streams_of[15], (FF, D), (FF // 2) ** -0.5, 0.125, ((0, 32),))
    down_bias = noise(streams_of[16], (D,), 0.2, 1.0, ((0, 32),))
    d_out = noise(streams_of[17], (GROUPS, GROUP_TOK, D), 1.0, 6.0, ((0, 2), (1, 16)))
    return {"tokens": tokens, "segment_ids": segment_ids, "lead_index": lead_index, "lead_table": lead_table, "ln1_gain": ln1_gain, "ln1_bias": ln1_bias, "qkv_weight": qkv_weight, "q_bias": q_bias, "v_bias": v_bias, "out_weight": out_weight, "out_bias": out_bias, "ln2_gain": ln2_gain, "ln2_bias": ln2_bias, "up_weight": up_weight, "up_bias": up_bias, "down_weight": down_weight, "down_bias": down_bias, "d_out": d_out}


epsilon = 1e-05
score_scale = 0.125
highest = lax.Precision.HIGHEST

@jax.custom_vjp
def low(v):
    return lax.optimization_barrier(v.astype(jnp.bfloat16)).astype(jnp.float32)

@jax.custom_vjp
def low_back(v):
    return v

def low_keep(v):
    return (low(v), None)

def low_pass(kept, grad):
    return (grad,)

def back_keep(v):
    return (v, None)

def back_low(kept, grad):
    return (low(grad),)
low.defvjp(low_keep, low_pass)
low_back.defvjp(back_keep, back_low)

def norm_rows(values, norm_gain, norm_bias):
    row_mean = lax.optimization_barrier(jnp.mean(values, -1, keepdims=True))
    centred = values - row_mean
    row_var = lax.optimization_barrier(jnp.mean(centred * centred, -1, keepdims=True))
    return centred * lax.rsqrt(row_var + epsilon) * norm_gain + norm_bias

def matmul(left, right):
    return jnp.dot(left, right, precision=highest, preferred_element_type=jnp.float32)

def forward_group(params, group_rows, group_seg, group_leads):
    lead_table, ln1_gain, ln1_bias, qkv_weight, q_bias, v_bias, out_weight, out_bias, ln2_gain, ln2_bias, up_weight, up_bias, down_weight, down_bias = params
    features = group_rows.shape[1]
    length = group_rows.shape[0]
    embedded = group_rows + lead_table[group_leads[group_seg]]
    normed = low(norm_rows(embedded, ln1_gain, ln1_bias))
    projected = matmul(normed, qkv_weight)
    queries = low(low_back(projected[:, :features] + q_bias))
    key_rows = low(low_back(projected[:, features:2 * features]))
    value_rows = low(low_back(projected[:, 2 * features:] + v_bias))
    key_heads = key_rows.reshape(length, HEADS, HEAD_DIM)
    value_heads = value_rows.reshape(length, HEADS, HEAD_DIM)
    block_len = math.gcd(length, 512)

    def attend(block_pair):
        query_block, seg_block = block_pair
        scores = low_back(score_scale * jnp.einsum('qhd,khd->hqk', query_block, key_heads, precision=highest))
        allowed = seg_block[:, None] == group_seg[None, :]
        scores = jnp.where(allowed[None], scores, -1e+30)
        attn_weights = low(jax.nn.softmax(scores, axis=-1))
        return jnp.einsum('hqk,khd->qhd', attn_weights, value_heads, precision=highest)
    attended = lax.map(jax.checkpoint(attend), (queries.reshape(length // block_len, block_len, HEADS, HEAD_DIM), group_seg.reshape(length // block_len, block_len)))
    attended = low(low_back(attended.reshape(length, features)))
    middle = embedded + low_back(matmul(attended, out_weight) + out_bias)
    normed_two = low(norm_rows(middle, ln2_gain, ln2_bias))
    hidden = low_back(matmul(normed_two, up_weight) + up_bias)
    activated = low(jax.nn.gelu(hidden, approximate=False))
    return middle + low_back(matmul(activated, down_weight) + down_bias)

def reference(tokens, segment_ids, lead_index, lead_table, ln1_gain, ln1_bias, qkv_weight, q_bias, v_bias, out_weight, out_bias, ln2_gain, ln2_bias, up_weight, up_bias, down_weight, down_bias, d_out):
    params = tuple((member.astype(jnp.float32) for member in (lead_table, ln1_gain, ln1_bias, qkv_weight, q_bias, v_bias, out_weight, out_bias, ln2_gain, ln2_bias, up_weight, up_bias, down_weight, down_bias)))

    def whole_layer(token_rows, weight_set):

        def group_step(group_data):
            return forward_group(weight_set, group_data[0], group_data[1], group_data[2])
        return lax.map(group_step, (token_rows, segment_ids, lead_index))
    outputs, backward = jax.vjp(whole_layer, tokens.astype(jnp.float32), params)
    d_rows, d_weights = backward(d_out.astype(jnp.float32))
    d_lead, d_gain_one, d_shift_one, d_project, d_query_shift, d_value_shift, d_out_proj, d_out_shift, d_gain_two, d_shift_two, d_up, d_up_shift, d_down, d_down_shift = d_weights
    return (outputs.astype(jnp.bfloat16), d_rows, d_lead, d_gain_one, d_shift_one, d_project, d_query_shift, d_value_shift, d_out_proj, d_out_shift, d_gain_two, d_shift_two, d_up, d_up_shift, d_down, d_down_shift)
```

```python
import functools
import math

import jax
import jax.numpy as jnp
from jax import lax
from jax.experimental import pallas as pl
from jax.experimental.pallas import tpu as pltpu
from jax.sharding import Mesh
from jax.sharding import PartitionSpec as P

bf16, f32 = jnp.bfloat16, jnp.float32

HEADS = 16


epsilon = 1e-05
score_scale = 0.125
masked_score = -1e30


def norm_rows(values, norm_gain, norm_bias):
    row_mean = jnp.mean(values, -1, keepdims=True)
    centred = values - row_mean
    row_var = jnp.mean(centred * centred, -1, keepdims=True)
    return centred * lax.rsqrt(row_var + epsilon) * norm_gain + norm_bias


def gelu_exact(values):
    return jax.nn.gelu(values, approximate=False)


def split_blocks(values, block_rows):
    return values.reshape((values.shape[0] // block_rows, block_rows) + values.shape[1:])


def block_scores(query_heads, key_heads, allowed):
    raw_scores = (
        jnp.einsum("qhd,khd->hqk", query_heads, key_heads, preferred_element_type=jnp.float32)
        * score_scale
    )
    return jnp.where(allowed[None], raw_scores, masked_score)


def softmax_rows(query_heads, key_heads, allowed, log_total):
    scores = block_scores(query_heads, key_heads, allowed)
    return jnp.where(allowed[None], jnp.exp(scores - log_total[:, :, None]), 0.0)


def score_grads(query_heads, key_heads, value_heads, d_heads, allowed, log_total, row_delta):
    soft_rows = softmax_rows(query_heads, key_heads, allowed, log_total)
    d_soft = jnp.einsum("qhd,khd->hqk", d_heads, value_heads, preferred_element_type=jnp.float32)
    d_scores = (soft_rows * (d_soft - row_delta[:, :, None])).astype(jnp.bfloat16)
    return (soft_rows.astype(jnp.bfloat16), d_scores)


def local(
    tokens,
    segment_ids,
    lead_index,
    lead_table,
    ln1_gain,
    ln1_bias,
    qkv_weight,
    q_bias,
    v_bias,
    out_weight,
    out_bias,
    ln2_gain,
    ln2_bias,
    up_weight,
    up_bias,
    down_weight,
    down_bias,
    d_out,
):
    (
        table_full,
        first_gain,
        first_shift,
        project_full,
        query_shift,
        value_shift,
        out_full,
        out_shift,
        second_gain,
        second_shift,
        up_full,
        up_shift,
        down_full,
        down_shift,
    ) = (
        lax.all_gather(lead_table, ("band", "grp"), axis=1, tiled=True),
        lax.all_gather(ln1_gain, ("band", "grp"), axis=0, tiled=True),
        lax.all_gather(ln1_bias, ("band", "grp"), axis=0, tiled=True),
        lax.all_gather(qkv_weight, ("band", "grp"), axis=0, tiled=True),
        lax.all_gather(q_bias, ("band", "grp"), axis=0, tiled=True),
        lax.all_gather(v_bias, ("band", "grp"), axis=0, tiled=True),
        lax.all_gather(out_weight, ("band", "grp"), axis=0, tiled=True),
        lax.all_gather(out_bias, ("band", "grp"), axis=0, tiled=True),
        lax.all_gather(ln2_gain, ("band", "grp"), axis=0, tiled=True),
        lax.all_gather(ln2_bias, ("band", "grp"), axis=0, tiled=True),
        lax.all_gather(up_weight, ("band", "grp"), axis=0, tiled=True),
        lax.all_gather(up_bias, ("band", "grp"), axis=0, tiled=True),
        lax.all_gather(down_weight, ("band", "grp"), axis=0, tiled=True),
        lax.all_gather(down_bias, ("band", "grp"), axis=0, tiled=True),
    )
    tok_rows = tokens.shape[1]
    features = tokens.shape[2]
    head_dim = features // HEADS
    band_count = lax.axis_size("band")
    group_rows = tok_rows * band_count
    block_rows = math.gcd(group_rows, 1024)
    own_segments = segment_ids[0]
    group_segments = jnp.tile(own_segments, band_count)
    sample_count = lead_index.shape[1]
    lead_count = lead_table.shape[0]
    sample_hot = (
        own_segments[:, None] == jnp.arange(sample_count, dtype=jnp.int32)[None, :]
    ).astype(jnp.float32)
    lead_hot = (lead_index[0][:, None] == jnp.arange(lead_count, dtype=jnp.int32)[None, :]).astype(
        jnp.float32
    )
    lead_pick = jnp.dot(sample_hot, lead_hot, precision=lax.Precision.HIGHEST)
    embedded = tokens[0].astype(jnp.float32) + jnp.dot(
        lead_pick.astype(jnp.bfloat16), table_full, preferred_element_type=jnp.float32
    )
    normed_first = norm_rows(
        embedded, first_gain.astype(jnp.float32), first_shift.astype(jnp.float32)
    ).astype(jnp.bfloat16)
    projected = jnp.dot(normed_first, project_full, preferred_element_type=jnp.float32)
    query_rows = (projected[:, :features] + query_shift.astype(jnp.float32)).astype(jnp.bfloat16)
    key_rows = projected[:, features : 2 * features].astype(jnp.bfloat16)
    value_rows = (projected[:, 2 * features :] + value_shift.astype(jnp.float32)).astype(
        jnp.bfloat16
    )
    key_all, value_all = (
        lax.all_gather(key_rows, "band", axis=0, tiled=True),
        lax.all_gather(value_rows, "band", axis=0, tiled=True),
    )
    query_heads = query_rows.reshape(tok_rows, HEADS, head_dim)
    key_blocks = split_blocks(key_all.reshape(group_rows, HEADS, head_dim), block_rows)
    value_blocks = split_blocks(value_all.reshape(group_rows, HEADS, head_dim), block_rows)
    segment_blocks = split_blocks(group_segments, block_rows)

    def stats_step(running, block_data):
        running_max, running_sum = running
        key_block, key_segments = block_data
        allowed = own_segments[:, None] == key_segments[None, :]
        scores = block_scores(query_heads, key_block, allowed)
        new_max = jnp.maximum(running_max, jnp.max(scores, -1))
        block_sum = jnp.sum(
            jnp.where(allowed[None], jnp.exp(scores - new_max[:, :, None]), 0.0), -1
        )
        return ((new_max, running_sum * jnp.exp(running_max - new_max) + block_sum), None)

    start_max = jnp.full((HEADS, tok_rows), masked_score, jnp.float32)
    start_sum = jnp.zeros((HEADS, tok_rows), jnp.float32)
    (final_max, final_sum), unused_out = lax.scan(
        stats_step, (start_max, start_sum), (key_blocks, segment_blocks)
    )
    log_total = final_max + jnp.log(final_sum)

    def output_step(running, block_data):
        high_part, low_part = running
        key_block, value_block, key_segments = block_data
        allowed = own_segments[:, None] == key_segments[None, :]
        soft_rows = softmax_rows(query_heads, key_block, allowed, log_total)
        soft_low = soft_rows.astype(jnp.bfloat16)
        soft_rest = (soft_rows - soft_low.astype(jnp.float32)).astype(jnp.bfloat16)
        high_part = high_part + jnp.einsum(
            "hqk,khd->qhd", soft_low, value_block, preferred_element_type=jnp.float32
        )
        low_part = low_part + jnp.einsum(
            "hqk,khd->qhd", soft_rest, value_block, preferred_element_type=jnp.float32
        )
        return ((high_part, low_part), None)

    empty_heads = jnp.zeros((tok_rows, HEADS, head_dim), jnp.float32)
    (attn_high, attn_low), unused_out = lax.scan(
        output_step, (empty_heads, empty_heads), (key_blocks, value_blocks, segment_blocks)
    )
    attended = attn_high.reshape(tok_rows, features).astype(jnp.bfloat16)
    middle = (
        embedded
        + jnp.dot(attended, out_full, preferred_element_type=jnp.float32)
        + out_shift.astype(jnp.float32)
    )
    normed_second = norm_rows(
        middle, second_gain.astype(jnp.float32), second_shift.astype(jnp.float32)
    ).astype(jnp.bfloat16)
    hidden = jnp.dot(normed_second, up_full, preferred_element_type=jnp.float32) + up_shift.astype(
        jnp.float32
    )
    activated = gelu_exact(hidden).astype(jnp.bfloat16)
    result = (
        middle
        + jnp.dot(activated, down_full, preferred_element_type=jnp.float32)
        + down_shift.astype(jnp.float32)
    )
    layer_out = result.astype(jnp.bfloat16)[None]
    first_gain_back, project_back, out_back, second_gain_back, up_back, down_back = (
        lax.all_gather(ln1_gain, ("band", "grp"), axis=0, tiled=True),
        lax.all_gather(qkv_weight, ("band", "grp"), axis=0, tiled=True),
        lax.all_gather(out_weight, ("band", "grp"), axis=0, tiled=True),
        lax.all_gather(ln2_gain, ("band", "grp"), axis=0, tiled=True),
        lax.all_gather(up_weight, ("band", "grp"), axis=0, tiled=True),
        lax.all_gather(down_weight, ("band", "grp"), axis=0, tiled=True),
    )
    d_rows = d_out[0]
    d_down_shift = jnp.sum(d_rows.astype(jnp.float32), 0)
    d_down = jnp.einsum("tf,td->fd", activated, d_rows, preferred_element_type=jnp.float32)
    d_act = jnp.einsum("td,fd->tf", d_rows, down_back, preferred_element_type=jnp.float32)
    unused_gelu, gelu_back = jax.vjp(gelu_exact, hidden)
    d_hidden = gelu_back(d_act)[0].astype(jnp.bfloat16)
    d_up_shift = jnp.sum(d_hidden.astype(jnp.float32), 0)
    d_up = jnp.einsum("td,tf->df", normed_second, d_hidden, preferred_element_type=jnp.float32)
    d_normed_second = jnp.einsum("tf,df->td", d_hidden, up_back, preferred_element_type=jnp.float32)
    unused_second, second_back = jax.vjp(
        norm_rows, middle, second_gain_back.astype(jnp.float32), second_shift.astype(jnp.float32)
    )
    d_middle_part, d_gain_second, d_shift_second = second_back(d_normed_second)
    d_middle = d_rows.astype(jnp.float32) + d_middle_part
    d_branch = d_middle.astype(jnp.bfloat16)
    d_out_shift = jnp.sum(d_branch.astype(jnp.float32), 0)
    d_out_full = jnp.einsum("ti,to->io", attended, d_branch, preferred_element_type=jnp.float32)
    d_attended = jnp.einsum(
        "to,io->ti", d_branch, out_back, preferred_element_type=jnp.float32
    ).astype(jnp.bfloat16)
    d_heads = d_attended.reshape(tok_rows, HEADS, head_dim)
    row_delta = jnp.sum(d_heads.astype(jnp.float32) * (attn_high + attn_low), -1).T

    def query_grad(d_query_acc, key_block, value_block, key_segments):
        allowed = own_segments[:, None] == key_segments[None, :]
        soft_low, d_scores = score_grads(
            query_heads, key_block, value_block, d_heads, allowed, log_total, row_delta
        )
        d_query_acc = d_query_acc + jnp.einsum(
            "hqk,khd->qhd", d_scores, key_block, preferred_element_type=jnp.float32
        )
        return (d_query_acc, soft_low, d_scores)

    def owner_step(d_query_acc, block_data):
        key_block, value_block, key_segments = block_data
        d_query_acc, soft_low, d_scores = query_grad(
            d_query_acc, key_block, value_block, key_segments
        )
        d_key_block = (
            jnp.einsum("hqk,qhd->khd", d_scores, query_heads, preferred_element_type=jnp.float32)
            * score_scale
        )
        d_value_block = jnp.einsum(
            "hqk,qhd->khd", soft_low, d_heads, preferred_element_type=jnp.float32
        )
        return (d_query_acc, (d_key_block, d_value_block))

    d_query_sum, (d_key_parts, d_value_parts) = lax.scan(
        owner_step, empty_heads, (key_blocks, value_blocks, segment_blocks)
    )
    d_key_sum, d_value_sum = (
        lax.psum_scatter(
            d_key_parts.reshape(group_rows, features).astype(jnp.bfloat16),
            "band",
            scatter_dimension=0,
            tiled=True,
        ).astype(jnp.float32),
        lax.psum_scatter(
            d_value_parts.reshape(group_rows, features).astype(jnp.bfloat16),
            "band",
            scatter_dimension=0,
            tiled=True,
        ).astype(jnp.float32),
    )
    d_query = (d_query_sum.reshape(tok_rows, features) * score_scale).astype(jnp.bfloat16)
    d_key = d_key_sum.astype(jnp.bfloat16)
    d_value = d_value_sum.astype(jnp.bfloat16)
    d_query_shift = jnp.sum(d_query.astype(jnp.float32), 0)
    d_value_shift = jnp.sum(d_value.astype(jnp.float32), 0)
    d_project_rows = jnp.concatenate([d_query, d_key, d_value], 1)
    d_project = jnp.einsum(
        "ti,to->io", normed_first, d_project_rows, preferred_element_type=jnp.float32
    )
    d_normed_first = jnp.einsum(
        "to,io->ti", d_project_rows, project_back, preferred_element_type=jnp.float32
    )
    unused_first, first_back = jax.vjp(
        norm_rows, embedded, first_gain_back.astype(jnp.float32), first_shift.astype(jnp.float32)
    )
    d_embed_part, d_gain_first, d_shift_first = first_back(d_normed_first)
    d_embedded = d_middle + d_embed_part
    d_table = jnp.einsum("tl,td->ld", lead_pick, d_embedded, precision=lax.Precision.HIGHEST)
    shards = (
        lax.psum_scatter(d_table, ("band", "grp"), scatter_dimension=1, tiled=True),
        lax.psum_scatter(d_gain_first, ("band", "grp"), scatter_dimension=0, tiled=True),
        lax.psum_scatter(d_shift_first, ("band", "grp"), scatter_dimension=0, tiled=True),
        lax.psum_scatter(d_project, ("band", "grp"), scatter_dimension=0, tiled=True),
        lax.psum_scatter(d_query_shift, ("band", "grp"), scatter_dimension=0, tiled=True),
        lax.psum_scatter(d_value_shift, ("band", "grp"), scatter_dimension=0, tiled=True),
        lax.psum_scatter(d_out_full, ("band", "grp"), scatter_dimension=0, tiled=True),
        lax.psum_scatter(d_out_shift, ("band", "grp"), scatter_dimension=0, tiled=True),
        lax.psum_scatter(d_gain_second, ("band", "grp"), scatter_dimension=0, tiled=True),
        lax.psum_scatter(d_shift_second, ("band", "grp"), scatter_dimension=0, tiled=True),
        lax.psum_scatter(d_up, ("band", "grp"), scatter_dimension=0, tiled=True),
        lax.psum_scatter(d_up_shift, ("band", "grp"), scatter_dimension=0, tiled=True),
        lax.psum_scatter(d_down, ("band", "grp"), scatter_dimension=0, tiled=True),
        lax.psum_scatter(d_down_shift, ("band", "grp"), scatter_dimension=0, tiled=True),
    )
    return (layer_out, d_embedded[None]) + tuple(shards)


DEPTH = 4
PLANE = 4
BIG = 1e30
VMEM = pltpu.MemorySpace.VMEM
SMEM = pltpu.MemorySpace.SMEM
LEADS, TAB_END = 16, 16
ROW_G1, ROW_B1, ROW_QB, ROW_VB, ROW_OB, ROW_G2, ROW_B2, ROW_DB = range(16, 24)
VEC_ROWS = 24


def mul(left, right, over_left, over_right):
    return lax.dot_general(
        left, right, (((over_left,), (over_right,)), ((), ())), preferred_element_type=jnp.float32
    )


def run(kernel, outs, ins, scratch=(), vmem_mb=48, flops=0, moved=0):
    specs = [pl.BlockSpec(memory_space=SMEM if a.ndim == 1 else VMEM) for a in ins]
    return pl.pallas_call(
        kernel,
        out_shape=[jax.ShapeDtypeStruct(s, d) for s, d in outs],
        in_specs=specs,
        out_specs=[pl.BlockSpec(memory_space=VMEM)] * len(outs),
        scratch_shapes=[pltpu.VMEM(s, d) for s, d in scratch],
        compiler_params=pltpu.CompilerParams(vmem_limit_bytes=vmem_mb << 20),
        cost_estimate=pl.CostEstimate(flops=flops, bytes_accessed=moved, transcendentals=0),
    )(*ins)


def row_stats(values):
    mean = jnp.mean(values, -1, keepdims=True)
    centred = values - mean
    inv = lax.rsqrt(jnp.mean(centred * centred, -1, keepdims=True) + epsilon)
    return centred * inv, inv


def norm_back(d_normal, normal, inv):
    first = jnp.mean(d_normal, -1, keepdims=True)
    second = jnp.mean(d_normal * normal, -1, keepdims=True)
    return inv * (d_normal - first - normal * second)


def lead_hot(lead_ref, seg_col_ref):
    seg = seg_col_ref[...]
    lead = jnp.zeros_like(seg)
    for slot in range(lead_ref.shape[0]):
        lead = jnp.where(seg == slot, lead_ref[slot], lead)
    slots = lax.broadcasted_iota(jnp.int32, (seg.shape[0], LEADS), 1)
    return jnp.where(slots == lead, 1.0, 0.0).astype(bf16)


def prep_kernel(pos, tok, dout, qkv, up, down, *outs):
    z, yx = pos[0], pos[1]
    q_outs, msgs, down_msg = outs[:4], outs[4:8], outs[8]
    rows = tok.shape[0]
    d = tok.shape[1]
    width = d // DEPTH
    for u in range(DEPTH):
        zu = (z + u) & (DEPTH - 1)
        for part in range(3):
            q_outs[u][:, part * width : (part + 1) * width] = qkv[
                :, pl.ds(pl.multiple_of(part * d + zu * width, width), width)
            ]
    up_rows, up_cols = up.shape
    fr = up_cols // (DEPTH * PLANE * 2)
    for k in range(PLANE):
        msgs[k][0:rows, :] = tok[...]
        msgs[k][rows : 2 * rows, :] = dout[...]
        for c in range(2):
            for zz in range(DEPTH):
                src = ((zz * PLANE + (yx ^ k)) * 2 + c) * fr
                dst = (c * DEPTH + zz) * fr
                msgs[k][2 * rows :, dst : dst + fr] = up[:, pl.ds(pl.multiple_of(src, fr), fr)]
    down_msg[...] = down[...]


def qkv_kernel(pos, lead, seg_col, vec, t0, t1, t2, t3, wa, wb, n1, w, o0, o1, o2, o3, proj):
    z, yx, c = pos[0], pos[1], pos[2]
    rows, d = t0.shape
    rw = wa.shape[2]
    for k in range(PLANE):
        for s in range(DEPTH):
            block = (((z - s) & (DEPTH - 1)) * PLANE + (yx ^ k)) * 2
            w[pl.ds(pl.multiple_of((block + c) * rw, rw), rw), :] = wa[k, s]
            w[pl.ds(pl.multiple_of((block + 1 - c) * rw, rw), rw), :] = wb[k, s]
    shift = mul(lead_hot(lead, seg_col), vec[0:LEADS, :], 1, 0)
    gain = vec[ROW_G1 : ROW_G1 + 1, :].astype(f32)
    bias = vec[ROW_B1 : ROW_B1 + 1, :].astype(f32)
    for s, t in enumerate((t0, t1, t2, t3)):
        normal, _ = row_stats(t[...].astype(f32) + shift)
        n1[s * rows : (s + 1) * rows, :] = (normal * gain + bias).astype(bf16)
    width = d // DEPTH
    head = width // PLANE
    at = pl.ds(pl.multiple_of(z * width, width), width)
    biases = jnp.concatenate(
        [
            vec[ROW_QB : ROW_QB + 1, at].astype(f32),
            jnp.zeros((1, width), f32),
            vec[ROW_VB : ROW_VB + 1, at].astype(f32),
        ],
        1,
    )
    first = lax.broadcasted_iota(jnp.int32, (8, 3 * width), 0) == 0
    biases = jnp.where(first, biases, 0.0).astype(bf16)
    ones = jnp.ones((8, DEPTH * rows), bf16)
    found = mul(w[...], n1[...], 0, 1) + mul(biases, ones, 0, 0)
    proj[...] = found.astype(bf16).reshape(proj.shape)
    for k, out in enumerate((o0, o1, o2, o3)):
        for part in range(3):
            out[part * head : (part + 1) * head, :] = proj[part * PLANE + (yx ^ k)]


def hot_rows(seg_row, count, tiles):
    seg = jnp.concatenate([seg_row[...]] * tiles, 1)
    slots = lax.broadcasted_iota(jnp.int32, (16, seg.shape[1]), 0)
    return jnp.where(slots == seg, 1.0, 0.0), slots < count


def fill_heads(seg_row, count, blocks, qa, ka, vt):
    head = blocks[0].shape[0] // 3
    span = blocks[0].shape[1]
    hot, real = hot_rows(seg_row, count, span // seg_row.shape[1])
    q_mark = jnp.where(real, (hot - 1.0) * BIG, 0.0).astype(bf16)
    k_mark = jnp.where(real, hot, 0.0).astype(bf16)
    rest = qa.shape[0] - head - 16
    for k, block in enumerate(blocks):
        cols = slice(k * span, (k + 1) * span)
        qa[0:head, cols] = block[0:head, :] * jnp.asarray(score_scale, bf16)
        qa[head : head + 16, cols] = q_mark
        qa[head + 16 :, cols] = jnp.zeros((rest, span), bf16)
        keys = jnp.concatenate([block[head : 2 * head, :], k_mark, jnp.zeros((rest, span), bf16)], 0)
        ka[cols, :] = keys.T
        vt[:, cols] = block[2 * head :, :]


def attend_kernel(count, seg_row, b0, b1, b2, b3, o0, o1, o2, o3, lse, qa, ka, vt):
    fill_heads(seg_row, count, (b0, b1, b2, b3), qa, ka, vt)
    span = b0.shape[1]
    rows = seg_row.shape[1]
    outs = (o0, o1, o2, o3)

    def step(k, carry):
        for half in range(DEPTH // 2):
            at = pl.ds(pl.multiple_of(k * span + half * 2 * rows, 2 * rows), 2 * rows)
            scores = mul(ka[...], qa[:, at], 1, 0)
            top = jnp.max(scores, 0, keepdims=True)
            soft = jnp.exp(scores - top)
            total = jnp.sum(soft, 0, keepdims=True)
            found = mul(vt[...], soft.astype(bf16), 1, 0) / total
            lse[:, at] = jnp.broadcast_to(top + jnp.log(total), (8, 2 * rows))
            for i in range(2):
                outs[half * 2 + i][:, pl.ds(pl.multiple_of(k * rows, rows), rows)] = found[
                    :, i * rows : (i + 1) * rows
                ].astype(bf16)
        return carry

    lax.fori_loop(0, PLANE, step, 0)


def mid_kernel(pos, lead, seg_col, vec, up_b, a0, a1, a2, a3, m0, m1, m2, m3, w_out, wa, wb,
               act, d_hid, n2, w_up, w_down, middle, att_own, p0, p1, p2, p3, d_vec, d_up_b,
               att, normal, inv, hid, w_scr):
    z, yx, c = pos[0], pos[1], pos[2]
    parts = (a0, a1, a2, a3)
    msgs = (m0, m1, m2, m3)
    head = a0.shape[1]
    rows = seg_col.shape[0]
    d = w_out.shape[1]
    rw = m0.shape[0] - 2 * rows
    fr = wa.shape[1] - PLANE * rw
    for zz in range(DEPTH):
        for k in range(PLANE):
            block = (zz * PLANE + (yx ^ k)) * 2
            src = slice(k * rw, (k + 1) * rw)
            w_up[pl.ds(pl.multiple_of((block + c) * rw, rw), rw), :] = wa[zz, src, :]
            w_up[pl.ds(pl.multiple_of((block + 1 - c) * rw, rw), rw), :] = wb[zz, src, :]
        src = slice(PLANE * rw, PLANE * rw + fr)
        w_down[pl.ds(pl.multiple_of((c * DEPTH + zz) * fr, fr), fr), :] = wa[zz, src, :]
        w_down[pl.ds(pl.multiple_of(((1 - c) * DEPTH + zz) * fr, fr), fr), :] = wb[zz, src, :]
    for u in range(DEPTH):
        for m in range(PLANE):
            h = ((z + u) & (DEPTH - 1)) * PLANE + (yx ^ m)
            for j in range(PLANE):
                k = m ^ j
                att[pl.ds(pl.multiple_of(h * head, head), head), j * rows : (j + 1) * rows] = parts[m][
                    u, :, k * rows : (k + 1) * rows
                ]
    att_own[...] = att[:, 0:rows]
    shift = mul(lead_hot(lead, seg_col), vec[0:LEADS, :], 1, 0)
    out_b = vec[ROW_OB : ROW_OB + 1, :].astype(f32)
    gain = vec[ROW_G2 : ROW_G2 + 1, :].astype(f32)
    bias = vec[ROW_B2 : ROW_B2 + 1, :].astype(f32)
    branch = mul(att[...], w_out[...], 0, 0)
    for j in range(PLANE):
        here = slice(j * rows, (j + 1) * rows)
        total = msgs[j][0:rows, :].astype(f32) + shift + branch[here, :] + out_b
        if j == 0:
            middle[...] = total
        norm, scale = row_stats(total)
        normal[here, :] = norm
        n2[here, :] = (norm * gain + bias).astype(bf16)
    hid[...] = mul(n2[...], w_up[...], 1, 0) + up_b[...].astype(f32)
    for j in range(PLANE):
        here = slice(j * rows, (j + 1) * rows)
        hidden = hid[here, :]
        phi = 0.5 * (1.0 + lax.erf(hidden * 0.7071067811865476))
        act[here, :] = (hidden * phi).astype(bf16)
        hid[here, :] = phi + hidden * (jnp.exp(-0.5 * hidden * hidden) * 0.3989422804014327)
    sums = jnp.zeros((1, d), f32)
    for j in range(PLANE):
        here = slice(j * rows, (j + 1) * rows)
        d_act = mul(msgs[j][rows : 2 * rows, :], w_down[...], 1, 1)
        low = (d_act * hid[here, :]).astype(bf16)
        d_hid[here, :] = low
        sums = sums + jnp.sum(low.astype(f32), 0, keepdims=True)
    d_up_b[...] = sums
    back = mul(d_hid[...], w_up[...], 1, 1)
    d_gain = jnp.zeros((1, d), f32)
    d_bias = jnp.zeros((1, d), f32)
    for j, out in enumerate((p0, p1, p2, p3)):
        here = slice(j * rows, (j + 1) * rows)
        piece = back[here, :]
        out[...] = piece.astype(out.dtype)
        d_gain = d_gain + jnp.sum(piece * normal[here, :], 0, keepdims=True)
        d_bias = d_bias + jnp.sum(piece, 0, keepdims=True)
    d_down_b = jnp.sum(m0[rows : 2 * rows, :].astype(f32), 0, keepdims=True)
    d_vec[...] = jnp.concatenate([d_gain, d_bias, d_down_b, jnp.zeros((5, d), f32)], 0)


def ffn_grad_kernel(pos, vec, act, d_hid, n2, w_down, middle, m0, m1, m2, m3,
                    o0, o1, o2, o3, mine, other, grad):
    c = pos[2]
    msgs = (m0, m1, m2, m3)
    rows, d = middle.shape
    rw = m0.shape[0] - 2 * rows
    fr = act.shape[1] // (2 * DEPTH)
    found = mul(act[...], w_down[...], 1, 0)
    o0[...] = found[0:rows, :] + middle[...] + vec[ROW_DB : ROW_DB + 1, :].astype(f32)
    for j, out in ((1, o1), (2, o2), (3, o3)):
        out[...] = found[j * rows : (j + 1) * rows, :].astype(bf16)
    grad[...] = mul(n2[...], d_hid[...], 0, 0).astype(bf16)
    for zz in range(DEPTH):
        for k in range(PLANE):
            block = (zz * PLANE + k) * 2
            dst = slice(k * rw, (k + 1) * rw)
            mine[zz, dst, :] = grad[pl.ds(pl.multiple_of((block + c) * rw, rw), rw), :]
            other[zz, dst, :] = grad[pl.ds(pl.multiple_of((block + 1 - c) * rw, rw), rw), :]
    d_down = jnp.zeros(grad.shape, f32)
    for j in range(PLANE):
        d_down = d_down + mul(act[j * rows : (j + 1) * rows, :], msgs[j][rows : 2 * rows, :], 0, 0)
    grad[...] = d_down.astype(bf16)
    dst = slice(PLANE * rw, PLANE * rw + fr)
    for zz in range(DEPTH):
        mine[zz, dst, :] = grad[pl.ds(pl.multiple_of((c * DEPTH + zz) * fr, fr), fr), :]
        other[zz, dst, :] = grad[pl.ds(pl.multiple_of(((1 - c) * DEPTH + zz) * fr, fr), fr), :]


def branch_kernel(pos, vec, middle, dout, w_out, p0, p1, p2, p3, d_mid, d_branch, d_out_b,
                  o0, o1, o2, o3, d_att):
    z, yx = pos[0], pos[1]
    dy = p0[...].astype(f32) + p1[...].astype(f32) + p2[...].astype(f32) + p3[...].astype(f32)
    normal, inv = row_stats(middle[...])
    gain = vec[ROW_G2 : ROW_G2 + 1, :].astype(f32)
    total = dout[...].astype(f32) + norm_back(dy * gain, normal, inv)
    d_mid[...] = total
    low = total.astype(bf16)
    d_branch[...] = low
    d_out_b[...] = jnp.broadcast_to(jnp.sum(low.astype(f32), 0, keepdims=True), d_out_b.shape)
    d_att[...] = mul(w_out[...], low, 1, 1).astype(bf16).reshape(d_att.shape)
    for k, out in enumerate((o0, o1, o2, o3)):
        for u in range(DEPTH):
            out[u] = d_att[((z + u) & (DEPTH - 1)) * PLANE + (yx ^ k)]


def turn_kernel(b0, b1, b2, b3, *outs):
    for u, out in enumerate(outs):
        for m, block in enumerate((b0, b1, b2, b3)):
            out[m] = block[u]


def out_grad_kernel(att_own, d_branch, grad):
    grad[...] = mul(att_own[...], d_branch[...], 1, 0).astype(bf16)


def attend_back_kernel(count, seg_row, b0, b1, b2, b3, c0, c1, c2, c3, lse,
                       o0, o1, o2, o3, qa, ka, vt, vn, dot, dq, dk, dv):
    fill_heads(seg_row, count, (b0, b1, b2, b3), qa, ka, vt)
    span = b0.shape[1]
    rows = seg_row.shape[1]
    head = vt.shape[0]
    total = vt.shape[1]
    for k in range(PLANE):
        cols = slice(k * span, (k + 1) * span)
        vn[cols, :] = vt[:, cols].T
        for s, block in enumerate((c0, c1, c2, c3)):
            dot[:, k * span + s * rows : k * span + (s + 1) * rows] = block[k]
    dk[...] = jnp.zeros_like(dk)
    dv[...] = jnp.zeros_like(dv)

    def step(i, carry):
        at = pl.ds(pl.multiple_of(i * 2 * rows, 2 * rows), 2 * rows)
        scores = mul(ka[...], qa[:, at], 1, 0)
        soft = jnp.exp(scores - lse[0:1, at])
        d_out = dot[:, at]
        d_soft = mul(vn[...], d_out, 1, 0)
        delta = jnp.sum(soft * d_soft, 0, keepdims=True)
        d_scores = (soft * (d_soft - delta)).astype(bf16)
        dv[...] += mul(d_out, soft.astype(bf16), 1, 1)
        dk[...] += mul(qa[0:head, at], d_scores, 1, 1)
        keys = ka[:, 0:head]
        dq[:, at] = (mul(keys, d_scores, 0, 0) * score_scale).astype(bf16)
        return carry

    lax.fori_loop(0, total // (2 * rows), step, 0)
    for k, out in enumerate((o0, o1, o2, o3)):
        cols = slice(k * span, (k + 1) * span)
        out[0:head, :] = dq[:, cols]
        out[head : 2 * head, :] = dk[:, cols].astype(bf16)
        out[2 * head :, :] = dv[:, cols].astype(bf16)


def qkv_back_kernel(pos, lead, seg_col, vec, t0, t1, t2, t3, n1, w, g0, g1, g2, g3, d_mid, d_mid_vec, d_out_b,
                    mine, other, r0, r1, r2, r3, d_vec, joined, grad):
    z, yx, c = pos[0], pos[1], pos[2]
    rows, d = t0.shape
    width = d // DEPTH
    head = width // PLANE
    rw = mine.shape[0] // (DEPTH * PLANE)
    for k, g in enumerate((g0, g1, g2, g3)):
        for part in range(3):
            joined[part * PLANE + (yx ^ k)] = g[part * head : (part + 1) * head, :]
    grads = joined[...].reshape(3 * width, DEPTH * rows)
    grad[...] = mul(n1[...], grads, 0, 1).astype(bf16)
    for i in range(DEPTH * PLANE):
        dst = slice(i * rw, (i + 1) * rw)
        mine[dst, :] = grad[pl.ds(pl.multiple_of((2 * i + c) * rw, rw), rw), :]
        other[dst, :] = grad[pl.ds(pl.multiple_of((2 * i + 1 - c) * rw, rw), rw), :]
    back = mul(grads, w[...], 0, 1)
    hot = lead_hot(lead, seg_col)
    shift = mul(hot, vec[0:LEADS, :], 1, 0)
    gain = vec[ROW_G1 : ROW_G1 + 1, :].astype(f32)
    d_gain = jnp.zeros((1, d), f32)
    d_bias = jnp.zeros((1, d), f32)
    d_emb = d_mid[...]
    for s, (t, out) in enumerate(zip((t0, t1, t2, t3), (r0, r1, r2, r3))):
        piece = back[s * rows : (s + 1) * rows, :]
        out[...] = piece.astype(out.dtype)
        normal, inv = row_stats(t[...].astype(f32) + shift)
        d_gain = d_gain + jnp.sum(piece * normal, 0, keepdims=True)
        d_bias = d_bias + jnp.sum(piece, 0, keepdims=True)
        d_emb = d_emb + norm_back(piece * gain, normal, inv)
    high = d_emb.astype(bf16)
    low = (d_emb - high.astype(f32)).astype(bf16)
    d_vec[0:LEADS, :] = mul(hot, high, 0, 0) + mul(hot, low, 0, 0)
    ones = jnp.ones((8, DEPTH * rows), bf16)
    sums = mul(ones, grads, 1, 1)
    d_vec[LEADS:, :] = jnp.zeros((VEC_ROWS - LEADS, d), f32)
    d_vec[ROW_G1 : ROW_G1 + 1, :] = d_gain
    d_vec[ROW_B1 : ROW_B1 + 1, :] = d_bias
    at = pl.ds(pl.multiple_of(z * width, width), width)
    d_vec[ROW_QB : ROW_QB + 1, at] = sums[0:1, 0:width]
    d_vec[ROW_VB : ROW_VB + 1, at] = sums[0:1, 2 * width :]
    d_vec[ROW_OB : ROW_OB + 1, :] = d_out_b[0:1, :]
    d_vec[ROW_G2 : ROW_G2 + 1, :] = d_mid_vec[0:1, :]
    d_vec[ROW_B2 : ROW_B2 + 1, :] = d_mid_vec[1:2, :]
    d_vec[ROW_DB : ROW_DB + 1, :] = d_mid_vec[2:3, :]


def first_back_kernel(lead, seg_col, vec, tok, d_mid, r0, r1, r2, r3, out):
    dy = r0[...].astype(f32) + r1[...].astype(f32) + r2[...].astype(f32) + r3[...].astype(f32)
    shift = mul(lead_hot(lead, seg_col), vec[0:LEADS, :], 1, 0)
    normal, inv = row_stats(tok[...].astype(f32) + shift)
    gain = vec[ROW_G1 : ROW_G1 + 1, :].astype(f32)
    out[...] = d_mid[...] + norm_back(dy * gain, normal, inv)


def pair_sum_kernel(mine, other, out):
    out[...] = (mine[...].astype(f32) + other[...].astype(f32)).astype(bf16)


def qkv_pair_kernel(pos, mine, other, o0, o1, o2, o3, total):
    yx = pos[1]
    total[...] = (mine[...].astype(f32) + other[...].astype(f32)).astype(bf16)
    rw = o0.shape[1]
    for k, out in enumerate((o0, o1, o2, o3)):
        for zz in range(DEPTH):
            out[zz] = total[pl.ds(pl.multiple_of((zz * PLANE + (yx ^ k)) * rw, rw), rw), :]


def qkv_quad_kernel(pos, b0, b1, b2, b3, o0, o1, o2, o3, total):
    z = pos[0]
    total[...] = (
        b0[...].astype(f32) + b1[...].astype(f32) + b2[...].astype(f32) + b3[...].astype(f32)
    ).astype(bf16)
    for u, out in enumerate((o0, o1, o2, o3)):
        out[...] = total[(z + u) & (DEPTH - 1)]


def qkv_join_kernel(pos, b0, b1, b2, b3, out):
    z = pos[0]
    width = b0.shape[1] // 3
    for s, block in enumerate((b0, b1, b2, b3)):
        at = ((z - s) & (DEPTH - 1)) * width
        for part in range(3):
            start = pl.multiple_of(part * DEPTH * width + at, width)
            out[:, pl.ds(start, width)] = block[:, part * width : (part + 1) * width].astype(f32)


def up_pick_kernel(pos, shard, o0, o1, o2, o3, d_down):
    yx = pos[1]
    rw = o0.shape[0]
    for k, out in enumerate((o0, o1, o2, o3)):
        out[...] = shard[pl.ds(pl.multiple_of((yx ^ k) * rw, rw), rw), :]
    d_down[...] = shard[PLANE * rw :, :].astype(f32)


def up_join_kernel(pos, b0, b1, b2, b3, out):
    yx = pos[1]
    fr = b0.shape[1] // (2 * DEPTH)
    for k, block in enumerate((b0, b1, b2, b3)):
        for c in range(2):
            for zz in range(DEPTH):
                src = (c * DEPTH + zz) * fr
                dst = pl.multiple_of(((zz * PLANE + (yx ^ k)) * 2 + c) * fr, fr)
                out[:, pl.ds(dst, fr)] = block[:, src : src + fr].astype(f32)


ALL = ("z", "y", "x", "g")


def across(blocks):
    swap = [(0, 1), (1, 0)]
    return (
        blocks[0],
        lax.ppermute(blocks[1], "x", swap),
        lax.ppermute(blocks[2], "y", swap),
        lax.ppermute(blocks[3], ("y", "x"), [(i, i ^ 3) for i in range(PLANE)]),
    )


def along(blocks):
    return (blocks[0],) + tuple(
        lax.ppermute(blocks[u], "z", [(i, (i + u) % DEPTH) for i in range(DEPTH)])
        for u in range(1, DEPTH)
    )


def turned(blocks):
    return (blocks[0], blocks[3], blocks[2], blocks[1])


def core_swap(block):
    return lax.ppermute(block, "g", [(0, 1), (1, 0)])


def fast_local(
    tokens, segment_ids, lead_index, lead_table, ln1_gain, ln1_bias, qkv_weight, q_bias, v_bias,
    out_weight, out_bias, ln2_gain, ln2_bias, up_weight, up_bias, down_weight, down_bias, d_out,
):
    z = lax.axis_index("z")
    yx = lax.axis_index("y") * 2 + lax.axis_index("x")
    c = lax.axis_index("g")
    pos = jnp.stack([z, yx, c]).astype(jnp.int32)
    tok = tokens[0]
    rows, d = tok.shape
    head = d // HEADS
    span = DEPTH * rows
    group = PLANE * span
    rw = qkv_weight.shape[0]
    fr = down_weight.shape[0]
    ff = 2 * DEPTH * fr
    devices = DEPTH * PLANE * 2
    seg_row = segment_ids
    seg_col = segment_ids.reshape(rows, 1)
    lead = lead_index[0]
    count = lead.shape[0]
    width = 3 * d // DEPTH

    flat = jnp.concatenate(
        [lead_table.reshape(-1), ln1_gain, ln1_bias, q_bias, v_bias, out_bias, ln2_gain, ln2_bias, down_bias, up_bias]
    )
    padded = -(-flat.shape[0] // 1024) * 1024
    flat = jnp.pad(flat, (0, padded - flat.shape[0])).reshape(8, padded // 8)
    smalls = lax.all_to_all(
        jnp.broadcast_to(flat[None], (devices,) + flat.shape), ALL, split_axis=0, concat_axis=0, tiled=True
    ).reshape(devices, padded)
    vec = smalls[:, : VEC_ROWS * rw].reshape(devices, VEC_ROWS, rw).transpose(1, 0, 2).reshape(VEC_ROWS, d)
    up_b = smalls[:, VEC_ROWS * rw : VEC_ROWS * rw + fr].reshape(DEPTH, PLANE, 2, fr)
    up_b = lax.dynamic_index_in_dim(up_b, yx, 1, keepdims=False).transpose(1, 0, 2).reshape(1, ff)

    w_out = lax.all_gather(out_weight, ALL, axis=0, tiled=True)

    prep = run(
        prep_kernel,
        [((rw, width), bf16)] * 4 + [((2 * rows + rw, d), bf16)] * 4 + [((fr, d), bf16)],
        [pos, tok, d_out[0], qkv_weight, up_weight, down_weight],
    )
    q_rows = along(prep[:4])
    toks = along((tok,) * DEPTH)
    q_stack = jnp.stack(q_rows)
    q_plane = across((q_stack,) * PLANE)
    wa = jnp.stack(q_plane)
    wb = core_swap(wa)
    msgs = across(prep[4:8])
    shard = jnp.concatenate([m[2 * rows :] for m in msgs] + [down_weight], 0)
    fa = lax.all_gather(shard[None], "z", axis=0, tiled=True)
    fb = core_swap(fa)

    n1, w_qkv, *blocks = run(
        qkv_kernel,
        [((span, d), bf16), ((d, width), bf16)] + [((3 * head, span), bf16)] * 4,
        [pos, lead, seg_col, vec, *toks, wa, wb],
        [((3 * PLANE, head, span), bf16)],
    )
    blocks = across(blocks)
    *att_parts, lse = run(
        functools.partial(attend_kernel, count),
        [((head, PLANE * rows), bf16)] * 4 + [((8, group), f32)],
        [seg_row, *blocks],
        [((128, group), bf16), ((group, 128), bf16), ((head, group), bf16)],
    )
    a0, a1, a2, a3 = along(turned(att_parts))
    att_parts = across((jnp.stack(turned((a0, a1, a2, a3))),) * PLANE)
    act, d_hid, n2, w_up, w_down, middle, att_own, p0, p1, p2, p3, d_mid_vec, d_up_b = run(
        mid_kernel,
        [((span, ff), bf16), ((span, ff), bf16), ((span, d), bf16), ((d, ff), bf16), ((ff, d), bf16),
         ((rows, d), f32), ((d, rows), bf16), ((rows, d), f32)] + [((rows, d), bf16)] * 3
        + [((8, d), f32), ((1, ff), f32)],
        [pos, lead, seg_col, vec, up_b, *att_parts, *msgs, w_out, fa, fb],
        [((d, span), bf16), ((span, d), f32), ((span, 128), f32), ((span, ff), f32), ((8, 128), f32)],
        vmem_mb=56,
    )
    parts = across((p0, p1, p2, p3))
    o0, o1, o2, o3, mine, other = run(
        ffn_grad_kernel,
        [((rows, d), f32)] + [((rows, d), bf16)] * 3 + [((DEPTH, PLANE * rw + fr, d), bf16)] * 2,
        [pos, vec, act, d_hid, n2, w_down, middle, *msgs],
        [((d, ff), bf16)],
    )
    o0, o1, o2, o3 = across((o0, o1, o2, o3))
    layer_out = (o0 + o1.astype(f32) + o2.astype(f32) + o3.astype(f32)).astype(bf16)
    (ffn_sum,) = run(pair_sum_kernel, [(mine.shape, bf16)], [mine, core_swap(other)])
    ffn_shard = lax.psum_scatter(ffn_sum, "z", scatter_dimension=0, tiled=True)[0]

    d_mid, d_branch, d_out_b, *d_att = run(
        branch_kernel,
        [((rows, d), f32), ((rows, d), bf16), ((8, d), f32)] + [((DEPTH, head, rows), bf16)] * 4,
        [pos, vec, middle, d_out[0], w_out, *parts],
        [((HEADS, head, rows), bf16)],
    )
    d_att = along(run(turn_kernel, [((PLANE, head, rows), bf16)] * 4, list(across(d_att))))
    (out_grad,) = run(out_grad_kernel, [((d, d), bf16)], [att_own, d_branch])
    d_out_weight = lax.psum_scatter(out_grad, ALL, scatter_dimension=0, tiled=True).astype(f32)
    d_blocks = run(
        functools.partial(attend_back_kernel, count),
        [((3 * head, span), bf16)] * 4,
        [seg_row, *blocks, *d_att, lse],
        [((128, group), bf16), ((group, 128), bf16), ((head, group), bf16), ((group, head), bf16),
         ((head, group), bf16), ((head, group), bf16), ((head, group), f32), ((head, group), f32)],
    )
    d_blocks = across(d_blocks)
    mine, other, r0, r1, r2, r3, d_vec = run(
        qkv_back_kernel,
        [((DEPTH * PLANE * rw, width), bf16)] * 2 + [((rows, d), f32)] + [((rows, d), bf16)] * 3
        + [((VEC_ROWS, d), f32)],
        [pos, lead, seg_col, vec, *toks, n1, w_qkv, *d_blocks, d_mid, d_mid_vec, d_out_b],
        [((3 * PLANE, head, span), bf16), ((d, width), bf16)],
    )
    back = along(turned((r0, r1, r2, r3)))
    other = core_swap(other)
    quads = run(qkv_pair_kernel, [((DEPTH, rw, width), bf16)] * 4, [pos, mine, other],
                [(mine.shape, bf16)])
    quads = across(quads)
    cols = along(run(qkv_quad_kernel, [((rw, width), bf16)] * 4, [pos, *quads], [((DEPTH, rw, width), bf16)]))
    (d_qkv,) = run(qkv_join_kernel, [((rw, 3 * d), f32)], [pos, *cols])
    (d_tokens,) = run(first_back_kernel, [((rows, d), f32)], [lead, seg_col, vec, tok, d_mid, *back])

    *ups, d_down = run(up_pick_kernel, [((rw, ff), bf16)] * 4 + [((fr, d), f32)], [pos, ffn_shard])
    (d_up,) = run(up_join_kernel, [((rw, PLANE * ff), f32)], [pos, *across(ups)])

    sums = d_vec.reshape(VEC_ROWS, devices, rw).transpose(1, 0, 2).reshape(devices, VEC_ROWS * rw)
    up_sums = d_up_b.reshape(2, DEPTH, fr).transpose(1, 0, 2)[:, None]
    up_sums = jnp.where(jnp.arange(PLANE)[None, :, None, None] == yx, up_sums, 0.0).reshape(devices, fr)
    flat = jnp.concatenate([sums, up_sums], 1)
    flat = jnp.pad(flat, ((0, 0), (0, padded - flat.shape[1]))).reshape(devices, 8, padded // 8)
    flat = jnp.sum(lax.all_to_all(flat, ALL, split_axis=0, concat_axis=0, tiled=True), 0).reshape(padded)
    table = flat[: LEADS * rw].reshape(LEADS, rw)
    vecs = flat[LEADS * rw : VEC_ROWS * rw].reshape(VEC_ROWS - LEADS, rw)
    d_g1, d_b1, d_qb, d_vb, d_ob, d_g2, d_b2, d_db = (vecs[i] for i in range(8))
    d_ub = flat[VEC_ROWS * rw : VEC_ROWS * rw + fr]
    return (
        layer_out[None], d_tokens[None], table, d_g1, d_b1, d_qkv, d_qb, d_vb, d_out_weight, d_ob,
        d_g2, d_b2, d_up, d_ub, d_down, d_db,
    )


def specs(band, grp):
    every = band + grp
    rows = P(grp, band, None)
    in_specs = (
        rows, P(grp, band), P(grp, None), P(None, every), P(every), P(every), P(every, None), P(every), P(every),
        P(every, None), P(every), P(every), P(every), P(every, None), P(every), P(every, None), P(every), rows,
    )
    out_specs = (
        rows, rows, P(None, every), P(every), P(every), P(every, None), P(every), P(every), P(every, None), P(every),
        P(every), P(every), P(every, None), P(every), P(every, None), P(every),
    )
    return in_specs, out_specs


def solution(mesh):
    band, grp = mesh.shape["band"], mesh.shape["grp"]
    if band == HEADS and grp == 2:
        mesh = Mesh(mesh.devices.reshape(DEPTH, 2, 2, grp), ("z", "y", "x", "g"))
        in_specs, out_specs = specs(("z", "y", "x"), ("g",))
        return jax.shard_map(fast_local, mesh=mesh, in_specs=in_specs, out_specs=out_specs, check_vma=False)
    in_specs, out_specs = specs(("band",), ("grp",))
    return jax.shard_map(local, mesh=mesh, in_specs=in_specs, out_specs=out_specs, check_vma=False)
```

```python
import functools
import math

import jax
import jax.numpy as jnp
from jax import lax
from jax.experimental import pallas as pl
from jax.experimental.pallas import tpu as pltpu
from jax.sharding import Mesh
from jax.sharding import PartitionSpec as P

bf16, f32 = jnp.bfloat16, jnp.float32

HEADS = 16


epsilon = 1e-05
score_scale = 0.125
masked_score = -1e30


def norm_rows(values, norm_gain, norm_bias):
    row_mean = jnp.mean(values, -1, keepdims=True)
    centred = values - row_mean
    row_var = jnp.mean(centred * centred, -1, keepdims=True)
    return centred * lax.rsqrt(row_var + epsilon) * norm_gain + norm_bias


def gelu_exact(values):
    return jax.nn.gelu(values, approximate=False)


def split_blocks(values, block_rows):
    return values.reshape((values.shape[0] // block_rows, block_rows) + values.shape[1:])


def block_scores(query_heads, key_heads, allowed):
    raw_scores = (
        jnp.einsum("qhd,khd->hqk", query_heads, key_heads, preferred_element_type=jnp.float32)
        * score_scale
    )
    return jnp.where(allowed[None], raw_scores, masked_score)


def softmax_rows(query_heads, key_heads, allowed, log_total):
    scores = block_scores(query_heads, key_heads, allowed)
    return jnp.where(allowed[None], jnp.exp(scores - log_total[:, :, None]), 0.0)


def score_grads(query_heads, key_heads, value_heads, d_heads, allowed, log_total, row_delta):
    soft_rows = softmax_rows(query_heads, key_heads, allowed, log_total)
    d_soft = jnp.einsum("qhd,khd->hqk", d_heads, value_heads, preferred_element_type=jnp.float32)
    d_scores = (soft_rows * (d_soft - row_delta[:, :, None])).astype(jnp.bfloat16)
    return (soft_rows.astype(jnp.bfloat16), d_scores)


def local(
    tokens,
    segment_ids,
    lead_index,
    lead_table,
    ln1_gain,
    ln1_bias,
    qkv_weight,
    q_bias,
    v_bias,
    out_weight,
    out_bias,
    ln2_gain,
    ln2_bias,
    up_weight,
    up_bias,
    down_weight,
    down_bias,
    d_out,
):
    (
        table_full,
        first_gain,
        first_shift,
        project_full,
        query_shift,
        value_shift,
        out_full,
        out_shift,
        second_gain,
        second_shift,
        up_full,
        up_shift,
        down_full,
        down_shift,
    ) = (
        lax.all_gather(lead_table, ("band", "grp"), axis=1, tiled=True),
        lax.all_gather(ln1_gain, ("band", "grp"), axis=0, tiled=True),
        lax.all_gather(ln1_bias, ("band", "grp"), axis=0, tiled=True),
        lax.all_gather(qkv_weight, ("band", "grp"), axis=0, tiled=True),
        lax.all_gather(q_bias, ("band", "grp"), axis=0, tiled=True),
        lax.all_gather(v_bias, ("band", "grp"), axis=0, tiled=True),
        lax.all_gather(out_weight, ("band", "grp"), axis=0, tiled=True),
        lax.all_gather(out_bias, ("band", "grp"), axis=0, tiled=True),
        lax.all_gather(ln2_gain, ("band", "grp"), axis=0, tiled=True),
        lax.all_gather(ln2_bias, ("band", "grp"), axis=0, tiled=True),
        lax.all_gather(up_weight, ("band", "grp"), axis=0, tiled=True),
        lax.all_gather(up_bias, ("band", "grp"), axis=0, tiled=True),
        lax.all_gather(down_weight, ("band", "grp"), axis=0, tiled=True),
        lax.all_gather(down_bias, ("band", "grp"), axis=0, tiled=True),
    )
    tok_rows = tokens.shape[1]
    features = tokens.shape[2]
    head_dim = features // HEADS
    band_count = lax.axis_size("band")
    group_rows = tok_rows * band_count
    block_rows = math.gcd(group_rows, 1024)
    own_segments = segment_ids[0]
    group_segments = jnp.tile(own_segments, band_count)
    sample_count = lead_index.shape[1]
    lead_count = lead_table.shape[0]
    sample_hot = (
        own_segments[:, None] == jnp.arange(sample_count, dtype=jnp.int32)[None, :]
    ).astype(jnp.float32)
    lead_hot = (lead_index[0][:, None] == jnp.arange(lead_count, dtype=jnp.int32)[None, :]).astype(
        jnp.float32
    )
    lead_pick = jnp.dot(sample_hot, lead_hot, precision=lax.Precision.HIGHEST)
    embedded = tokens[0].astype(jnp.float32) + jnp.dot(
        lead_pick.astype(jnp.bfloat16), table_full, preferred_element_type=jnp.float32
    )
    normed_first = norm_rows(
        embedded, first_gain.astype(jnp.float32), first_shift.astype(jnp.float32)
    ).astype(jnp.bfloat16)
    projected = jnp.dot(normed_first, project_full, preferred_element_type=jnp.float32)
    query_rows = (projected[:, :features] + query_shift.astype(jnp.float32)).astype(jnp.bfloat16)
    key_rows = projected[:, features : 2 * features].astype(jnp.bfloat16)
    value_rows = (projected[:, 2 * features :] + value_shift.astype(jnp.float32)).astype(
        jnp.bfloat16
    )
    key_all, value_all = (
        lax.all_gather(key_rows, "band", axis=0, tiled=True),
        lax.all_gather(value_rows, "band", axis=0, tiled=True),
    )
    query_heads = query_rows.reshape(tok_rows, HEADS, head_dim)
    key_blocks = split_blocks(key_all.reshape(group_rows, HEADS, head_dim), block_rows)
    value_blocks = split_blocks(value_all.reshape(group_rows, HEADS, head_dim), block_rows)
    segment_blocks = split_blocks(group_segments, block_rows)

    def stats_step(running, block_data):
        running_max, running_sum = running
        key_block, key_segments = block_data
        allowed = own_segments[:, None] == key_segments[None, :]
        scores = block_scores(query_heads, key_block, allowed)
        new_max = jnp.maximum(running_max, jnp.max(scores, -1))
        block_sum = jnp.sum(
            jnp.where(allowed[None], jnp.exp(scores - new_max[:, :, None]), 0.0), -1
        )
        return ((new_max, running_sum * jnp.exp(running_max - new_max) + block_sum), None)

    start_max = jnp.full((HEADS, tok_rows), masked_score, jnp.float32)
    start_sum = jnp.zeros((HEADS, tok_rows), jnp.float32)
    (final_max, final_sum), unused_out = lax.scan(
        stats_step, (start_max, start_sum), (key_blocks, segment_blocks)
    )
    log_total = final_max + jnp.log(final_sum)

    def output_step(running, block_data):
        high_part, low_part = running
        key_block, value_block, key_segments = block_data
        allowed = own_segments[:, None] == key_segments[None, :]
        soft_rows = softmax_rows(query_heads, key_block, allowed, log_total)
        soft_low = soft_rows.astype(jnp.bfloat16)
        soft_rest = (soft_rows - soft_low.astype(jnp.float32)).astype(jnp.bfloat16)
        high_part = high_part + jnp.einsum(
            "hqk,khd->qhd", soft_low, value_block, preferred_element_type=jnp.float32
        )
        low_part = low_part + jnp.einsum(
            "hqk,khd->qhd", soft_rest, value_block, preferred_element_type=jnp.float32
        )
        return ((high_part, low_part), None)

    empty_heads = jnp.zeros((tok_rows, HEADS, head_dim), jnp.float32)
    (attn_high, attn_low), unused_out = lax.scan(
        output_step, (empty_heads, empty_heads), (key_blocks, value_blocks, segment_blocks)
    )
    attended = attn_high.reshape(tok_rows, features).astype(jnp.bfloat16)
    middle = (
        embedded
        + jnp.dot(attended, out_full, preferred_element_type=jnp.float32)
        + out_shift.astype(jnp.float32)
    )
    normed_second = norm_rows(
        middle, second_gain.astype(jnp.float32), second_shift.astype(jnp.float32)
    ).astype(jnp.bfloat16)
    hidden = jnp.dot(normed_second, up_full, preferred_element_type=jnp.float32) + up_shift.astype(
        jnp.float32
    )
    activated = gelu_exact(hidden).astype(jnp.bfloat16)
    result = (
        middle
        + jnp.dot(activated, down_full, preferred_element_type=jnp.float32)
        + down_shift.astype(jnp.float32)
    )
    layer_out = result.astype(jnp.bfloat16)[None]
    first_gain_back, project_back, out_back, second_gain_back, up_back, down_back = (
        lax.all_gather(ln1_gain, ("band", "grp"), axis=0, tiled=True),
        lax.all_gather(qkv_weight, ("band", "grp"), axis=0, tiled=True),
        lax.all_gather(out_weight, ("band", "grp"), axis=0, tiled=True),
        lax.all_gather(ln2_gain, ("band", "grp"), axis=0, tiled=True),
        lax.all_gather(up_weight, ("band", "grp"), axis=0, tiled=True),
        lax.all_gather(down_weight, ("band", "grp"), axis=0, tiled=True),
    )
    d_rows = d_out[0]
    d_down_shift = jnp.sum(d_rows.astype(jnp.float32), 0)
    d_down = jnp.einsum("tf,td->fd", activated, d_rows, preferred_element_type=jnp.float32)
    d_act = jnp.einsum("td,fd->tf", d_rows, down_back, preferred_element_type=jnp.float32)
    unused_gelu, gelu_back = jax.vjp(gelu_exact, hidden)
    d_hidden = gelu_back(d_act)[0].astype(jnp.bfloat16)
    d_up_shift = jnp.sum(d_hidden.astype(jnp.float32), 0)
    d_up = jnp.einsum("td,tf->df", normed_second, d_hidden, preferred_element_type=jnp.float32)
    d_normed_second = jnp.einsum("tf,df->td", d_hidden, up_back, preferred_element_type=jnp.float32)
    unused_second, second_back = jax.vjp(
        norm_rows, middle, second_gain_back.astype(jnp.float32), second_shift.astype(jnp.float32)
    )
    d_middle_part, d_gain_second, d_shift_second = second_back(d_normed_second)
    d_middle = d_rows.astype(jnp.float32) + d_middle_part
    d_branch = d_middle.astype(jnp.bfloat16)
    d_out_shift = jnp.sum(d_branch.astype(jnp.float32), 0)
    d_out_full = jnp.einsum("ti,to->io", attended, d_branch, preferred_element_type=jnp.float32)
    d_attended = jnp.einsum(
        "to,io->ti", d_branch, out_back, preferred_element_type=jnp.float32
    ).astype(jnp.bfloat16)
    d_heads = d_attended.reshape(tok_rows, HEADS, head_dim)
    row_delta = jnp.sum(d_heads.astype(jnp.float32) * (attn_high + attn_low), -1).T

    def query_grad(d_query_acc, key_block, value_block, key_segments):
        allowed = own_segments[:, None] == key_segments[None, :]
        soft_low, d_scores = score_grads(
            query_heads, key_block, value_block, d_heads, allowed, log_total, row_delta
        )
        d_query_acc = d_query_acc + jnp.einsum(
            "hqk,khd->qhd", d_scores, key_block, preferred_element_type=jnp.float32
        )
        return (d_query_acc, soft_low, d_scores)

    def owner_step(d_query_acc, block_data):
        key_block, value_block, key_segments = block_data
        d_query_acc, soft_low, d_scores = query_grad(
            d_query_acc, key_block, value_block, key_segments
        )
        d_key_block = (
            jnp.einsum("hqk,qhd->khd", d_scores, query_heads, preferred_element_type=jnp.float32)
            * score_scale
        )
        d_value_block = jnp.einsum(
            "hqk,qhd->khd", soft_low, d_heads, preferred_element_type=jnp.float32
        )
        return (d_query_acc, (d_key_block, d_value_block))

    d_query_sum, (d_key_parts, d_value_parts) = lax.scan(
        owner_step, empty_heads, (key_blocks, value_blocks, segment_blocks)
    )
    d_key_sum, d_value_sum = (
        lax.psum_scatter(
            d_key_parts.reshape(group_rows, features).astype(jnp.bfloat16),
            "band",
            scatter_dimension=0,
            tiled=True,
        ).astype(jnp.float32),
        lax.psum_scatter(
            d_value_parts.reshape(group_rows, features).astype(jnp.bfloat16),
            "band",
            scatter_dimension=0,
            tiled=True,
        ).astype(jnp.float32),
    )
    d_query = (d_query_sum.reshape(tok_rows, features) * score_scale).astype(jnp.bfloat16)
    d_key = d_key_sum.astype(jnp.bfloat16)
    d_value = d_value_sum.astype(jnp.bfloat16)
    d_query_shift = jnp.sum(d_query.astype(jnp.float32), 0)
    d_value_shift = jnp.sum(d_value.astype(jnp.float32), 0)
    d_project_rows = jnp.concatenate([d_query, d_key, d_value], 1)
    d_project = jnp.einsum(
        "ti,to->io", normed_first, d_project_rows, preferred_element_type=jnp.float32
    )
    d_normed_first = jnp.einsum(
        "to,io->ti", d_project_rows, project_back, preferred_element_type=jnp.float32
    )
    unused_first, first_back = jax.vjp(
        norm_rows, embedded, first_gain_back.astype(jnp.float32), first_shift.astype(jnp.float32)
    )
    d_embed_part, d_gain_first, d_shift_first = first_back(d_normed_first)
    d_embedded = d_middle + d_embed_part
    d_table = jnp.einsum("tl,td->ld", lead_pick, d_embedded, precision=lax.Precision.HIGHEST)
    shards = (
        lax.psum_scatter(d_table, ("band", "grp"), scatter_dimension=1, tiled=True),
        lax.psum_scatter(d_gain_first, ("band", "grp"), scatter_dimension=0, tiled=True),
        lax.psum_scatter(d_shift_first, ("band", "grp"), scatter_dimension=0, tiled=True),
        lax.psum_scatter(d_project, ("band", "grp"), scatter_dimension=0, tiled=True),
        lax.psum_scatter(d_query_shift, ("band", "grp"), scatter_dimension=0, tiled=True),
        lax.psum_scatter(d_value_shift, ("band", "grp"), scatter_dimension=0, tiled=True),
        lax.psum_scatter(d_out_full, ("band", "grp"), scatter_dimension=0, tiled=True),
        lax.psum_scatter(d_out_shift, ("band", "grp"), scatter_dimension=0, tiled=True),
        lax.psum_scatter(d_gain_second, ("band", "grp"), scatter_dimension=0, tiled=True),
        lax.psum_scatter(d_shift_second, ("band", "grp"), scatter_dimension=0, tiled=True),
        lax.psum_scatter(d_up, ("band", "grp"), scatter_dimension=0, tiled=True),
        lax.psum_scatter(d_up_shift, ("band", "grp"), scatter_dimension=0, tiled=True),
        lax.psum_scatter(d_down, ("band", "grp"), scatter_dimension=0, tiled=True),
        lax.psum_scatter(d_down_shift, ("band", "grp"), scatter_dimension=0, tiled=True),
    )
    return (layer_out, d_embedded[None]) + tuple(shards)


DEPTH = 4
PLANE = 4
BIG = 1e30
HBM = pltpu.MemorySpace.HBM
VMEM = pltpu.MemorySpace.VMEM
SMEM = pltpu.MemorySpace.SMEM
LEADS = 16
ROW_G1, ROW_B1, ROW_QB, ROW_VB, ROW_OB, ROW_G2, ROW_B2, ROW_DB = range(16, 24)
VEC_ROWS = 24


def mul(left, right, over_left, over_right):
    return lax.dot_general(
        left, right, (((over_left,), (over_right,)), ((), ())), preferred_element_type=jnp.float32
    )


class Mover:
    def __init__(self, sems):
        self.sems, self.used, self.open = sems, 0, []

    def start(self, source, target):
        copy = pltpu.make_async_copy(source, target, self.sems.at[self.used])
        self.used += 1
        copy.start()
        self.open.append(copy)
        return copy

    def wait(self, copies=None):
        for copy in list(self.open if copies is None else copies):
            copy.wait()
            self.open = [other for other in self.open if other is not copy]


class Far:
    def __init__(self, value):
        self.value = value


class Raw(Far):
    pass


class Given:
    def __init__(self, ref, held, mover):
        self.ref, self.mover, self.copy = held, mover, mover.start(ref, held)
        self.shape, self.dtype = ref.shape, ref.dtype

    def ready(self):
        if self.copy is not None:
            self.mover.wait([self.copy])
            self.copy = None
        return self.ref

    def __getitem__(self, at):
        return self.ready()[at]


def run(order, kernel, outs, ins, scratch=(), after=()):
    after = list(after) + order
    kinds = [type(a) if isinstance(a, Far) else None for a in ins]
    ins = [a.value if kind else a for a, kind in zip(ins, kinds)]
    staged = [pltpu.VMEM(a.shape, a.dtype) for a, kind in zip(ins, kinds) if kind is Far]
    outs = [o if len(o) == 3 else o + ("",) for o in outs]
    staged += [pltpu.VMEM(o[0], o[1]) for o in outs if o[2] == "far"]
    n_in, n_after, n_out, n_staged = len(ins), len(after), len(outs), len(staged)
    name = getattr(kernel, "func", kernel).__name__
    micros, room = COSTS[name]
    cost = pl.CostEstimate(flops=micros * 1_100_000_000, bytes_accessed=micros * 3_600_000, transcendentals=0)

    def body(*refs):
        mover = Mover(refs[-1])
        held = list(refs[len(refs) - 1 - n_staged : -1])
        given = [
            Given(ref, held.pop(0), mover) if kind is Far else ref for ref, kind in zip(refs[:n_in], kinds)
        ]
        refs = refs[n_in + n_after : len(refs) - 1 - n_staged]
        made = [held.pop(0) if o[2] == "far" else ref for ref, o in zip(refs, outs)]
        kernel(mover, *given, *made, *refs[n_out + 1 :])
        for ref, written, o in zip(refs, made, outs):
            if o[2] == "far":
                mover.start(written, ref)
        for operand in given:
            if isinstance(operand, Given):
                operand.ready()
        refs[n_out][...] = jnp.zeros_like(refs[n_out])
        mover.wait()

    spaces = [pl.ANY if kind else SMEM if a.ndim == 1 else VMEM for a, kind in zip(ins, kinds)]
    results = pl.pallas_call(
        body,
        name=name,
        out_shape=[HBM(o[0], o[1]) if o[2] else jax.ShapeDtypeStruct(o[0], o[1]) for o in outs]
        + [jax.ShapeDtypeStruct((8, 128), f32)],
        in_specs=[pl.BlockSpec(memory_space=space) for space in spaces + [pl.ANY] * n_after],
        out_specs=[pl.BlockSpec(memory_space=pl.ANY if o[2] else VMEM) for o in outs] + [pl.BlockSpec(memory_space=VMEM)],
        scratch_shapes=[pltpu.VMEM(s, d) for s, d in scratch] + staged + [pltpu.SemaphoreType.DMA((64,))],
        compiler_params=pltpu.CompilerParams(vmem_limit_bytes=room << 20),
        cost_estimate=cost,
    )(*[pltpu.with_memory_space_constraint(a, HBM) if kind else a for a, kind in zip(ins, kinds)], *after)
    order[:] = results[n_out:]
    return results[:n_out]


def row_stats(values):
    mean = jnp.mean(values, -1, keepdims=True)
    centred = values - mean
    inv = lax.rsqrt(jnp.mean(centred * centred, -1, keepdims=True) + epsilon)
    return centred * inv, inv


def norm_back(d_normal, normal, inv):
    first = jnp.mean(d_normal, -1, keepdims=True)
    second = jnp.mean(d_normal * normal, -1, keepdims=True)
    return inv * (d_normal - first - normal * second)


def lead_hot(lead, seg_row):
    seg = seg_row[...]
    found = jnp.zeros_like(seg)
    for slot in range(lead.shape[0]):
        found = jnp.where(seg == slot, lead[slot], found)
    slots = lax.broadcasted_iota(jnp.int32, (LEADS, seg.shape[1]), 0)
    return jnp.where(slots == found, 1.0, 0.0).astype(bf16)


def vec_row(vec, row):
    return vec[row : row + 1, :].astype(f32)


def q_prep_kernel(mover, pos, qkv, o0, o1, o2, o3):
    z = pos[0]
    width = o0.shape[1] // 3
    d = qkv.shape[1] // 3
    for u, out in enumerate((o0, o1, o2, o3)):
        for part in range(3):
            start = pl.multiple_of(part * d + (z ^ u) * width, width)
            mover.start(qkv.at[:, pl.ds(start, width)], out.at[:, part * width : (part + 1) * width])


def q_stack_kernel(mover, pos, b0, b1, b2, b3, out):
    for u, block in enumerate((b0, b1, b2, b3)):
        mover.start(block, out.at[pos[0] ^ u])


def up_prep_kernel(mover, up, out):
    fr = up.shape[1] // (DEPTH * PLANE * 2)
    for k in range(PLANE):
        for c in range(2):
            for zz in range(DEPTH):
                src = ((zz * PLANE + k) * 2 + c) * fr
                dst = (c * DEPTH + zz) * fr
                out[k, :, dst : dst + fr] = up[:, src : src + fr]


def shard_kernel(mover, ups, down, out_rows, out):
    out[0:PLANE] = ups[...]
    out[PLANE : 2 * PLANE] = down[...].reshape(PLANE, -1, down.shape[1])
    out[2 * PLANE] = out_rows[...]


def qkv_kernel(mover, pos, lead, seg_row, vec, t0, t1, t2, t3, *refs):
    z, yx, c = pos[0], pos[1], pos[2]
    qa, qc, (n1, w_out, o0, o1, o2, o3, w, proj) = refs[:4], refs[4:8], refs[8:]
    rows, d = t0.shape
    pending = [mover.start(qa[k], w.at[:, yx ^ k, c]) for k in range(PLANE)]
    pending += [mover.start(qc[k], w.at[:, yx ^ k, 1 - c]) for k in range(PLANE)]
    shift = mul(lead_hot(lead, seg_row), vec[0:LEADS, :], 0, 0)
    gain, bias = vec_row(vec, ROW_G1), vec_row(vec, ROW_B1)
    for s, t in enumerate((t0, t1, t2, t3)):
        normal, _ = row_stats(t[...].astype(f32) + shift)
        n1[s * rows : (s + 1) * rows, :] = (normal * gain + bias).astype(bf16)
    width = d // DEPTH
    head = width // PLANE
    at = pl.ds(pl.multiple_of(z * width, width), width)
    held = vec
    biases = jnp.concatenate(
        [held[ROW_QB : ROW_QB + 1, at].astype(f32), jnp.zeros((1, width), f32), held[ROW_VB : ROW_VB + 1, at].astype(f32)],
        1,
    )
    first = lax.broadcasted_iota(jnp.int32, (8, 3 * width), 0) == 0
    biases = jnp.where(first, biases, 0.0).astype(bf16)
    ones = jnp.ones((8, DEPTH * rows), bf16)
    mover.wait(pending)
    mover.start(w, w_out)
    found = mul(w[...].reshape(d, 3 * width), n1[...], 0, 1) + mul(biases, ones, 0, 0)
    proj[...] = found.astype(bf16).reshape(proj.shape)
    for k, out in enumerate((o0, o1, o2, o3)):
        for part in range(3):
            mover.start(proj.at[part * PLANE + (yx ^ k)], out.at[part * head : (part + 1) * head])


def fill_heads(seg_row, count, blocks, qa, ka, vt):
    head = blocks[0].shape[0] // 3
    span = blocks[0].shape[1]
    seg = jnp.concatenate([seg_row[...]] * (span // seg_row.shape[1]), 1)
    slots = lax.broadcasted_iota(jnp.int32, (16, span), 0)
    hot, real = jnp.where(slots == seg, 1.0, 0.0), slots < count
    q_mark = jnp.where(real, (hot - 1.0) * BIG, 0.0).astype(bf16)
    k_mark = jnp.where(real, hot, 0.0).astype(bf16)
    rest = qa.shape[0] - head - 16
    for k, block in enumerate(blocks):
        cols = slice(k * span, (k + 1) * span)
        qa[0:head, cols] = block[0:head, :] * jnp.asarray(score_scale, bf16)
        qa[head : head + 16, cols] = q_mark
        qa[head + 16 :, cols] = jnp.zeros((rest, span), bf16)
        keys = jnp.concatenate([block[head : 2 * head, :], k_mark, jnp.zeros((rest, span), bf16)], 0)
        ka[cols, :] = keys.T
        vt[:, cols] = block[2 * head :, :]


def attend_kernel(count, mover, seg_row, b0, b1, b2, b3, o0, o1, o2, o3, lse, qa, ka, vt):
    fill_heads(seg_row, count, (b0, b1, b2, b3), qa, ka, vt)
    span = b0.shape[1]
    rows = seg_row.shape[1]
    outs = (o0, o1, o2, o3)

    def step(k, carry):
        for half in range(DEPTH // 2):
            at = pl.ds(pl.multiple_of(k * span + half * 2 * rows, 2 * rows), 2 * rows)
            scores = mul(ka[...], qa[:, at], 1, 0)
            top = jnp.max(scores, 0, keepdims=True)
            soft = jnp.exp(scores - top)
            total = jnp.sum(soft, 0, keepdims=True)
            found = mul(vt[...], soft.astype(bf16), 1, 0) / total
            lse[:, at] = jnp.broadcast_to(top + jnp.log(total), (8, 2 * rows))
            for i in range(2):
                outs[half * 2 + i][:, pl.ds(pl.multiple_of(k * rows, rows), rows)] = found[
                    :, i * rows : (i + 1) * rows
                ].astype(bf16)
        return carry

    lax.fori_loop(0, PLANE, step, 0)


def out_kernel(mover, pos, a0, a1, a2, a3, ff, p0, p1, p2, p3, att, w_out):
    z = pos[0]
    head = a0.shape[0]
    rows, d = p0.shape
    pending = [mover.start(ff.at[:, :, 2 * PLANE], w_out)]
    for u, block in enumerate((a0, a1, a2, a3)):
        att[pl.ds(pl.multiple_of((z ^ u) * head, head), head), :] = block[...]
    mover.wait(pending)
    found = mul(att[...], w_out[...].reshape(-1, d), 0, 0)
    for j, out in enumerate((p0, p1, p2, p3)):
        out[...] = found[j * rows : (j + 1) * rows, :].astype(out.dtype)


def norm_kernel(mover, lead, seg_row, vec, tok, p0, p1, p2, p3, middle, n2):
    shift = mul(lead_hot(lead, seg_row), vec[0:LEADS, :], 0, 0) + vec_row(vec, ROW_OB)
    total = p0[...].astype(f32) + p1[...].astype(f32) + p2[...].astype(f32) + p3[...].astype(f32)
    total = tok[...].astype(f32) + shift + total
    middle[...] = total
    normal, _ = row_stats(total)
    n2[...] = (normal * vec_row(vec, ROW_G2) + vec_row(vec, ROW_B2)).astype(bf16)


def ffn_kernel(mover, pos, up_b, n0, n1, n2, n3, d_outs, ff, act, d_hid, p0, p1, p2, p3, d_up_b, w_up, w_down, hid):
    yx = pos[1]
    rows, d = n0.shape
    for_up = [mover.start(ff.at[:, c, 0:PLANE], w_up.at[:, :, c]) for c in range(2)]
    for_down = [mover.start(ff.at[:, c, PLANE : 2 * PLANE], w_down.at[c]) for c in range(2)]
    mover.wait(for_up)
    normed = jnp.concatenate([n0[...], n1[...], n2[...], n3[...]], 0)
    up = w_up[...].reshape(d, -1)
    hid[...] = mul(normed, up, 1, 0) + up_b[...].astype(f32)
    mover.wait(for_down)
    down = w_down[...].reshape(-1, d)
    sums = jnp.zeros(d_up_b.shape, f32)
    for j in range(PLANE):
        here = slice(j * rows, (j + 1) * rows)
        hidden = hid[here, :]
        phi = 0.5 * (1.0 + lax.erf(hidden * 0.7071067811865476))
        act[here, :] = (hidden * phi).astype(bf16)
        slope = phi + hidden * (jnp.exp(-0.5 * hidden * hidden) * 0.3989422804014327)
        d_act = mul(d_outs[yx ^ j], down, 1, 1)
        low = (d_act * slope).astype(bf16)
        d_hid[here, :] = low
        sums = sums + jnp.sum(low.astype(f32), 0, keepdims=True)
    d_up_b[...] = sums
    back = mul(d_hid[...], up, 1, 1)
    for j, out in enumerate((p0, p1, p2, p3)):
        out[...] = back[j * rows : (j + 1) * rows, :].astype(out.dtype)


def ffn_grad_kernel(mover, pos, act, d_hid, n0, n1, n2, n3, ff, d_outs, grads, outs, up_grad, down_grad, w_down):
    yx = pos[1]
    rows, d = outs.shape[1:]
    pending = [mover.start(ff.at[:, c, PLANE : 2 * PLANE], w_down.at[c]) for c in range(2)]
    normed = jnp.concatenate([n0[...], n1[...], n2[...], n3[...]], 0)
    up_grad[...] = mul(normed, d_hid[...], 0, 0).astype(bf16).reshape(up_grad.shape)
    for c in range(2):
        mover.start(up_grad.at[:, :, c], grads.at[:, c, 0:PLANE])
    d_down = jnp.zeros((act.shape[1], d), f32)
    for j in range(PLANE):
        d_down = d_down + mul(act[j * rows : (j + 1) * rows, :], d_outs[yx ^ j], 0, 0)
    down_grad[...] = d_down.astype(bf16).reshape(down_grad.shape)
    for c in range(2):
        mover.start(down_grad.at[c], grads.at[:, c, PLANE:])
    mover.wait(pending)
    found = mul(act[...], w_down[...].reshape(-1, d), 1, 0)
    for j in range(PLANE):
        outs[yx ^ j] = found[j * rows : (j + 1) * rows, :].astype(bf16)


def ffn_last_kernel(mover, shard, ups, down):
    ups[...] = shard[0:PLANE]
    down[...] = shard[PLANE:].astype(f32).reshape(down.shape)


def branch_kernel(mover, vec, middle, d_out, p0, p1, p2, p3, d_mid, d_branch, d_vec):
    dy = p0[...].astype(f32) + p1[...].astype(f32) + p2[...].astype(f32) + p3[...].astype(f32)
    normal, inv = row_stats(middle[...])
    d_rows = d_out[...].astype(f32)
    total = d_rows + norm_back(dy * vec_row(vec, ROW_G2), normal, inv)
    d_mid[...] = total
    low = total.astype(bf16)
    d_branch[...] = low
    sums = [jnp.sum(v, 0, keepdims=True) for v in (dy * normal, dy, d_rows, low.astype(f32))]
    d_vec[...] = jnp.concatenate(sums + [jnp.zeros((4, dy.shape[1]), f32)], 0)


def out_back_kernel(mover, pos, att, w_out, b0, b1, b2, b3, o0, o1, o2, o3, grad, d_att):
    z = pos[0]
    head = o0.shape[0]
    branch = jnp.concatenate([b0[...], b1[...], b2[...], b3[...]], 0)
    d = branch.shape[1]
    d_att[...] = mul(w_out[...].reshape(-1, d), branch, 1, 1).astype(bf16).reshape(d_att.shape)
    for u, out in enumerate((o0, o1, o2, o3)):
        out[...] = d_att[z ^ u]
    grad[...] = mul(att[...], branch, 1, 0).astype(bf16).reshape(grad.shape)


def attend_back_kernel(count, mover, seg_row, b0, b1, b2, b3, c0, c1, c2, c3, lse,
                       o0, o1, o2, o3, qa, ka, vt, vn, dot, dq, dk, dv):
    fill_heads(seg_row, count, (b0, b1, b2, b3), qa, ka, vt)
    span = b0.shape[1]
    rows = seg_row.shape[1]
    head, total = vt.shape
    for k in range(PLANE):
        cols = slice(k * span, (k + 1) * span)
        vn[cols, :] = vt[:, cols].T
        for s, block in enumerate((c0, c1, c2, c3)):
            dot[:, k * span + s * rows : k * span + (s + 1) * rows] = block[:, k * rows : (k + 1) * rows]
    dk[...] = jnp.zeros_like(dk)
    dv[...] = jnp.zeros_like(dv)
    logs = lse

    def step(i, carry):
        at = pl.ds(pl.multiple_of(i * 2 * rows, 2 * rows), 2 * rows)
        scores = mul(ka[...], qa[:, at], 1, 0)
        soft = jnp.exp(scores - logs[0:1, at])
        d_out = dot[:, at]
        d_soft = mul(vn[...], d_out, 1, 0)
        delta = jnp.sum(soft * d_soft, 0, keepdims=True)
        d_scores = (soft * (d_soft - delta)).astype(bf16)
        dv[...] += mul(d_out, soft.astype(bf16), 1, 1)
        dk[...] += mul(qa[0:head, at], d_scores, 1, 1)
        dq[:, at] = (mul(ka[:, 0:head], d_scores, 0, 0) * score_scale).astype(bf16)
        return carry

    lax.fori_loop(0, total // (2 * rows), step, 0)
    for k, out in enumerate((o0, o1, o2, o3)):
        cols = slice(k * span, (k + 1) * span)
        out[0:head, :] = dq[:, cols]
        out[head : 2 * head, :] = dk[:, cols].astype(bf16)
        out[2 * head :, :] = dv[:, cols].astype(bf16)


def join_heads(yx, blocks, joined):
    head = blocks[0].shape[0] // 3
    for k, block in enumerate(blocks):
        for part in range(3):
            joined[part * PLANE + (yx ^ k)] = block[part * head : (part + 1) * head, :]
    return joined[...].reshape(3 * PLANE * head, -1)


def qkv_back_kernel(mover, pos, w, g0, g1, g2, g3, r0, r1, r2, r3, back, joined):
    grads = join_heads(pos[1], (g0, g1, g2, g3), joined)
    rows, d = r0.shape
    found = mul(grads, w[...].reshape(d, -1), 0, 1)
    back[...] = found
    for s, out in enumerate((r0, r1, r2, r3)):
        out[...] = found[s * rows : (s + 1) * rows, :].astype(out.dtype)


def qkv_grad_kernel(mover, pos, lead, seg_row, vec, t0, t1, t2, t3, n1, g0, g1, g2, g3, back, d_mid, d_mid_vec, d_up_b,
                    out, joined, d_vec):
    z, yx = pos[0], pos[1]
    rows, d = t0.shape
    width = d // DEPTH
    grads = join_heads(yx, (g0, g1, g2, g3), joined)
    rw = out.shape[3]
    cols = 3 * width
    grad = mul(n1[...], grads, 0, 1).astype(bf16)
    hot = lead_hot(lead, seg_row)
    shift = mul(hot, vec[0:LEADS, :], 0, 0)
    gain = vec_row(vec, ROW_G1)
    d_gain = jnp.zeros((1, d), f32)
    d_bias = jnp.zeros((1, d), f32)
    d_emb = d_mid[...]
    for s, t in enumerate((t0, t1, t2, t3)):
        piece = back[s * rows : (s + 1) * rows, :]
        normal, inv = row_stats(t[...].astype(f32) + shift)
        d_gain = d_gain + jnp.sum(piece * normal, 0, keepdims=True)
        d_bias = d_bias + jnp.sum(piece, 0, keepdims=True)
        d_emb = d_emb + norm_back(piece * gain, normal, inv)
    high = d_emb.astype(bf16)
    low = (d_emb - high.astype(f32)).astype(bf16)
    d_vec[...] = jnp.zeros_like(d_vec)
    d_vec[0:LEADS, :] = mul(hot, high, 1, 0) + mul(hot, low, 1, 0)
    sums = mul(jnp.ones((8, DEPTH * rows), bf16), grads, 1, 1)
    d_vec[ROW_G1 : ROW_G1 + 1, :] = d_gain
    d_vec[ROW_B1 : ROW_B1 + 1, :] = d_bias
    at = pl.ds(pl.multiple_of(z * width, width), width)
    d_vec[ROW_QB : ROW_QB + 1, at] = sums[0:1, 0:width]
    d_vec[ROW_VB : ROW_VB + 1, at] = sums[0:1, 2 * width :]
    for i, row in enumerate((ROW_G2, ROW_B2, ROW_DB, ROW_OB)):
        d_vec[row : row + 1, :] = d_mid_vec[i : i + 1, :]
    small = d_vec[...].astype(bf16)
    fr = out.shape[4] - cols
    for zz in range(DEPTH):
        for k in range(PLANE):
            for c in range(2):
                i = (zz * PLANE + k) * 2 + c
                out[k, c, zz, :, 0:cols] = grad[i * rw : (i + 1) * rw, :]
                side = jnp.concatenate([small[:, i * rw : (i + 1) * rw], jnp.zeros((rw, fr - rw), bf16)], 1)
                start = (c * DEPTH + zz) * fr
                last = jnp.where(yx == k, d_up_b[:, start : start + fr], 0.0).astype(bf16)
                mark = lax.broadcasted_iota(jnp.int32, (rw, fr), 0) == VEC_ROWS
                out[k, c, zz, :, cols:] = jnp.where(mark, last.astype(f32), side.astype(f32)).astype(bf16)


def first_back_kernel(mover, lead, seg_row, vec, tok, d_mid, r0, r1, r2, r3, out):
    shift = mul(lead_hot(lead, seg_row), vec[0:LEADS, :], 0, 0)
    normal, inv = row_stats(tok[...].astype(f32) + shift)
    dy = r0[...].astype(f32) + r1[...].astype(f32) + r2[...].astype(f32) + r3[...].astype(f32)
    out[...] = d_mid[...] + norm_back(dy * vec_row(vec, ROW_G1), normal, inv)


def layer_out_kernel(mover, vec, middle, blocks, out):
    total = middle[...] + vec_row(vec, ROW_DB)
    for k in range(PLANE):
        total = total + blocks[k].astype(f32)
    out[...] = total.astype(bf16)


def octet_kernel(mover, pos, blocks, o0, o1, o2, o3, total):
    found = jnp.zeros(total.shape, f32)
    for k in range(PLANE):
        for c in range(2):
            found = found + blocks[k, c].astype(f32)
    total[...] = found.astype(bf16)
    for u, out in enumerate((o0, o1, o2, o3)):
        out[...] = total[pos[0] ^ u]


def qkv_join_kernel(mover, pos, b0, b1, b2, b3, out, table, *rest):
    z = pos[0]
    rw = out.shape[0]
    width = out.shape[1] // (3 * DEPTH)
    side = jnp.zeros((rw, b0.shape[1] - 3 * width), f32)
    for s, block in enumerate((b0, b1, b2, b3)):
        for part in range(3):
            start = pl.multiple_of((part * DEPTH + (z ^ s)) * width, width)
            out[:, pl.ds(start, width)] = block[:, part * width : (part + 1) * width].astype(f32)
        side = side + block[:, 3 * width :].astype(f32)
    table[...] = side[0:LEADS, 0:rw]
    for i, row in enumerate(rest[:-1]):
        row[...] = side[LEADS + i : LEADS + i + 1, 0:rw]
    rest[-1][...] = side[VEC_ROWS : VEC_ROWS + 1, :]


def up_join_kernel(mover, blocks, out):
    fr = blocks.shape[2] // (2 * DEPTH)
    for k in range(PLANE):
        for c in range(2):
            for zz in range(DEPTH):
                src = (c * DEPTH + zz) * fr
                dst = ((zz * PLANE + k) * 2 + c) * fr
                out[:, dst : dst + fr] = blocks[k, :, src : src + fr].astype(f32)


COSTS = {
    "q_prep_kernel": (1, 4), "q_stack_kernel": (1, 4), "up_prep_kernel": (1, 4), "shard_kernel": (1, 4), "qkv_kernel": (5, 20),
    "attend_kernel": (11, 16), "out_kernel": (2, 12), "norm_kernel": (2, 8), "ffn_kernel": (8, 32), "ffn_grad_kernel": (8, 32),
    "branch_kernel": (2, 12), "out_back_kernel": (3, 12), "attend_back_kernel": (19, 24),
    "qkv_back_kernel": (3, 16), "qkv_grad_kernel": (6, 24), "first_back_kernel": (2, 8), "layer_out_kernel": (1, 8),
    "octet_kernel": (2, 8), "qkv_join_kernel": (1, 4), "up_join_kernel": (2, 8), "ffn_last_kernel": (1, 8),
}
PLANE_AXES = ("y", "x")


def trade(blocks, axes):
    return lax.all_to_all(blocks, axes, split_axis=0, concat_axis=0, tiled=True)


ALL = ("z", "y", "x", "g")


def across(blocks):
    swap = [(0, 1), (1, 0)]
    return (
        blocks[0],
        lax.ppermute(blocks[1], "x", swap),
        lax.ppermute(blocks[2], "y", swap),
        lax.ppermute(blocks[3], ("y", "x"), [(i, i ^ 3) for i in range(PLANE)]),
    )


def to_depth(block, step):
    return lax.ppermute(block, "z", [(i, i ^ step) for i in range(DEPTH)])


def along(blocks):
    return (blocks[0],) + tuple(to_depth(blocks[u], u) for u in range(1, DEPTH))


def spread(block):
    far = to_depth(block, 2)
    return block, to_depth(block, 1), far, to_depth(far, 1)


def core_swap(block):
    return lax.ppermute(block, "g", [(0, 1), (1, 0)])


def far(blocks):
    return [Far(block) for block in blocks]


def raw(blocks):
    return [Raw(block) for block in blocks]


def fast_local(
    tokens, segment_ids, lead_index, lead_table, ln1_gain, ln1_bias, qkv_weight, q_bias, v_bias,
    out_weight, out_bias, ln2_gain, ln2_bias, up_weight, up_bias, down_weight, down_bias, d_out,
):
    z = lax.axis_index("z")
    yx = lax.axis_index("y") * 2 + lax.axis_index("x")
    c = lax.axis_index("g")
    pos = jnp.stack([z, yx, c]).astype(jnp.int32)
    tok, d_rows = tokens[0], d_out[0]
    rows, d = tok.shape
    head = d // HEADS
    span = DEPTH * rows
    group = PLANE * span
    rw = qkv_weight.shape[0]
    fr = down_weight.shape[0]
    ff = 2 * DEPTH * fr
    devices = DEPTH * PLANE * 2
    lead = lead_index[0]
    count = lead.shape[0]
    width = 3 * d // DEPTH
    seg_row = segment_ids
    up_shape, down_shape = (DEPTH, PLANE, 2, rw, ff), (2, DEPTH, PLANE, rw, d)

    order = []
    call = functools.partial(run, order)
    flat = jnp.concatenate(
        [lead_table.reshape(-1), ln1_gain, ln1_bias, q_bias, v_bias, out_bias, ln2_gain, ln2_bias, down_bias, up_bias]
    )
    padded = -(-flat.shape[0] // 1024) * 1024
    flat = jnp.pad(flat, (0, padded - flat.shape[0])).reshape(8, padded // 8)
    smalls = lax.all_to_all(
        jnp.broadcast_to(flat[None], (devices,) + flat.shape), ALL, split_axis=0, concat_axis=0, tiled=True
    ).reshape(devices, padded)
    vec = smalls[:, : VEC_ROWS * rw].reshape(devices, VEC_ROWS, rw).transpose(1, 0, 2).reshape(VEC_ROWS, d)
    up_b = smalls[:, VEC_ROWS * rw : VEC_ROWS * rw + fr].reshape(DEPTH, PLANE, 2, fr)
    up_b = lax.dynamic_index_in_dim(up_b, yx, 1, keepdims=False).transpose(1, 0, 2).reshape(1, ff)

    q_rows = along(call(q_prep_kernel, [((rw, width), bf16)] * 4, [pos, qkv_weight]))
    toks = spread(tok)
    (up_cols,) = call(up_prep_kernel, [((PLANE, rw, ff), bf16)], [up_weight])
    up_cols = trade(up_cols, PLANE_AXES)
    d_outs = lax.all_gather(d_rows, PLANE_AXES, axis=0)
    (q_stack,) = call(
        q_stack_kernel, [((DEPTH, rw, width), bf16)], [pos, *q_rows], after=[flat, toks[2]]
    )
    q_plane = across((q_stack,) * PLANE)
    q_other = [core_swap(block) for block in q_plane]
    (ff_shard,) = call(
        shard_kernel, [((2 * PLANE + 1, rw, d), bf16, "far")], [up_cols, down_weight, out_weight], after=[smalls]
    )
    ff_all = lax.all_gather(ff_shard, ("z", "g"), axis=0).reshape(DEPTH, 2, 2 * PLANE + 1, rw, d)
    n1, w_qkv, *blocks = call(
        qkv_kernel,
        [((span, d), bf16, "far"), ((DEPTH, PLANE, 2, rw, width), bf16, "raw")] + [((3 * head, span), bf16)] * 4,
        [pos, lead, seg_row, vec, *toks, *q_plane, *q_other],
        [((DEPTH, PLANE, 2, rw, width), bf16), ((3 * PLANE, head, span), bf16)],
    )
    blocks = across(blocks)

    *att_parts, lse = call(
        functools.partial(attend_kernel, count),
        [((head, PLANE * rows), bf16)] * 4 + [((8, group), f32)],
        [seg_row, *blocks],
        [((128, group), bf16), ((group, 128), bf16), ((head, group), bf16)],
    )
    att_parts = along(att_parts)
    *parts, att, w_out = call(
        out_kernel,
        [((rows, d), f32)] + [((rows, d), bf16)] * 3 + [((DEPTH * head, span), bf16), ((DEPTH, 2, rw, d), bf16)],
        [pos, *att_parts, Raw(ff_all)],
    )
    parts = across(parts)
    middle, n2 = call(norm_kernel, [((rows, d), f32, "far"), ((rows, d), bf16)], [lead, seg_row, vec, Far(tok), *parts])
    n2_plane = across((n2,) * PLANE)

    act, d_hid, p0, p1, p2, p3, d_up_b = call(
        ffn_kernel,
        [((span, ff), bf16), ((span, ff), bf16), ((rows, d), f32)] + [((rows, d), bf16)] * 3 + [((1, ff), f32)],
        [pos, up_b, *n2_plane, Far(d_outs), Raw(ff_all)],
        [(up_shape, bf16), (down_shape, bf16), ((span, ff), f32)],
    )
    parts = across((p0, p1, p2, p3))
    ff_grad, outs = call(
        ffn_grad_kernel,
        [((DEPTH, 2, 2 * PLANE, rw, d), bf16, "raw"), ((PLANE, rows, d), bf16, "far")],
        [pos, act, d_hid, *n2_plane, Raw(ff_all), Far(d_outs)],
        [(up_shape, bf16), (down_shape, bf16), (down_shape, bf16)],
        after=[parts[1]],
    )
    ff_grad = lax.psum_scatter(
        ff_grad.reshape(2 * DEPTH, 2 * PLANE, rw, d), ("z", "g"), scatter_dimension=0, tiled=True
    )[0]
    d_mid, d_branch, d_mid_vec = call(
        branch_kernel,
        [((rows, d), f32, "far"), ((rows, d), bf16), ((8, d), f32)],
        [vec, Far(middle), Far(d_rows), *parts],
    )
    branch_plane = across((d_branch,) * PLANE)
    *d_att, out_grad = call(
        out_back_kernel,
        [((head, span), bf16)] * 4 + [((DEPTH, 2, rw, d), bf16, "far")],
        [pos, att, w_out, *branch_plane],
        [((DEPTH, head, span), bf16)],
    )
    d_att = along(d_att)
    outs = trade(outs, PLANE_AXES)
    d_out_weight = lax.psum_scatter(
        out_grad.reshape(2 * DEPTH, rw, d), ("z", "g"), scatter_dimension=0, tiled=True
    )[0].astype(f32)

    d_blocks = call(
        functools.partial(attend_back_kernel, count),
        [((3 * head, span), bf16)] * 4,
        [seg_row, *blocks, *d_att, lse],
        [((128, group), bf16), ((group, 128), bf16), ((head, group), bf16), ((group, head), bf16),
         ((head, group), bf16), ((head, group), bf16), ((head, group), f32), ((head, group), f32)],
    )
    d_blocks = across(d_blocks)
    (layer_out,) = call(layer_out_kernel, [((rows, d), bf16)], [vec, Far(middle), outs])
    ups, d_down = call(ffn_last_kernel, [((PLANE, rw, ff), bf16), ((fr, d), f32)], [ff_grad])
    ups = trade(ups, PLANE_AXES)
    *returned, back = call(
        qkv_back_kernel,
        [((rows, d), f32)] + [((rows, d), bf16)] * 3 + [((span, d), f32)],
        [pos, Far(w_qkv), *d_blocks],
        [((3 * PLANE, head, span), bf16)],
        after=[ups],
    )
    returned = along(returned)
    side = width + -(-max(rw, fr) // 128) * 128
    (octets,) = call(
        qkv_grad_kernel,
        [((PLANE, 2, DEPTH, rw, side), bf16)],
        [pos, lead, seg_row, vec, *far(toks), Far(n1), *d_blocks, back, Far(d_mid), d_mid_vec, d_up_b],
        [((3 * PLANE, head, span), bf16), ((rw, d), f32)],
    )
    octets = trade(octets.reshape(2 * PLANE, DEPTH, rw, side), ("y", "x", "g")).reshape(octets.shape)
    (d_up,) = call(up_join_kernel, [((rw, PLANE * ff), f32)], [ups])
    (d_tokens,) = call(
        first_back_kernel, [((rows, d), f32)], [lead, seg_row, vec, Far(tok), Far(d_mid), *returned]
    )
    cols = along(call(octet_kernel, [((rw, side), bf16)] * 4, [pos, octets], [((DEPTH, rw, side), bf16)]))
    d_qkv, table, *smalls, d_ub = call(
        qkv_join_kernel,
        [((rw, 3 * d), f32), ((LEADS, rw), f32)] + [((1, rw), f32)] * 8 + [((1, fr), f32)],
        [pos, *cols],
    )
    d_g1, d_b1, d_qb, d_vb, d_ob, d_g2, d_b2, d_db, d_ub = (small[0] for small in (*smalls, d_ub))
    return (
        layer_out[None], d_tokens[None], table, d_g1, d_b1, d_qkv, d_qb, d_vb, d_out_weight, d_ob,
        d_g2, d_b2, d_up, d_ub, d_down, d_db,
    )


def specs(band, grp):
    every = band + grp
    rows = P(grp, band, None)
    in_specs = (
        rows, P(grp, band), P(grp, None), P(None, every), P(every), P(every), P(every, None), P(every), P(every),
        P(every, None), P(every), P(every), P(every), P(every, None), P(every), P(every, None), P(every), rows,
    )
    out_specs = (
        rows, rows, P(None, every), P(every), P(every), P(every, None), P(every), P(every), P(every, None), P(every),
        P(every), P(every), P(every, None), P(every), P(every, None), P(every),
    )
    return in_specs, out_specs


def solution(mesh):
    band, grp = mesh.shape["band"], mesh.shape["grp"]
    if band == HEADS and grp == 2:
        mesh = Mesh(mesh.devices.reshape(DEPTH, 2, 2, grp), ("z", "y", "x", "g"))
        in_specs, out_specs = specs(("z", "y", "x"), ("g",))
        return jax.shard_map(fast_local, mesh=mesh, in_specs=in_specs, out_specs=out_specs, check_vma=False)
    in_specs, out_specs = specs(("band",), ("grp",))
    return jax.shard_map(local, mesh=mesh, in_specs=in_specs, out_specs=out_specs, check_vma=False)
```

```python
import functools
import math

import jax
import jax.numpy as jnp
from jax import lax
from jax.experimental import pallas as pl
from jax.experimental.pallas import tpu as pltpu
from jax.sharding import Mesh
from jax.sharding import PartitionSpec as P

bf16, f32 = jnp.bfloat16, jnp.float32

HEADS = 16


epsilon = 1e-05
score_scale = 0.125
masked_score = -1e30


def norm_rows(values, norm_gain, norm_bias):
    row_mean = jnp.mean(values, -1, keepdims=True)
    centred = values - row_mean
    row_var = jnp.mean(centred * centred, -1, keepdims=True)
    return centred * lax.rsqrt(row_var + epsilon) * norm_gain + norm_bias


def gelu_exact(values):
    return jax.nn.gelu(values, approximate=False)


def split_blocks(values, block_rows):
    return values.reshape((values.shape[0] // block_rows, block_rows) + values.shape[1:])


def block_scores(query_heads, key_heads, allowed):
    raw_scores = (
        jnp.einsum("qhd,khd->hqk", query_heads, key_heads, preferred_element_type=jnp.float32)
        * score_scale
    )
    return jnp.where(allowed[None], raw_scores, masked_score)


def softmax_rows(query_heads, key_heads, allowed, log_total):
    scores = block_scores(query_heads, key_heads, allowed)
    return jnp.where(allowed[None], jnp.exp(scores - log_total[:, :, None]), 0.0)


def score_grads(query_heads, key_heads, value_heads, d_heads, allowed, log_total, row_delta):
    soft_rows = softmax_rows(query_heads, key_heads, allowed, log_total)
    d_soft = jnp.einsum("qhd,khd->hqk", d_heads, value_heads, preferred_element_type=jnp.float32)
    d_scores = (soft_rows * (d_soft - row_delta[:, :, None])).astype(jnp.bfloat16)
    return (soft_rows.astype(jnp.bfloat16), d_scores)


def local(
    tokens,
    segment_ids,
    lead_index,
    lead_table,
    ln1_gain,
    ln1_bias,
    qkv_weight,
    q_bias,
    v_bias,
    out_weight,
    out_bias,
    ln2_gain,
    ln2_bias,
    up_weight,
    up_bias,
    down_weight,
    down_bias,
    d_out,
):
    (
        table_full,
        first_gain,
        first_shift,
        project_full,
        query_shift,
        value_shift,
        out_full,
        out_shift,
        second_gain,
        second_shift,
        up_full,
        up_shift,
        down_full,
        down_shift,
    ) = (
        lax.all_gather(lead_table, ("band", "grp"), axis=1, tiled=True),
        lax.all_gather(ln1_gain, ("band", "grp"), axis=0, tiled=True),
        lax.all_gather(ln1_bias, ("band", "grp"), axis=0, tiled=True),
        lax.all_gather(qkv_weight, ("band", "grp"), axis=0, tiled=True),
        lax.all_gather(q_bias, ("band", "grp"), axis=0, tiled=True),
        lax.all_gather(v_bias, ("band", "grp"), axis=0, tiled=True),
        lax.all_gather(out_weight, ("band", "grp"), axis=0, tiled=True),
        lax.all_gather(out_bias, ("band", "grp"), axis=0, tiled=True),
        lax.all_gather(ln2_gain, ("band", "grp"), axis=0, tiled=True),
        lax.all_gather(ln2_bias, ("band", "grp"), axis=0, tiled=True),
        lax.all_gather(up_weight, ("band", "grp"), axis=0, tiled=True),
        lax.all_gather(up_bias, ("band", "grp"), axis=0, tiled=True),
        lax.all_gather(down_weight, ("band", "grp"), axis=0, tiled=True),
        lax.all_gather(down_bias, ("band", "grp"), axis=0, tiled=True),
    )
    tok_rows = tokens.shape[1]
    features = tokens.shape[2]
    head_dim = features // HEADS
    band_count = lax.axis_size("band")
    group_rows = tok_rows * band_count
    block_rows = math.gcd(group_rows, 1024)
    own_segments = segment_ids[0]
    group_segments = jnp.tile(own_segments, band_count)
    sample_count = lead_index.shape[1]
    lead_count = lead_table.shape[0]
    sample_hot = (
        own_segments[:, None] == jnp.arange(sample_count, dtype=jnp.int32)[None, :]
    ).astype(jnp.float32)
    lead_hot = (lead_index[0][:, None] == jnp.arange(lead_count, dtype=jnp.int32)[None, :]).astype(
        jnp.float32
    )
    lead_pick = jnp.dot(sample_hot, lead_hot, precision=lax.Precision.HIGHEST)
    embedded = tokens[0].astype(jnp.float32) + jnp.dot(
        lead_pick.astype(jnp.bfloat16), table_full, preferred_element_type=jnp.float32
    )
    normed_first = norm_rows(
        embedded, first_gain.astype(jnp.float32), first_shift.astype(jnp.float32)
    ).astype(jnp.bfloat16)
    projected = jnp.dot(normed_first, project_full, preferred_element_type=jnp.float32)
    query_rows = (projected[:, :features] + query_shift.astype(jnp.float32)).astype(jnp.bfloat16)
    key_rows = projected[:, features : 2 * features].astype(jnp.bfloat16)
    value_rows = (projected[:, 2 * features :] + value_shift.astype(jnp.float32)).astype(
        jnp.bfloat16
    )
    key_all, value_all = (
        lax.all_gather(key_rows, "band", axis=0, tiled=True),
        lax.all_gather(value_rows, "band", axis=0, tiled=True),
    )
    query_heads = query_rows.reshape(tok_rows, HEADS, head_dim)
    key_blocks = split_blocks(key_all.reshape(group_rows, HEADS, head_dim), block_rows)
    value_blocks = split_blocks(value_all.reshape(group_rows, HEADS, head_dim), block_rows)
    segment_blocks = split_blocks(group_segments, block_rows)

    def stats_step(running, block_data):
        running_max, running_sum = running
        key_block, key_segments = block_data
        allowed = own_segments[:, None] == key_segments[None, :]
        scores = block_scores(query_heads, key_block, allowed)
        new_max = jnp.maximum(running_max, jnp.max(scores, -1))
        block_sum = jnp.sum(
            jnp.where(allowed[None], jnp.exp(scores - new_max[:, :, None]), 0.0), -1
        )
        return ((new_max, running_sum * jnp.exp(running_max - new_max) + block_sum), None)

    start_max = jnp.full((HEADS, tok_rows), masked_score, jnp.float32)
    start_sum = jnp.zeros((HEADS, tok_rows), jnp.float32)
    (final_max, final_sum), unused_out = lax.scan(
        stats_step, (start_max, start_sum), (key_blocks, segment_blocks)
    )
    log_total = final_max + jnp.log(final_sum)

    def output_step(running, block_data):
        high_part, low_part = running
        key_block, value_block, key_segments = block_data
        allowed = own_segments[:, None] == key_segments[None, :]
        soft_rows = softmax_rows(query_heads, key_block, allowed, log_total)
        soft_low = soft_rows.astype(jnp.bfloat16)
        soft_rest = (soft_rows - soft_low.astype(jnp.float32)).astype(jnp.bfloat16)
        high_part = high_part + jnp.einsum(
            "hqk,khd->qhd", soft_low, value_block, preferred_element_type=jnp.float32
        )
        low_part = low_part + jnp.einsum(
            "hqk,khd->qhd", soft_rest, value_block, preferred_element_type=jnp.float32
        )
        return ((high_part, low_part), None)

    empty_heads = jnp.zeros((tok_rows, HEADS, head_dim), jnp.float32)
    (attn_high, attn_low), unused_out = lax.scan(
        output_step, (empty_heads, empty_heads), (key_blocks, value_blocks, segment_blocks)
    )
    attended = attn_high.reshape(tok_rows, features).astype(jnp.bfloat16)
    middle = (
        embedded
        + jnp.dot(attended, out_full, preferred_element_type=jnp.float32)
        + out_shift.astype(jnp.float32)
    )
    normed_second = norm_rows(
        middle, second_gain.astype(jnp.float32), second_shift.astype(jnp.float32)
    ).astype(jnp.bfloat16)
    hidden = jnp.dot(normed_second, up_full, preferred_element_type=jnp.float32) + up_shift.astype(
        jnp.float32
    )
    activated = gelu_exact(hidden).astype(jnp.bfloat16)
    result = (
        middle
        + jnp.dot(activated, down_full, preferred_element_type=jnp.float32)
        + down_shift.astype(jnp.float32)
    )
    layer_out = result.astype(jnp.bfloat16)[None]
    first_gain_back, project_back, out_back, second_gain_back, up_back, down_back = (
        lax.all_gather(ln1_gain, ("band", "grp"), axis=0, tiled=True),
        lax.all_gather(qkv_weight, ("band", "grp"), axis=0, tiled=True),
        lax.all_gather(out_weight, ("band", "grp"), axis=0, tiled=True),
        lax.all_gather(ln2_gain, ("band", "grp"), axis=0, tiled=True),
        lax.all_gather(up_weight, ("band", "grp"), axis=0, tiled=True),
        lax.all_gather(down_weight, ("band", "grp"), axis=0, tiled=True),
    )
    d_rows = d_out[0]
    d_down_shift = jnp.sum(d_rows.astype(jnp.float32), 0)
    d_down = jnp.einsum("tf,td->fd", activated, d_rows, preferred_element_type=jnp.float32)
    d_act = jnp.einsum("td,fd->tf", d_rows, down_back, preferred_element_type=jnp.float32)
    unused_gelu, gelu_back = jax.vjp(gelu_exact, hidden)
    d_hidden = gelu_back(d_act)[0].astype(jnp.bfloat16)
    d_up_shift = jnp.sum(d_hidden.astype(jnp.float32), 0)
    d_up = jnp.einsum("td,tf->df", normed_second, d_hidden, preferred_element_type=jnp.float32)
    d_normed_second = jnp.einsum("tf,df->td", d_hidden, up_back, preferred_element_type=jnp.float32)
    unused_second, second_back = jax.vjp(
        norm_rows, middle, second_gain_back.astype(jnp.float32), second_shift.astype(jnp.float32)
    )
    d_middle_part, d_gain_second, d_shift_second = second_back(d_normed_second)
    d_middle = d_rows.astype(jnp.float32) + d_middle_part
    d_branch = d_middle.astype(jnp.bfloat16)
    d_out_shift = jnp.sum(d_branch.astype(jnp.float32), 0)
    d_out_full = jnp.einsum("ti,to->io", attended, d_branch, preferred_element_type=jnp.float32)
    d_attended = jnp.einsum(
        "to,io->ti", d_branch, out_back, preferred_element_type=jnp.float32
    ).astype(jnp.bfloat16)
    d_heads = d_attended.reshape(tok_rows, HEADS, head_dim)
    row_delta = jnp.sum(d_heads.astype(jnp.float32) * (attn_high + attn_low), -1).T

    def query_grad(d_query_acc, key_block, value_block, key_segments):
        allowed = own_segments[:, None] == key_segments[None, :]
        soft_low, d_scores = score_grads(
            query_heads, key_block, value_block, d_heads, allowed, log_total, row_delta
        )
        d_query_acc = d_query_acc + jnp.einsum(
            "hqk,khd->qhd", d_scores, key_block, preferred_element_type=jnp.float32
        )
        return (d_query_acc, soft_low, d_scores)

    def owner_step(d_query_acc, block_data):
        key_block, value_block, key_segments = block_data
        d_query_acc, soft_low, d_scores = query_grad(
            d_query_acc, key_block, value_block, key_segments
        )
        d_key_block = (
            jnp.einsum("hqk,qhd->khd", d_scores, query_heads, preferred_element_type=jnp.float32)
            * score_scale
        )
        d_value_block = jnp.einsum(
            "hqk,qhd->khd", soft_low, d_heads, preferred_element_type=jnp.float32
        )
        return (d_query_acc, (d_key_block, d_value_block))

    d_query_sum, (d_key_parts, d_value_parts) = lax.scan(
        owner_step, empty_heads, (key_blocks, value_blocks, segment_blocks)
    )
    d_key_sum, d_value_sum = (
        lax.psum_scatter(
            d_key_parts.reshape(group_rows, features).astype(jnp.bfloat16),
            "band",
            scatter_dimension=0,
            tiled=True,
        ).astype(jnp.float32),
        lax.psum_scatter(
            d_value_parts.reshape(group_rows, features).astype(jnp.bfloat16),
            "band",
            scatter_dimension=0,
            tiled=True,
        ).astype(jnp.float32),
    )
    d_query = (d_query_sum.reshape(tok_rows, features) * score_scale).astype(jnp.bfloat16)
    d_key = d_key_sum.astype(jnp.bfloat16)
    d_value = d_value_sum.astype(jnp.bfloat16)
    d_query_shift = jnp.sum(d_query.astype(jnp.float32), 0)
    d_value_shift = jnp.sum(d_value.astype(jnp.float32), 0)
    d_project_rows = jnp.concatenate([d_query, d_key, d_value], 1)
    d_project = jnp.einsum(
        "ti,to->io", normed_first, d_project_rows, preferred_element_type=jnp.float32
    )
    d_normed_first = jnp.einsum(
        "to,io->ti", d_project_rows, project_back, preferred_element_type=jnp.float32
    )
    unused_first, first_back = jax.vjp(
        norm_rows, embedded, first_gain_back.astype(jnp.float32), first_shift.astype(jnp.float32)
    )
    d_embed_part, d_gain_first, d_shift_first = first_back(d_normed_first)
    d_embedded = d_middle + d_embed_part
    d_table = jnp.einsum("tl,td->ld", lead_pick, d_embedded, precision=lax.Precision.HIGHEST)
    shards = (
        lax.psum_scatter(d_table, ("band", "grp"), scatter_dimension=1, tiled=True),
        lax.psum_scatter(d_gain_first, ("band", "grp"), scatter_dimension=0, tiled=True),
        lax.psum_scatter(d_shift_first, ("band", "grp"), scatter_dimension=0, tiled=True),
        lax.psum_scatter(d_project, ("band", "grp"), scatter_dimension=0, tiled=True),
        lax.psum_scatter(d_query_shift, ("band", "grp"), scatter_dimension=0, tiled=True),
        lax.psum_scatter(d_value_shift, ("band", "grp"), scatter_dimension=0, tiled=True),
        lax.psum_scatter(d_out_full, ("band", "grp"), scatter_dimension=0, tiled=True),
        lax.psum_scatter(d_out_shift, ("band", "grp"), scatter_dimension=0, tiled=True),
        lax.psum_scatter(d_gain_second, ("band", "grp"), scatter_dimension=0, tiled=True),
        lax.psum_scatter(d_shift_second, ("band", "grp"), scatter_dimension=0, tiled=True),
        lax.psum_scatter(d_up, ("band", "grp"), scatter_dimension=0, tiled=True),
        lax.psum_scatter(d_up_shift, ("band", "grp"), scatter_dimension=0, tiled=True),
        lax.psum_scatter(d_down, ("band", "grp"), scatter_dimension=0, tiled=True),
        lax.psum_scatter(d_down_shift, ("band", "grp"), scatter_dimension=0, tiled=True),
    )
    return (layer_out, d_embedded[None]) + tuple(shards)


DEPTH = 4
PLANE = 4
BIG = 1e30
HBM = pltpu.MemorySpace.HBM
VMEM = pltpu.MemorySpace.VMEM
SMEM = pltpu.MemorySpace.SMEM
LEADS = 16
ROW_G1, ROW_B1, ROW_QB, ROW_VB, ROW_OB, ROW_G2, ROW_B2, ROW_DB = range(16, 24)
VEC_ROWS = 24


def mul(left, right, over_left, over_right):
    return lax.dot_general(
        left, right, (((over_left,), (over_right,)), ((), ())), preferred_element_type=jnp.float32
    )


class Mover:
    def __init__(self, sems):
        self.sems, self.used, self.open = sems, 0, []

    def start(self, source, target):
        copy = pltpu.make_async_copy(source, target, self.sems.at[self.used])
        self.used += 1
        copy.start()
        self.open.append(copy)
        return copy

    def wait(self, copies=None):
        for copy in list(self.open if copies is None else copies):
            copy.wait()
            self.open = [other for other in self.open if other is not copy]


class Far:
    def __init__(self, value):
        self.value = value


class Raw(Far):
    pass


class Given:
    def __init__(self, ref, held, mover):
        self.ref, self.mover, self.copy = held, mover, mover.start(ref, held)
        self.shape, self.dtype = ref.shape, ref.dtype

    def ready(self):
        if self.copy is not None:
            self.mover.wait([self.copy])
            self.copy = None
        return self.ref

    def __getitem__(self, at):
        return self.ready()[at]


def run(order, kernel, outs, ins, scratch=(), after=(), alias=None):
    after = list(after) + order
    kinds = [type(a) if isinstance(a, Far) else None for a in ins]
    ins = [a.value if kind else a for a, kind in zip(ins, kinds)]
    staged = [pltpu.VMEM(a.shape, a.dtype) for a, kind in zip(ins, kinds) if kind is Far]
    outs = [o if len(o) == 3 else o + ("",) for o in outs]
    staged += [pltpu.VMEM(o[0], o[1]) for o in outs if o[2] == "far"]
    n_in, n_after, n_out, n_staged = len(ins), len(after), len(outs), len(staged)
    name = getattr(kernel, "func", kernel).__name__
    micros, room = COSTS[name]
    cost = pl.CostEstimate(flops=micros * 1_100_000_000, bytes_accessed=micros * 3_600_000, transcendentals=0)

    def body(*refs):
        mover = Mover(refs[-1])
        held = list(refs[len(refs) - 1 - n_staged : -1])
        given = [
            Given(ref, held.pop(0), mover) if kind is Far else ref for ref, kind in zip(refs[:n_in], kinds)
        ]
        refs = refs[n_in + n_after : len(refs) - 1 - n_staged]
        made = [held.pop(0) if o[2] == "far" else ref for ref, o in zip(refs, outs)]
        kernel(mover, *given, *made, *refs[n_out + 1 :])
        for ref, written, o in zip(refs, made, outs):
            if o[2] == "far":
                mover.start(written, ref)
        for operand in given:
            if isinstance(operand, Given):
                operand.ready()
        refs[n_out][...] = jnp.zeros_like(refs[n_out])
        mover.wait()

    spaces = [pl.ANY if kind else SMEM if a.dtype == jnp.int32 and a.ndim == 1 else VMEM for a, kind in zip(ins, kinds)]
    results = pl.pallas_call(
        body,
        name=name,
        out_shape=[HBM(o[0], o[1]) if o[2] else jax.ShapeDtypeStruct(o[0], o[1]) for o in outs]
        + [jax.ShapeDtypeStruct((8, 128), f32)],
        in_specs=[pl.BlockSpec(memory_space=space) for space in spaces + [pl.ANY] * n_after],
        out_specs=[pl.BlockSpec(memory_space=pl.ANY if o[2] else VMEM) for o in outs] + [pl.BlockSpec(memory_space=VMEM)],
        scratch_shapes=[pltpu.VMEM(s, d) for s, d in scratch] + staged + [pltpu.SemaphoreType.DMA((64,))],
        compiler_params=pltpu.CompilerParams(vmem_limit_bytes=room << 20),
        cost_estimate=cost,
        input_output_aliases=dict([alias] if alias else []),
    )(
        *[pltpu.with_memory_space_constraint(a, HBM) if kind else a for a, kind in zip(ins, kinds)],
        *[pltpu.with_memory_space_constraint(a, HBM) if a.size > 4096 else a for a in after],
    )
    order[:] = results[n_out:]
    return results[:n_out]


def row_stats(values):
    mean = jnp.mean(values, -1, keepdims=True)
    centred = values - mean
    inv = lax.rsqrt(jnp.mean(centred * centred, -1, keepdims=True) + epsilon)
    return centred * inv, inv


def norm_back(d_normal, normal, inv):
    first = jnp.mean(d_normal, -1, keepdims=True)
    second = jnp.mean(d_normal * normal, -1, keepdims=True)
    return inv * (d_normal - first - normal * second)


def lead_hot(lead, seg_row):
    seg = seg_row[...]
    found = jnp.zeros_like(seg)
    for slot in range(lead.shape[0]):
        found = jnp.where(seg == slot, lead[slot], found)
    slots = lax.broadcasted_iota(jnp.int32, (LEADS, seg.shape[1]), 0)
    return jnp.where(slots == found, 1.0, 0.0).astype(bf16)


def vec_row(vec, row):
    return vec[row : row + 1, :].astype(f32)


def q_prep_kernel(mover, pos, qkv, table, g1, b1, qb, vb, ob, g2, b2, db, ub, *outs):
    z = pos[0]
    rw = qkv.shape[0]
    d = qkv.shape[1] // 3
    width = d // DEPTH
    side = outs[0].shape[1] - 3 * width

    def wide(values):
        values = values.astype(f32)
        return jnp.concatenate([values, jnp.zeros((values.shape[0], side - values.shape[1]), f32)], 1)

    rows = [wide(table[...])] + [wide(v[...].reshape(1, -1)) for v in (g1, b1, qb, vb, ob, g2, b2, db)]
    rows += [ub[...].reshape(1, -1).astype(f32), jnp.zeros((rw - VEC_ROWS - 1, side), f32)]
    small = jnp.concatenate(rows, 0).astype(bf16)
    for u, out in enumerate(outs):
        for part in range(3):
            start = pl.multiple_of(part * d + (z ^ u) * width, width)
            out[:, part * width : (part + 1) * width] = qkv[:, pl.ds(start, width)]
        out[:, 3 * width :] = small


def q_stack_kernel(mover, pos, b0, b1, b2, b3, out):
    for u, block in enumerate((b0, b1, b2, b3)):
        mover.start(block, out.at[pos[0] ^ u])


def up_prep_kernel(mover, up, out):
    fr = up.shape[1] // (DEPTH * PLANE * 2)
    for k in range(PLANE):
        for c in range(2):
            for zz in range(DEPTH):
                src = ((zz * PLANE + k) * 2 + c) * fr
                dst = (c * DEPTH + zz) * fr
                out[k, :, dst : dst + fr] = up[:, src : src + fr]


def first_shard_kernel(mover, out_rows, down, out):
    out[0] = out_rows[...]
    out[1] = down[0 : out.shape[1], :]


def shard_kernel(mover, ups, down, out):
    out[0:PLANE] = ups[...]
    out[PLANE:] = down[out.shape[1] :, :].reshape(PLANE - 1, -1, down.shape[1])


def qkv_kernel(mover, pos, lead, seg_row, toks, *refs):
    z, yx, c = pos[0], pos[1], pos[2]
    qa, qc, (n1, w_out, vec, up_b, o0, o1, o2, o3, w, proj) = refs[:4], refs[4:8], refs[8:]
    rows, d = toks.shape[1:]
    width = d // DEPTH
    head = width // PLANE
    rw = w.shape[3]
    fr = w.shape[4] - 3 * width
    pending = [mover.start(qa[k], w.at[:, yx ^ k, c]) for k in range(PLANE)]
    pending += [mover.start(qc[k], w.at[:, yx ^ k, 1 - c]) for k in range(PLANE)]
    mover.wait(pending)
    mover.start(w.at[:, :, :, :, 0 : 3 * width], w_out)
    for zz in range(DEPTH):
        for k in range(PLANE):
            for core in range(2):
                i = (zz * PLANE + k) * 2 + core
                side = w[zz, k, core, :, 3 * width :].astype(f32)
                vec[:, i * rw : (i + 1) * rw] = side[0:VEC_ROWS, 0:rw]
        for core in range(2):
            side = w[zz, yx, core, :, 3 * width :].astype(f32)
            start = (core * DEPTH + zz) * fr
            up_b[:, start : start + fr] = side[VEC_ROWS : VEC_ROWS + 1, :]
    shift = mul(lead_hot(lead, seg_row), vec[0:LEADS, :].astype(bf16), 0, 0)
    gain, bias = vec_row(vec, ROW_G1), vec_row(vec, ROW_B1)
    for s in range(DEPTH):
        normal, _ = row_stats(toks[z ^ s].astype(f32) + shift)
        n1[s * rows : (s + 1) * rows, :] = (normal * gain + bias).astype(bf16)
    at = pl.ds(pl.multiple_of(z * width, width), width)
    biases = jnp.concatenate(
        [vec[ROW_QB : ROW_QB + 1, at], jnp.zeros((1, width), f32), vec[ROW_VB : ROW_VB + 1, at]], 1
    )
    first = lax.broadcasted_iota(jnp.int32, (8, 3 * width), 0) == 0
    biases = jnp.where(first, biases, 0.0).astype(bf16)
    ones = jnp.ones((8, DEPTH * rows), bf16)
    weight = w[:, :, :, :, 0 : 3 * width].reshape(d, 3 * width)
    found = mul(weight, n1[...], 0, 1) + mul(biases, ones, 0, 0)
    proj[...] = found.astype(bf16).reshape(proj.shape)
    for k, out in enumerate((o0, o1, o2, o3)):
        for part in range(3):
            mover.start(proj.at[part * PLANE + (yx ^ k)], out.at[part * head : (part + 1) * head])


def fill_heads(seg_row, count, blocks, qa, ka, vt):
    head = blocks[0].shape[0] // 3
    span = blocks[0].shape[1]
    seg = jnp.concatenate([seg_row[...]] * (span // seg_row.shape[1]), 1)
    slots = lax.broadcasted_iota(jnp.int32, (16, span), 0)
    hot, real = jnp.where(slots == seg, 1.0, 0.0), slots < count
    q_mark = jnp.where(real, (hot - 1.0) * BIG, 0.0).astype(bf16)
    k_mark = jnp.where(real, hot, 0.0).astype(bf16)
    rest = qa.shape[0] - head - 16
    for k, block in enumerate(blocks):
        cols = slice(k * span, (k + 1) * span)
        qa[0:head, cols] = block[0:head, :] * jnp.asarray(score_scale, bf16)
        qa[head : head + 16, cols] = q_mark
        qa[head + 16 :, cols] = jnp.zeros((rest, span), bf16)
        keys = jnp.concatenate([block[head : 2 * head, :], k_mark, jnp.zeros((rest, span), bf16)], 0)
        ka[cols, :] = keys.T
        vt[:, cols] = block[2 * head :, :]


def attend_kernel(count, mover, seg_row, b0, b1, b2, b3, o0, o1, o2, o3, lse, qa, ka, vt):
    fill_heads(seg_row, count, (b0, b1, b2, b3), qa, ka, vt)
    span = b0.shape[1]
    rows = seg_row.shape[1]
    outs = (o0, o1, o2, o3)

    def step(k, carry):
        for half in range(DEPTH // 2):
            at = pl.ds(pl.multiple_of(k * span + half * 2 * rows, 2 * rows), 2 * rows)
            scores = mul(ka[...], qa[:, at], 1, 0)
            top = jnp.max(scores, 0, keepdims=True)
            soft = jnp.exp(scores - top)
            total = jnp.sum(soft, 0, keepdims=True)
            found = mul(vt[...], soft.astype(bf16), 1, 0) / total
            lse[:, at] = jnp.broadcast_to(top + jnp.log(total), (8, 2 * rows))
            for i in range(2):
                outs[half * 2 + i][:, pl.ds(pl.multiple_of(k * rows, rows), rows)] = found[
                    :, i * rows : (i + 1) * rows
                ].astype(bf16)
        return carry

    lax.fori_loop(0, PLANE, step, 0)


def out_kernel(mover, pos, a0, a1, a2, a3, first, p0, p1, p2, p3, att, w_out):
    z = pos[0]
    head = a0.shape[0]
    rows, d = p0.shape
    pending = [mover.start(first.at[:, :, 0], w_out)]
    for u, block in enumerate((a0, a1, a2, a3)):
        att[pl.ds(pl.multiple_of((z ^ u) * head, head), head), :] = block[...]
    mover.wait(pending)
    found = mul(att[...], w_out[...].reshape(-1, d), 0, 0)
    for j, out in enumerate((p0, p1, p2, p3)):
        out[...] = found[j * rows : (j + 1) * rows, :].astype(out.dtype)


def norm_kernel(mover, lead, seg_row, vec, tok, p0, p1, p2, p3, middle, n2):
    shift = mul(lead_hot(lead, seg_row), vec[0:LEADS, :].astype(bf16), 0, 0) + vec_row(vec, ROW_OB)
    total = p0[...].astype(f32) + p1[...].astype(f32) + p2[...].astype(f32) + p3[...].astype(f32)
    total = tok[...].astype(f32) + shift + total
    middle[...] = total
    normal, _ = row_stats(total)
    n2[...] = (normal * vec_row(vec, ROW_G2) + vec_row(vec, ROW_B2)).astype(bf16)


def down_copies(mover, first, ff, w_down):
    copies = [mover.start(first.at[:, c, 1], w_down.at[c, :, 0]) for c in range(2)]
    return copies + [mover.start(ff.at[:, c, PLANE:], w_down.at[c, :, 1:]) for c in range(2)]


def ffn_kernel(mover, pos, up_b, n0, n1, n2, n3, d_outs, first, ff, act, d_hid, p0, p1, p2, p3, d_up_b, w_up, w_down, hid):
    yx = pos[1]
    rows, d = n0.shape
    for_up = [mover.start(ff.at[:, c, 0:PLANE], w_up.at[:, :, c]) for c in range(2)]
    for_down = down_copies(mover, first, ff, w_down)
    mover.wait(for_up)
    normed = jnp.concatenate([n0[...], n1[...], n2[...], n3[...]], 0)
    up = w_up[...].reshape(d, -1)
    hid[...] = mul(normed, up, 1, 0) + up_b[...].astype(f32)
    mover.wait(for_down)
    down = w_down[...].reshape(-1, d)
    sums = jnp.zeros(d_up_b.shape, f32)
    for j in range(PLANE):
        here = slice(j * rows, (j + 1) * rows)
        hidden = hid[here, :]
        phi = 0.5 * (1.0 + lax.erf(hidden * 0.7071067811865476))
        act[here, :] = (hidden * phi).astype(bf16)
        slope = phi + hidden * (jnp.exp(-0.5 * hidden * hidden) * 0.3989422804014327)
        d_act = mul(d_outs[yx ^ j], down, 1, 1)
        low = (d_act * slope).astype(bf16)
        d_hid[here, :] = low
        sums = sums + jnp.sum(low.astype(f32), 0, keepdims=True)
    d_up_b[...] = sums
    back = mul(d_hid[...], up, 1, 1)
    for j, out in enumerate((p0, p1, p2, p3)):
        out[...] = back[j * rows : (j + 1) * rows, :].astype(out.dtype)


def ffn_grad_kernel(mover, pos, act, d_hid, n0, n1, n2, n3, first, ff, d_outs, grads, outs, up_grad, down_grad, w_down):
    yx = pos[1]
    rows, d = outs.shape[1:]
    pending = down_copies(mover, first, ff, w_down)
    normed = jnp.concatenate([n0[...], n1[...], n2[...], n3[...]], 0)
    up_grad[...] = mul(normed, d_hid[...], 0, 0).astype(bf16).reshape(up_grad.shape)
    for c in range(2):
        mover.start(up_grad.at[:, :, c], grads.at[:, c, 0:PLANE])
    d_down = jnp.zeros((act.shape[1], d), f32)
    for j in range(PLANE):
        d_down = d_down + mul(act[j * rows : (j + 1) * rows, :], d_outs[yx ^ j], 0, 0)
    down_grad[...] = d_down.astype(bf16).reshape(down_grad.shape)
    for c in range(2):
        mover.start(down_grad.at[c], grads.at[:, c, PLANE : 2 * PLANE])
    mover.wait(pending)
    found = mul(act[...], w_down[...].reshape(-1, d), 1, 0)
    for j in range(PLANE):
        outs[yx ^ j] = found[j * rows : (j + 1) * rows, :].astype(bf16)


def ffn_last_kernel(mover, shard, ups, down, out_rows):
    ups[...] = shard[0:PLANE]
    down[...] = shard[PLANE : 2 * PLANE].astype(f32).reshape(down.shape)
    out_rows[...] = shard[2 * PLANE].astype(f32)


def branch_kernel(mover, vec, middle, d_out, p0, p1, p2, p3, d_mid, d_branch, d_vec):
    dy = p0[...].astype(f32) + p1[...].astype(f32) + p2[...].astype(f32) + p3[...].astype(f32)
    normal, inv = row_stats(middle[...])
    d_rows = d_out[...].astype(f32)
    total = d_rows + norm_back(dy * vec_row(vec, ROW_G2), normal, inv)
    d_mid[...] = total
    low = total.astype(bf16)
    d_branch[...] = low
    sums = [jnp.sum(v, 0, keepdims=True) for v in (dy * normal, dy, d_rows, low.astype(f32))]
    d_vec[...] = jnp.concatenate(sums + [jnp.zeros((4, dy.shape[1]), f32)], 0)


def out_back_kernel(mover, pos, att, w_out, b0, b1, b2, b3, others, o0, o1, o2, o3, grads, d_att, grad):
    z = pos[0]
    head = o0.shape[0]
    branch = jnp.concatenate([b0[...], b1[...], b2[...], b3[...]], 0)
    d = branch.shape[1]
    d_att[...] = mul(w_out[...].reshape(-1, d), branch, 1, 1).astype(bf16).reshape(d_att.shape)
    for u, out in enumerate((o0, o1, o2, o3)):
        out[...] = d_att[z ^ u]
    grad[...] = mul(att[...], branch, 1, 0).astype(bf16).reshape(grad.shape)
    mover.start(grad, grads.at[:, :, 2 * PLANE])


def attend_back_kernel(count, mover, seg_row, b0, b1, b2, b3, c0, c1, c2, c3, lse,
                       o0, o1, o2, o3, qa, ka, vt, vn, dot, dq, dk, dv):
    fill_heads(seg_row, count, (b0, b1, b2, b3), qa, ka, vt)
    span = b0.shape[1]
    rows = seg_row.shape[1]
    head, total = vt.shape
    for k in range(PLANE):
        cols = slice(k * span, (k + 1) * span)
        vn[cols, :] = vt[:, cols].T
        for s, block in enumerate((c0, c1, c2, c3)):
            dot[:, k * span + s * rows : k * span + (s + 1) * rows] = block[:, k * rows : (k + 1) * rows]
    dk[...] = jnp.zeros_like(dk)
    dv[...] = jnp.zeros_like(dv)
    logs = lse

    def step(i, carry):
        at = pl.ds(pl.multiple_of(i * 2 * rows, 2 * rows), 2 * rows)
        scores = mul(ka[...], qa[:, at], 1, 0)
        soft = jnp.exp(scores - logs[0:1, at])
        d_out = dot[:, at]
        d_soft = mul(vn[...], d_out, 1, 0)
        delta = jnp.sum(soft * d_soft, 0, keepdims=True)
        d_scores = (soft * (d_soft - delta)).astype(bf16)
        dv[...] += mul(d_out, soft.astype(bf16), 1, 1)
        dk[...] += mul(qa[0:head, at], d_scores, 1, 1)
        dq[:, at] = (mul(ka[:, 0:head], d_scores, 0, 0) * score_scale).astype(bf16)
        return carry

    lax.fori_loop(0, total // (2 * rows), step, 0)
    for k, out in enumerate((o0, o1, o2, o3)):
        cols = slice(k * span, (k + 1) * span)
        out[0:head, :] = dq[:, cols]
        out[head : 2 * head, :] = dk[:, cols].astype(bf16)
        out[2 * head :, :] = dv[:, cols].astype(bf16)


def join_heads(yx, blocks, joined):
    head = blocks[0].shape[0] // 3
    for k, block in enumerate(blocks):
        for part in range(3):
            joined[part * PLANE + (yx ^ k)] = block[part * head : (part + 1) * head, :]
    return joined[...].reshape(3 * PLANE * head, -1)


def qkv_back_kernel(mover, pos, w, g0, g1, g2, g3, out, back, joined):
    grads = join_heads(pos[1], (g0, g1, g2, g3), joined)
    rows, d = out.shape[1:]
    found = mul(grads, w[...].reshape(d, -1), 0, 1)
    back[...] = found
    for s in range(DEPTH):
        out[pos[0] ^ s] = found[s * rows : (s + 1) * rows, :].astype(bf16)


def qkv_grad_kernel(mover, pos, lead, seg_row, vec, toks, n1, g0, g1, g2, g3, back, d_mid, d_mid_vec, d_up_b,
                    mine, o0, o1, joined, d_vec, both):
    z, yx, core = pos[0], pos[1], pos[2]
    rows, d = toks.shape[1:]
    width = d // DEPTH
    grads = join_heads(yx, (g0, g1, g2, g3), joined)
    rw = mine.shape[2]
    cols = 3 * width
    grad = mul(n1[...], grads, 0, 1).astype(bf16)
    hot = lead_hot(lead, seg_row)
    shift = mul(hot, vec[0:LEADS, :].astype(bf16), 0, 0)
    gain = vec_row(vec, ROW_G1)
    d_gain = jnp.zeros((1, d), f32)
    d_bias = jnp.zeros((1, d), f32)
    d_emb = d_mid[...]
    for s in range(DEPTH):
        piece = back[s * rows : (s + 1) * rows, :]
        normal, inv = row_stats(toks[z ^ s].astype(f32) + shift)
        d_gain = d_gain + jnp.sum(piece * normal, 0, keepdims=True)
        d_bias = d_bias + jnp.sum(piece, 0, keepdims=True)
        d_emb = d_emb + norm_back(piece * gain, normal, inv)
    high = d_emb.astype(bf16)
    low = (d_emb - high.astype(f32)).astype(bf16)
    d_vec[...] = jnp.zeros_like(d_vec)
    d_vec[0:LEADS, :] = mul(hot, high, 1, 0) + mul(hot, low, 1, 0)
    sums = mul(jnp.ones((8, DEPTH * rows), bf16), grads, 1, 1)
    d_vec[ROW_G1 : ROW_G1 + 1, :] = d_gain
    d_vec[ROW_B1 : ROW_B1 + 1, :] = d_bias
    at = pl.ds(pl.multiple_of(z * width, width), width)
    d_vec[ROW_QB : ROW_QB + 1, at] = sums[0:1, 0:width]
    d_vec[ROW_VB : ROW_VB + 1, at] = sums[0:1, 2 * width :]
    for i, row in enumerate((ROW_G2, ROW_B2, ROW_DB, ROW_OB)):
        d_vec[row : row + 1, :] = d_mid_vec[i : i + 1, :]
    small = d_vec[...].astype(bf16)
    fr = mine.shape[3] - cols
    for zz in range(DEPTH):
        for k in range(PLANE):
            for c in range(2):
                i = (zz * PLANE + k) * 2 + c
                side = jnp.concatenate([small[:, i * rw : (i + 1) * rw], jnp.zeros((rw, fr - rw), bf16)], 1)
                start = (c * DEPTH + zz) * fr
                last = jnp.where(yx == k, d_up_b[:, start : start + fr], 0.0).astype(bf16)
                mark = lax.broadcasted_iota(jnp.int32, (rw, fr), 0) == VEC_ROWS
                whole = jnp.concatenate(
                    [grad[i * rw : (i + 1) * rw, :], jnp.where(mark, last.astype(f32), side.astype(f32)).astype(bf16)], 1
                )
                both[zz, k, c] = whole
    mover.start(both.at[0:2, :, 1 - core], o0)
    mover.start(both.at[2:4, :, 1 - core], o1)
    mover.start(both.at[:, :, core], mine)


def first_back_kernel(mover, lead, seg_row, vec, tok, d_mid, blocks, out):
    shift = mul(lead_hot(lead, seg_row), vec[0:LEADS, :].astype(bf16), 0, 0)
    normal, inv = row_stats(tok[...].astype(f32) + shift)
    dy = blocks[0].astype(f32)
    for s in range(1, DEPTH):
        dy = dy + blocks[s].astype(f32)
    out[...] = d_mid[...] + norm_back(dy * vec_row(vec, ROW_G1), normal, inv)


def layer_out_kernel(mover, vec, middle, blocks, out):
    total = middle[...] + vec_row(vec, ROW_DB)
    for k in range(PLANE):
        total = total + blocks[k].astype(f32)
    out[...] = total.astype(bf16)


def pair_kernel(mover, pos, mine, o0, o1, p0, p1, p2, p3, total):
    yx = pos[1]
    total[0:2] = (mine[0:2].astype(f32) + o0[...].astype(f32)).astype(bf16)
    total[2:4] = (mine[2:4].astype(f32) + o1[...].astype(f32)).astype(bf16)
    for k, out in enumerate((p0, p1, p2, p3)):
        mover.start(total.at[:, yx ^ k], out)


def quad_kernel(mover, pos, b0, b1, b2, b3, o0, o1, o2, o3, total):
    found = b0[...].astype(f32) + b1[...].astype(f32) + b2[...].astype(f32) + b3[...].astype(f32)
    total[...] = found.astype(bf16)
    for u, out in enumerate((o0, o1, o2, o3)):
        out[...] = total[pos[0] ^ u]


def qkv_join_kernel(mover, pos, b0, b1, b2, b3, out, table, *rest):
    z = pos[0]
    rw = out.shape[0]
    width = out.shape[1] // (3 * DEPTH)
    side = jnp.zeros((rw, b0.shape[1] - 3 * width), f32)
    for s, block in enumerate((b0, b1, b2, b3)):
        for part in range(3):
            start = pl.multiple_of((part * DEPTH + (z ^ s)) * width, width)
            out[:, pl.ds(start, width)] = block[:, part * width : (part + 1) * width].astype(f32)
        side = side + block[:, 3 * width :].astype(f32)
    table[...] = side[0:LEADS, 0:rw]
    for i, row in enumerate(rest[:-1]):
        row[...] = side[LEADS + i : LEADS + i + 1, 0:rw].reshape(rw)
    rest[-1][...] = side[VEC_ROWS : VEC_ROWS + 1, :].reshape(-1)


def up_join_kernel(mover, blocks, out):
    fr = blocks.shape[2] // (2 * DEPTH)
    for k in range(PLANE):
        for c in range(2):
            for zz in range(DEPTH):
                src = (c * DEPTH + zz) * fr
                dst = ((zz * PLANE + k) * 2 + c) * fr
                out[:, dst : dst + fr] = blocks[k, :, src : src + fr].astype(f32)


COSTS = {
    "q_prep_kernel": (1, 4), "q_stack_kernel": (1, 4), "up_prep_kernel": (1, 4), "shard_kernel": (1, 4), "first_shard_kernel": (1, 4), "qkv_kernel": (5, 20),
    "attend_kernel": (11, 16), "out_kernel": (2, 12), "norm_kernel": (2, 8), "ffn_kernel": (8, 32), "ffn_grad_kernel": (8, 32),
    "branch_kernel": (2, 12), "out_back_kernel": (3, 12), "attend_back_kernel": (19, 24),
    "qkv_back_kernel": (3, 16), "qkv_grad_kernel": (6, 24), "first_back_kernel": (2, 8), "layer_out_kernel": (1, 8),
    "pair_kernel": (2, 8), "quad_kernel": (1, 8), "qkv_join_kernel": (1, 4), "up_join_kernel": (2, 8), "ffn_last_kernel": (1, 8),
}
PLANE_AXES = ("y", "x")


def trade(blocks, axes):
    return lax.all_to_all(blocks, axes, split_axis=0, concat_axis=0, tiled=True)


ALL = ("z", "y", "x", "g")


def across(blocks):
    swap = [(0, 1), (1, 0)]
    return (
        blocks[0],
        lax.ppermute(blocks[1], "x", swap),
        lax.ppermute(blocks[2], "y", swap),
        lax.ppermute(blocks[3], ("y", "x"), [(i, i ^ 3) for i in range(PLANE)]),
    )


def to_depth(block, step):
    return lax.ppermute(block, "z", [(i, i ^ step) for i in range(DEPTH)])


def along(blocks):
    return (blocks[0],) + tuple(to_depth(blocks[u], u) for u in range(1, DEPTH))


def core_swap(block):
    return lax.ppermute(block, "g", [(0, 1), (1, 0)])


def far(blocks):
    return [Far(block) for block in blocks]


def raw(blocks):
    return [Raw(block) for block in blocks]


def fast_local(
    tokens, segment_ids, lead_index, lead_table, ln1_gain, ln1_bias, qkv_weight, q_bias, v_bias,
    out_weight, out_bias, ln2_gain, ln2_bias, up_weight, up_bias, down_weight, down_bias, d_out,
):
    z = lax.axis_index("z")
    yx = lax.axis_index("y") * 2 + lax.axis_index("x")
    c = lax.axis_index("g")
    pos = jnp.stack([z, yx, c]).astype(jnp.int32)
    tok, d_rows = tokens[0], d_out[0]
    rows, d = tok.shape
    head = d // HEADS
    span = DEPTH * rows
    group = PLANE * span
    rw = qkv_weight.shape[0]
    fr = down_weight.shape[0]
    ff = 2 * DEPTH * fr
    lead = lead_index[0]
    count = lead.shape[0]
    width = 3 * d // DEPTH
    seg_row = segment_ids
    up_shape, down_shape = (DEPTH, PLANE, 2, rw, ff), (2, DEPTH, PLANE, rw, d)

    order = []
    call = functools.partial(run, order)
    side = width + -(-max(rw, fr) // 128) * 128

    q_rows = along(
        call(
            q_prep_kernel,
            [((rw, side), bf16)] * 4,
            [pos]
            + far((qkv_weight, lead_table, ln1_gain, ln1_bias, q_bias, v_bias, out_bias, ln2_gain, ln2_bias, down_bias, up_bias)),
        )
    )
    toks = lax.all_gather(tok, "z", axis=0)
    d_outs = trade(jnp.broadcast_to(d_rows[None], (PLANE, rows, d)), PLANE_AXES)
    (q_stack,) = call(q_stack_kernel, [((DEPTH, rw, side), bf16)], [pos, *q_rows], after=[d_outs])
    q_plane = across((q_stack,) * PLANE)
    q_other = [core_swap(block) for block in q_plane]
    (first_shard,) = call(first_shard_kernel, [((2, rw, d), bf16, "far")], [out_weight, down_weight])
    first = lax.all_gather(first_shard, ("z", "g"), axis=0).reshape(DEPTH, 2, 2, rw, d)
    (up_cols,) = call(up_prep_kernel, [((PLANE, rw, ff), bf16)], [up_weight])
    up_cols = trade(up_cols, PLANE_AXES)
    n1, w_qkv, vec, up_b, *blocks = call(
        qkv_kernel,
        [((span, d), bf16, "far"), ((DEPTH, PLANE, 2, rw, width), bf16, "raw"), ((VEC_ROWS, d), f32), ((1, ff), f32)]
        + [((3 * head, span), bf16)] * 4,
        [pos, lead, seg_row, Far(toks), *q_plane, *q_other],
        [((DEPTH, PLANE, 2, rw, side), bf16), ((3 * PLANE, head, span), bf16)],
    )
    (ff_shard,) = call(shard_kernel, [((2 * PLANE - 1, rw, d), bf16, "far")], [up_cols, down_weight])
    ff_all = lax.all_gather(ff_shard, ("z", "g"), axis=0).reshape(DEPTH, 2, 2 * PLANE - 1, rw, d)
    blocks = across(blocks)

    *att_parts, lse = call(
        functools.partial(attend_kernel, count),
        [((head, PLANE * rows), bf16)] * 4 + [((8, group), f32)],
        [seg_row, *blocks],
        [((128, group), bf16), ((group, 128), bf16), ((head, group), bf16)],
    )
    att_parts = along(att_parts)
    *parts, att, w_out = call(
        out_kernel,
        [((rows, d), f32)] + [((rows, d), bf16)] * 3 + [((DEPTH * head, span), bf16), ((DEPTH, 2, rw, d), bf16)],
        [pos, *att_parts, Raw(first)],
    )
    parts = across(parts)
    middle, n2 = call(norm_kernel, [((rows, d), f32, "far"), ((rows, d), bf16)], [lead, seg_row, vec, Far(tok), *parts])
    n2_plane = across((n2,) * PLANE)

    act, d_hid, p0, p1, p2, p3, d_up_b = call(
        ffn_kernel,
        [((span, ff), bf16), ((span, ff), bf16), ((rows, d), f32)] + [((rows, d), bf16)] * 3 + [((1, ff), f32)],
        [pos, up_b, *n2_plane, Far(d_outs), Raw(first), Raw(ff_all)],
        [(up_shape, bf16), (down_shape, bf16), ((span, ff), f32)],
    )
    parts = across((p0, p1, p2, p3))
    ff_grad, outs = call(
        ffn_grad_kernel,
        [((DEPTH, 2, 2 * PLANE + 1, rw, d), bf16, "raw"), ((PLANE, rows, d), bf16, "far")],
        [pos, act, d_hid, *n2_plane, Raw(first), Raw(ff_all), Far(d_outs)],
        [(up_shape, bf16), (down_shape, bf16), (down_shape, bf16)],
    )
    d_mid, d_branch, d_mid_vec = call(
        branch_kernel,
        [((rows, d), f32, "far"), ((rows, d), bf16), ((8, d), f32)],
        [vec, Far(middle), Far(d_rows), *parts],
    )
    branch_plane = across((d_branch,) * PLANE)
    *d_att, ff_grad = call(
        out_back_kernel,
        [((head, span), bf16)] * 4 + [(ff_grad.shape, bf16, "raw")],
        [pos, att, w_out, *branch_plane, Raw(ff_grad)],
        [((DEPTH, head, span), bf16), ((DEPTH, 2, rw, d), bf16)],
        alias=(7, 4),
    )
    d_att = along(d_att)
    ff_grad = lax.psum_scatter(
        ff_grad.reshape(2 * DEPTH, 2 * PLANE + 1, rw, d), ("z", "g"), scatter_dimension=0, tiled=True
    )[0]
    outs = trade(outs, PLANE_AXES)

    d_blocks = call(
        functools.partial(attend_back_kernel, count),
        [((3 * head, span), bf16)] * 4,
        [seg_row, *blocks, *d_att, lse],
        [((128, group), bf16), ((group, 128), bf16), ((head, group), bf16), ((group, head), bf16),
         ((head, group), bf16), ((head, group), bf16), ((head, group), f32), ((head, group), f32)],
    )
    d_blocks = across(d_blocks)
    (layer_out,) = call(layer_out_kernel, [((rows, d), bf16)], [vec, Far(middle), outs])
    returned, back = call(
        qkv_back_kernel,
        [((DEPTH, rows, d), bf16), ((span, d), f32, "far")],
        [pos, Far(w_qkv), *d_blocks],
        [((3 * PLANE, head, span), bf16)],
    )
    returned = trade(returned, ("z",))
    mine, o0, o1 = call(
        qkv_grad_kernel,
        [((DEPTH, PLANE, rw, side), bf16, "raw")] + [((DEPTH // 2, PLANE, rw, side), bf16)] * 2,
        [pos, lead, seg_row, vec, Far(toks), Far(n1), *d_blocks, Far(back), Far(d_mid), d_mid_vec, d_up_b],
        [((3 * PLANE, head, span), bf16), ((rw, d), f32), ((DEPTH, PLANE, 2, rw, side), bf16)],
    )
    quads = call(
        pair_kernel,
        [((DEPTH, rw, side), bf16, "raw")] + [((DEPTH, rw, side), bf16)] * 3,
        [pos, Far(mine), core_swap(o0), core_swap(o1)],
        [((DEPTH, PLANE, rw, side), bf16)],
    )
    quads = across(quads)
    ups, d_down, d_out_weight = call(
        ffn_last_kernel, [((PLANE, rw, ff), bf16), ((fr, d), f32), ((rw, d), f32)], [ff_grad]
    )
    ups = trade(ups, PLANE_AXES)
    cols = along(call(quad_kernel, [((rw, side), bf16)] * 4, [pos, Far(quads[0]), *quads[1:]], [((DEPTH, rw, side), bf16)]))
    (d_tokens,) = call(
        first_back_kernel, [((rows, d), f32)], [lead, seg_row, vec, Far(tok), Far(d_mid), returned]
    )
    d_qkv, table, d_g1, d_b1, d_qb, d_vb, d_ob, d_g2, d_b2, d_db, d_ub = call(
        qkv_join_kernel,
        [((rw, 3 * d), f32), ((LEADS, rw), f32)] + [((rw,), f32)] * 8 + [((fr,), f32)],
        [pos, *cols],
    )
    (d_up,) = call(up_join_kernel, [((rw, PLANE * ff), f32)], [ups])
    return (
        layer_out[None], d_tokens[None], table, d_g1, d_b1, d_qkv, d_qb, d_vb, d_out_weight, d_ob,
        d_g2, d_b2, d_up, d_ub, d_down, d_db,
    )


def specs(band, grp):
    every = band + grp
    rows = P(grp, band, None)
    in_specs = (
        rows, P(grp, band), P(grp, None), P(None, every), P(every), P(every), P(every, None), P(every), P(every),
        P(every, None), P(every), P(every), P(every), P(every, None), P(every), P(every, None), P(every), rows,
    )
    out_specs = (
        rows, rows, P(None, every), P(every), P(every), P(every, None), P(every), P(every), P(every, None), P(every),
        P(every), P(every), P(every, None), P(every), P(every, None), P(every),
    )
    return in_specs, out_specs


def solution(mesh):
    band, grp = mesh.shape["band"], mesh.shape["grp"]
    if band == HEADS and grp == 2:
        mesh = Mesh(mesh.devices.reshape(DEPTH, 2, 2, grp), ("z", "y", "x", "g"))
        in_specs, out_specs = specs(("z", "y", "x"), ("g",))
        return jax.shard_map(fast_local, mesh=mesh, in_specs=in_specs, out_specs=out_specs, check_vma=False)
    in_specs, out_specs = specs(("band",), ("grp",))
    return jax.shard_map(local, mesh=mesh, in_specs=in_specs, out_specs=out_specs, check_vma=False)
```

```python
import functools
import math

import jax
import jax.numpy as jnp
from jax import lax
from jax.experimental import pallas as pl
from jax.experimental.pallas import tpu as pltpu
from jax.sharding import Mesh
from jax.sharding import PartitionSpec as P

bf16, f32 = jnp.bfloat16, jnp.float32

HEADS = 16


epsilon = 1e-05
score_scale = 0.125
masked_score = -1e30


def norm_rows(values, norm_gain, norm_bias):
    row_mean = jnp.mean(values, -1, keepdims=True)
    centred = values - row_mean
    row_var = jnp.mean(centred * centred, -1, keepdims=True)
    return centred * lax.rsqrt(row_var + epsilon) * norm_gain + norm_bias


def gelu_exact(values):
    return jax.nn.gelu(values, approximate=False)


def split_blocks(values, block_rows):
    return values.reshape((values.shape[0] // block_rows, block_rows) + values.shape[1:])


def block_scores(query_heads, key_heads, allowed):
    raw_scores = (
        jnp.einsum("qhd,khd->hqk", query_heads, key_heads, preferred_element_type=jnp.float32)
        * score_scale
    )
    return jnp.where(allowed[None], raw_scores, masked_score)


def softmax_rows(query_heads, key_heads, allowed, log_total):
    scores = block_scores(query_heads, key_heads, allowed)
    return jnp.where(allowed[None], jnp.exp(scores - log_total[:, :, None]), 0.0)


def score_grads(query_heads, key_heads, value_heads, d_heads, allowed, log_total, row_delta):
    soft_rows = softmax_rows(query_heads, key_heads, allowed, log_total)
    d_soft = jnp.einsum("qhd,khd->hqk", d_heads, value_heads, preferred_element_type=jnp.float32)
    d_scores = (soft_rows * (d_soft - row_delta[:, :, None])).astype(jnp.bfloat16)
    return (soft_rows.astype(jnp.bfloat16), d_scores)


def local(
    tokens,
    segment_ids,
    lead_index,
    lead_table,
    ln1_gain,
    ln1_bias,
    qkv_weight,
    q_bias,
    v_bias,
    out_weight,
    out_bias,
    ln2_gain,
    ln2_bias,
    up_weight,
    up_bias,
    down_weight,
    down_bias,
    d_out,
):
    (
        table_full,
        first_gain,
        first_shift,
        project_full,
        query_shift,
        value_shift,
        out_full,
        out_shift,
        second_gain,
        second_shift,
        up_full,
        up_shift,
        down_full,
        down_shift,
    ) = (
        lax.all_gather(lead_table, ("band", "grp"), axis=1, tiled=True),
        lax.all_gather(ln1_gain, ("band", "grp"), axis=0, tiled=True),
        lax.all_gather(ln1_bias, ("band", "grp"), axis=0, tiled=True),
        lax.all_gather(qkv_weight, ("band", "grp"), axis=0, tiled=True),
        lax.all_gather(q_bias, ("band", "grp"), axis=0, tiled=True),
        lax.all_gather(v_bias, ("band", "grp"), axis=0, tiled=True),
        lax.all_gather(out_weight, ("band", "grp"), axis=0, tiled=True),
        lax.all_gather(out_bias, ("band", "grp"), axis=0, tiled=True),
        lax.all_gather(ln2_gain, ("band", "grp"), axis=0, tiled=True),
        lax.all_gather(ln2_bias, ("band", "grp"), axis=0, tiled=True),
        lax.all_gather(up_weight, ("band", "grp"), axis=0, tiled=True),
        lax.all_gather(up_bias, ("band", "grp"), axis=0, tiled=True),
        lax.all_gather(down_weight, ("band", "grp"), axis=0, tiled=True),
        lax.all_gather(down_bias, ("band", "grp"), axis=0, tiled=True),
    )
    tok_rows = tokens.shape[1]
    features = tokens.shape[2]
    head_dim = features // HEADS
    band_count = lax.axis_size("band")
    group_rows = tok_rows * band_count
    block_rows = math.gcd(group_rows, 1024)
    own_segments = segment_ids[0]
    group_segments = jnp.tile(own_segments, band_count)
    sample_count = lead_index.shape[1]
    lead_count = lead_table.shape[0]
    sample_hot = (
        own_segments[:, None] == jnp.arange(sample_count, dtype=jnp.int32)[None, :]
    ).astype(jnp.float32)
    lead_hot = (lead_index[0][:, None] == jnp.arange(lead_count, dtype=jnp.int32)[None, :]).astype(
        jnp.float32
    )
    lead_pick = jnp.dot(sample_hot, lead_hot, precision=lax.Precision.HIGHEST)
    embedded = tokens[0].astype(jnp.float32) + jnp.dot(
        lead_pick.astype(jnp.bfloat16), table_full, preferred_element_type=jnp.float32
    )
    normed_first = norm_rows(
        embedded, first_gain.astype(jnp.float32), first_shift.astype(jnp.float32)
    ).astype(jnp.bfloat16)
    projected = jnp.dot(normed_first, project_full, preferred_element_type=jnp.float32)
    query_rows = (projected[:, :features] + query_shift.astype(jnp.float32)).astype(jnp.bfloat16)
    key_rows = projected[:, features : 2 * features].astype(jnp.bfloat16)
    value_rows = (projected[:, 2 * features :] + value_shift.astype(jnp.float32)).astype(
        jnp.bfloat16
    )
    key_all, value_all = (
        lax.all_gather(key_rows, "band", axis=0, tiled=True),
        lax.all_gather(value_rows, "band", axis=0, tiled=True),
    )
    query_heads = query_rows.reshape(tok_rows, HEADS, head_dim)
    key_blocks = split_blocks(key_all.reshape(group_rows, HEADS, head_dim), block_rows)
    value_blocks = split_blocks(value_all.reshape(group_rows, HEADS, head_dim), block_rows)
    segment_blocks = split_blocks(group_segments, block_rows)

    def stats_step(running, block_data):
        running_max, running_sum = running
        key_block, key_segments = block_data
        allowed = own_segments[:, None] == key_segments[None, :]
        scores = block_scores(query_heads, key_block, allowed)
        new_max = jnp.maximum(running_max, jnp.max(scores, -1))
        block_sum = jnp.sum(
            jnp.where(allowed[None], jnp.exp(scores - new_max[:, :, None]), 0.0), -1
        )
        return ((new_max, running_sum * jnp.exp(running_max - new_max) + block_sum), None)

    start_max = jnp.full((HEADS, tok_rows), masked_score, jnp.float32)
    start_sum = jnp.zeros((HEADS, tok_rows), jnp.float32)
    (final_max, final_sum), unused_out = lax.scan(
        stats_step, (start_max, start_sum), (key_blocks, segment_blocks)
    )
    log_total = final_max + jnp.log(final_sum)

    def output_step(running, block_data):
        high_part, low_part = running
        key_block, value_block, key_segments = block_data
        allowed = own_segments[:, None] == key_segments[None, :]
        soft_rows = softmax_rows(query_heads, key_block, allowed, log_total)
        soft_low = soft_rows.astype(jnp.bfloat16)
        soft_rest = (soft_rows - soft_low.astype(jnp.float32)).astype(jnp.bfloat16)
        high_part = high_part + jnp.einsum(
            "hqk,khd->qhd", soft_low, value_block, preferred_element_type=jnp.float32
        )
        low_part = low_part + jnp.einsum(
            "hqk,khd->qhd", soft_rest, value_block, preferred_element_type=jnp.float32
        )
        return ((high_part, low_part), None)

    empty_heads = jnp.zeros((tok_rows, HEADS, head_dim), jnp.float32)
    (attn_high, attn_low), unused_out = lax.scan(
        output_step, (empty_heads, empty_heads), (key_blocks, value_blocks, segment_blocks)
    )
    attended = attn_high.reshape(tok_rows, features).astype(jnp.bfloat16)
    middle = (
        embedded
        + jnp.dot(attended, out_full, preferred_element_type=jnp.float32)
        + out_shift.astype(jnp.float32)
    )
    normed_second = norm_rows(
        middle, second_gain.astype(jnp.float32), second_shift.astype(jnp.float32)
    ).astype(jnp.bfloat16)
    hidden = jnp.dot(normed_second, up_full, preferred_element_type=jnp.float32) + up_shift.astype(
        jnp.float32
    )
    activated = gelu_exact(hidden).astype(jnp.bfloat16)
    result = (
        middle
        + jnp.dot(activated, down_full, preferred_element_type=jnp.float32)
        + down_shift.astype(jnp.float32)
    )
    layer_out = result.astype(jnp.bfloat16)[None]
    first_gain_back, project_back, out_back, second_gain_back, up_back, down_back = (
        lax.all_gather(ln1_gain, ("band", "grp"), axis=0, tiled=True),
        lax.all_gather(qkv_weight, ("band", "grp"), axis=0, tiled=True),
        lax.all_gather(out_weight, ("band", "grp"), axis=0, tiled=True),
        lax.all_gather(ln2_gain, ("band", "grp"), axis=0, tiled=True),
        lax.all_gather(up_weight, ("band", "grp"), axis=0, tiled=True),
        lax.all_gather(down_weight, ("band", "grp"), axis=0, tiled=True),
    )
    d_rows = d_out[0]
    d_down_shift = jnp.sum(d_rows.astype(jnp.float32), 0)
    d_down = jnp.einsum("tf,td->fd", activated, d_rows, preferred_element_type=jnp.float32)
    d_act = jnp.einsum("td,fd->tf", d_rows, down_back, preferred_element_type=jnp.float32)
    unused_gelu, gelu_back = jax.vjp(gelu_exact, hidden)
    d_hidden = gelu_back(d_act)[0].astype(jnp.bfloat16)
    d_up_shift = jnp.sum(d_hidden.astype(jnp.float32), 0)
    d_up = jnp.einsum("td,tf->df", normed_second, d_hidden, preferred_element_type=jnp.float32)
    d_normed_second = jnp.einsum("tf,df->td", d_hidden, up_back, preferred_element_type=jnp.float32)
    unused_second, second_back = jax.vjp(
        norm_rows, middle, second_gain_back.astype(jnp.float32), second_shift.astype(jnp.float32)
    )
    d_middle_part, d_gain_second, d_shift_second = second_back(d_normed_second)
    d_middle = d_rows.astype(jnp.float32) + d_middle_part
    d_branch = d_middle.astype(jnp.bfloat16)
    d_out_shift = jnp.sum(d_branch.astype(jnp.float32), 0)
    d_out_full = jnp.einsum("ti,to->io", attended, d_branch, preferred_element_type=jnp.float32)
    d_attended = jnp.einsum(
        "to,io->ti", d_branch, out_back, preferred_element_type=jnp.float32
    ).astype(jnp.bfloat16)
    d_heads = d_attended.reshape(tok_rows, HEADS, head_dim)
    row_delta = jnp.sum(d_heads.astype(jnp.float32) * (attn_high + attn_low), -1).T

    def query_grad(d_query_acc, key_block, value_block, key_segments):
        allowed = own_segments[:, None] == key_segments[None, :]
        soft_low, d_scores = score_grads(
            query_heads, key_block, value_block, d_heads, allowed, log_total, row_delta
        )
        d_query_acc = d_query_acc + jnp.einsum(
            "hqk,khd->qhd", d_scores, key_block, preferred_element_type=jnp.float32
        )
        return (d_query_acc, soft_low, d_scores)

    def owner_step(d_query_acc, block_data):
        key_block, value_block, key_segments = block_data
        d_query_acc, soft_low, d_scores = query_grad(
            d_query_acc, key_block, value_block, key_segments
        )
        d_key_block = (
            jnp.einsum("hqk,qhd->khd", d_scores, query_heads, preferred_element_type=jnp.float32)
            * score_scale
        )
        d_value_block = jnp.einsum(
            "hqk,qhd->khd", soft_low, d_heads, preferred_element_type=jnp.float32
        )
        return (d_query_acc, (d_key_block, d_value_block))

    d_query_sum, (d_key_parts, d_value_parts) = lax.scan(
        owner_step, empty_heads, (key_blocks, value_blocks, segment_blocks)
    )
    d_key_sum, d_value_sum = (
        lax.psum_scatter(
            d_key_parts.reshape(group_rows, features).astype(jnp.bfloat16),
            "band",
            scatter_dimension=0,
            tiled=True,
        ).astype(jnp.float32),
        lax.psum_scatter(
            d_value_parts.reshape(group_rows, features).astype(jnp.bfloat16),
            "band",
            scatter_dimension=0,
            tiled=True,
        ).astype(jnp.float32),
    )
    d_query = (d_query_sum.reshape(tok_rows, features) * score_scale).astype(jnp.bfloat16)
    d_key = d_key_sum.astype(jnp.bfloat16)
    d_value = d_value_sum.astype(jnp.bfloat16)
    d_query_shift = jnp.sum(d_query.astype(jnp.float32), 0)
    d_value_shift = jnp.sum(d_value.astype(jnp.float32), 0)
    d_project_rows = jnp.concatenate([d_query, d_key, d_value], 1)
    d_project = jnp.einsum(
        "ti,to->io", normed_first, d_project_rows, preferred_element_type=jnp.float32
    )
    d_normed_first = jnp.einsum(
        "to,io->ti", d_project_rows, project_back, preferred_element_type=jnp.float32
    )
    unused_first, first_back = jax.vjp(
        norm_rows, embedded, first_gain_back.astype(jnp.float32), first_shift.astype(jnp.float32)
    )
    d_embed_part, d_gain_first, d_shift_first = first_back(d_normed_first)
    d_embedded = d_middle + d_embed_part
    d_table = jnp.einsum("tl,td->ld", lead_pick, d_embedded, precision=lax.Precision.HIGHEST)
    shards = (
        lax.psum_scatter(d_table, ("band", "grp"), scatter_dimension=1, tiled=True),
        lax.psum_scatter(d_gain_first, ("band", "grp"), scatter_dimension=0, tiled=True),
        lax.psum_scatter(d_shift_first, ("band", "grp"), scatter_dimension=0, tiled=True),
        lax.psum_scatter(d_project, ("band", "grp"), scatter_dimension=0, tiled=True),
        lax.psum_scatter(d_query_shift, ("band", "grp"), scatter_dimension=0, tiled=True),
        lax.psum_scatter(d_value_shift, ("band", "grp"), scatter_dimension=0, tiled=True),
        lax.psum_scatter(d_out_full, ("band", "grp"), scatter_dimension=0, tiled=True),
        lax.psum_scatter(d_out_shift, ("band", "grp"), scatter_dimension=0, tiled=True),
        lax.psum_scatter(d_gain_second, ("band", "grp"), scatter_dimension=0, tiled=True),
        lax.psum_scatter(d_shift_second, ("band", "grp"), scatter_dimension=0, tiled=True),
        lax.psum_scatter(d_up, ("band", "grp"), scatter_dimension=0, tiled=True),
        lax.psum_scatter(d_up_shift, ("band", "grp"), scatter_dimension=0, tiled=True),
        lax.psum_scatter(d_down, ("band", "grp"), scatter_dimension=0, tiled=True),
        lax.psum_scatter(d_down_shift, ("band", "grp"), scatter_dimension=0, tiled=True),
    )
    return (layer_out, d_embedded[None]) + tuple(shards)


DEPTH = 4
PLANE = 4
BIG = 1e30
HBM = pltpu.MemorySpace.HBM
VMEM = pltpu.MemorySpace.VMEM
SMEM = pltpu.MemorySpace.SMEM
LEADS = 16
ROW_G1, ROW_B1, ROW_QB, ROW_VB, ROW_OB, ROW_G2, ROW_B2, ROW_DB = range(16, 24)
VEC_ROWS = 24


def mul(left, right, over_left, over_right):
    return lax.dot_general(
        left, right, (((over_left,), (over_right,)), ((), ())), preferred_element_type=jnp.float32
    )


class Mover:
    def __init__(self, sems):
        self.sems, self.used, self.open = sems, 0, []

    def start(self, source, target):
        copy = pltpu.make_async_copy(source, target, self.sems.at[self.used])
        self.used += 1
        copy.start()
        self.open.append(copy)
        return copy

    def wait(self, copies=None):
        for copy in list(self.open if copies is None else copies):
            copy.wait()
            self.open = [other for other in self.open if other is not copy]


class Far:
    def __init__(self, value):
        self.value = value


class Raw(Far):
    pass


class Given:
    def __init__(self, ref, held, mover):
        self.ref, self.mover, self.copy = held, mover, mover.start(ref, held)
        self.shape, self.dtype = ref.shape, ref.dtype

    def ready(self):
        if self.copy is not None:
            self.mover.wait([self.copy])
            self.copy = None
        return self.ref

    def __getitem__(self, at):
        return self.ready()[at]


def run(order, kernel, outs, ins, scratch=(), after=(), alias=None):
    after = list(after) + order
    kinds = [type(a) if isinstance(a, Far) else None for a in ins]
    ins = [a.value if kind else a for a, kind in zip(ins, kinds)]
    staged = [pltpu.VMEM(a.shape, a.dtype) for a, kind in zip(ins, kinds) if kind is Far]
    outs = [o if len(o) == 3 else o + ("",) for o in outs]
    staged += [pltpu.VMEM(o[0], o[1]) for o in outs if o[2] == "far"]
    n_in, n_after, n_out, n_staged = len(ins), len(after), len(outs), len(staged)
    name = getattr(kernel, "func", kernel).__name__
    micros, room = COSTS[name]
    cost = pl.CostEstimate(flops=micros * 1_100_000_000, bytes_accessed=micros * 3_600_000, transcendentals=0)

    def body(*refs):
        mover = Mover(refs[-1])
        held = list(refs[len(refs) - 1 - n_staged : -1])
        given = [
            Given(ref, held.pop(0), mover) if kind is Far else ref for ref, kind in zip(refs[:n_in], kinds)
        ]
        refs = refs[n_in + n_after : len(refs) - 1 - n_staged]
        made = [held.pop(0) if o[2] == "far" else ref for ref, o in zip(refs, outs)]
        kernel(mover, *given, *made, *refs[n_out + 1 :])
        for ref, written, o in zip(refs, made, outs):
            if o[2] == "far":
                mover.start(written, ref)
        for operand in given:
            if isinstance(operand, Given):
                operand.ready()
        refs[n_out][...] = jnp.zeros_like(refs[n_out])
        mover.wait()

    spaces = [pl.ANY if kind else SMEM if a.dtype == jnp.int32 and a.ndim == 1 else VMEM for a, kind in zip(ins, kinds)]
    results = pl.pallas_call(
        body,
        name=name,
        out_shape=[HBM(o[0], o[1]) if o[2] else jax.ShapeDtypeStruct(o[0], o[1]) for o in outs]
        + [jax.ShapeDtypeStruct((8, 128), f32)],
        in_specs=[pl.BlockSpec(memory_space=space) for space in spaces + [pl.ANY] * n_after],
        out_specs=[pl.BlockSpec(memory_space=pl.ANY if o[2] else VMEM) for o in outs] + [pl.BlockSpec(memory_space=VMEM)],
        scratch_shapes=[pltpu.VMEM(s, d) for s, d in scratch] + staged + [pltpu.SemaphoreType.DMA((64,))],
        compiler_params=pltpu.CompilerParams(vmem_limit_bytes=room << 20),
        cost_estimate=cost,
        input_output_aliases=dict([alias] if alias else []),
    )(
        *[pltpu.with_memory_space_constraint(a, HBM) if kind else a for a, kind in zip(ins, kinds)],
        *[pltpu.with_memory_space_constraint(a, HBM) if a.size > 4096 else a for a in after],
    )
    order[:] = results[n_out:]
    return results[:n_out]


def row_stats(values):
    mean = jnp.mean(values, -1, keepdims=True)
    centred = values - mean
    inv = lax.rsqrt(jnp.mean(centred * centred, -1, keepdims=True) + epsilon)
    return centred * inv, inv


def norm_back(d_normal, normal, inv):
    first = jnp.mean(d_normal, -1, keepdims=True)
    second = jnp.mean(d_normal * normal, -1, keepdims=True)
    return inv * (d_normal - first - normal * second)


def lead_hot(lead, seg_row):
    seg = seg_row[...]
    found = jnp.zeros_like(seg)
    for slot in range(lead.shape[0]):
        found = jnp.where(seg == slot, lead[slot], found)
    slots = lax.broadcasted_iota(jnp.int32, (LEADS, seg.shape[1]), 0)
    return jnp.where(slots == found, 1.0, 0.0).astype(bf16)


def vec_row(vec, row):
    return vec[row : row + 1, :].astype(f32)


def q_prep_kernel(mover, pos, qkv, table, g1, b1, qb, vb, ob, g2, b2, db, ub, *outs):
    z = pos[0]
    rw = qkv.shape[0]
    d = qkv.shape[1] // 3
    width = d // DEPTH
    side = outs[0].shape[1] - 3 * width

    def wide(values):
        values = values.astype(f32)
        return jnp.concatenate([values, jnp.zeros((values.shape[0], side - values.shape[1]), f32)], 1)

    rows = [wide(table[...])] + [wide(v[...].reshape(1, -1)) for v in (g1, b1, qb, vb, ob, g2, b2, db)]
    rows += [ub[...].reshape(1, -1).astype(f32), jnp.zeros((rw - VEC_ROWS - 1, side), f32)]
    small = jnp.concatenate(rows, 0).astype(bf16)
    for u, out in enumerate(outs):
        for part in range(3):
            start = pl.multiple_of(part * d + (z ^ u) * width, width)
            out[:, part * width : (part + 1) * width] = qkv[:, pl.ds(start, width)]
        out[:, 3 * width :] = small


def q_stack_kernel(mover, pos, b0, b1, b2, b3, out):
    for u, block in enumerate((b0, b1, b2, b3)):
        mover.start(block, out.at[pos[0] ^ u])


def up_prep_kernel(mover, up, out):
    fr = up.shape[1] // (DEPTH * PLANE * 2)
    for k in range(PLANE):
        for c in range(2):
            for zz in range(DEPTH):
                src = ((zz * PLANE + k) * 2 + c) * fr
                dst = (c * DEPTH + zz) * fr
                out[k, :, dst : dst + fr] = up[:, src : src + fr]


def first_shard_kernel(mover, out_rows, down, out):
    out[0] = out_rows[...]
    out[1] = down[0 : out.shape[1], :]


def shard_kernel(mover, ups, down, out):
    out[0:PLANE] = ups[...]
    out[PLANE:] = down[out.shape[1] :, :].reshape(PLANE - 1, -1, down.shape[1])


def qkv_kernel(mover, pos, lead, seg_row, toks, *refs):
    z, yx, c = pos[0], pos[1], pos[2]
    qa, qc, (n1, w_out, vec, up_b, o0, o1, o2, o3, w, proj) = refs[:4], refs[4:8], refs[8:]
    rows, d = toks.shape[1:]
    width = d // DEPTH
    head = width // PLANE
    rw = w.shape[3]
    fr = w.shape[4] - 3 * width
    pending = [mover.start(qa[k], w.at[:, yx ^ k, c]) for k in range(PLANE)]
    pending += [mover.start(qc[k], w.at[:, yx ^ k, 1 - c]) for k in range(PLANE)]
    mover.wait(pending)
    mover.start(w.at[:, :, :, :, 0 : 3 * width], w_out)
    for zz in range(DEPTH):
        for k in range(PLANE):
            for core in range(2):
                i = (zz * PLANE + k) * 2 + core
                side = w[zz, k, core, :, 3 * width :].astype(f32)
                vec[:, i * rw : (i + 1) * rw] = side[0:VEC_ROWS, 0:rw]
        for core in range(2):
            side = w[zz, yx, core, :, 3 * width :].astype(f32)
            start = (core * DEPTH + zz) * fr
            up_b[:, start : start + fr] = side[VEC_ROWS : VEC_ROWS + 1, :]
    shift = mul(lead_hot(lead, seg_row), vec[0:LEADS, :].astype(bf16), 0, 0)
    gain, bias = vec_row(vec, ROW_G1), vec_row(vec, ROW_B1)
    for s in range(DEPTH):
        normal, _ = row_stats(toks[z ^ s].astype(f32) + shift)
        n1[s * rows : (s + 1) * rows, :] = (normal * gain + bias).astype(bf16)
    at = pl.ds(pl.multiple_of(z * width, width), width)
    biases = jnp.concatenate(
        [vec[ROW_QB : ROW_QB + 1, at], jnp.zeros((1, width), f32), vec[ROW_VB : ROW_VB + 1, at]], 1
    )
    first = lax.broadcasted_iota(jnp.int32, (8, 3 * width), 0) == 0
    biases = jnp.where(first, biases, 0.0).astype(bf16)
    ones = jnp.ones((8, DEPTH * rows), bf16)
    weight = w[:, :, :, :, 0 : 3 * width].reshape(d, 3 * width)
    found = mul(weight, n1[...], 0, 1) + mul(biases, ones, 0, 0)
    proj[...] = found.astype(bf16).reshape(proj.shape)
    for k, out in enumerate((o0, o1, o2, o3)):
        for part in range(3):
            mover.start(proj.at[part * PLANE + (yx ^ k)], out.at[part * head : (part + 1) * head])


def fill_heads(seg_row, count, blocks, qa, ka, vt):
    head = blocks[0].shape[0] // 3
    span = blocks[0].shape[1]
    seg = jnp.concatenate([seg_row[...]] * (span // seg_row.shape[1]), 1)
    slots = lax.broadcasted_iota(jnp.int32, (16, span), 0)
    hot, real = jnp.where(slots == seg, 1.0, 0.0), slots < count
    q_mark = jnp.where(real, (hot - 1.0) * BIG, 0.0).astype(bf16)
    k_mark = jnp.where(real, hot, 0.0).astype(bf16)
    rest = qa.shape[0] - head - 16
    for k, block in enumerate(blocks):
        cols = slice(k * span, (k + 1) * span)
        qa[0:head, cols] = block[0:head, :] * jnp.asarray(score_scale, bf16)
        qa[head : head + 16, cols] = q_mark
        qa[head + 16 :, cols] = jnp.zeros((rest, span), bf16)
        keys = jnp.concatenate([block[head : 2 * head, :], k_mark, jnp.zeros((rest, span), bf16)], 0)
        ka[cols, :] = keys.T
        vt[:, cols] = block[2 * head :, :]


def attend_kernel(count, mover, seg_row, b0, b1, b2, b3, o0, o1, o2, o3, lse, qa, ka, vt):
    fill_heads(seg_row, count, (b0, b1, b2, b3), qa, ka, vt)
    span = b0.shape[1]
    rows = seg_row.shape[1]
    outs = (o0, o1, o2, o3)

    def step(k, carry):
        for half in range(DEPTH // 2):
            at = pl.ds(pl.multiple_of(k * span + half * 2 * rows, 2 * rows), 2 * rows)
            scores = mul(ka[...], qa[:, at], 1, 0)
            top = jnp.max(scores, 0, keepdims=True)
            soft = jnp.exp(scores - top)
            total = jnp.sum(soft, 0, keepdims=True)
            found = mul(vt[...], soft.astype(bf16), 1, 0) / total
            lse[:, at] = jnp.broadcast_to(top + jnp.log(total), (8, 2 * rows))
            for i in range(2):
                outs[half * 2 + i][:, pl.ds(pl.multiple_of(k * rows, rows), rows)] = found[
                    :, i * rows : (i + 1) * rows
                ].astype(bf16)
        return carry

    lax.fori_loop(0, PLANE, step, 0)


def out_kernel(mover, pos, a0, a1, a2, a3, first, p0, p1, p2, p3, att, w_out):
    z = pos[0]
    head = a0.shape[0]
    rows, d = p0.shape
    pending = [mover.start(first.at[:, :, 0], w_out)]
    for u, block in enumerate((a0, a1, a2, a3)):
        att[pl.ds(pl.multiple_of((z ^ u) * head, head), head), :] = block[...]
    mover.wait(pending)
    found = mul(att[...], w_out[...].reshape(-1, d), 0, 0)
    for j, out in enumerate((p0, p1, p2, p3)):
        out[...] = found[j * rows : (j + 1) * rows, :].astype(out.dtype)


def norm_kernel(mover, lead, seg_row, vec, tok, p0, p1, p2, p3, middle, n2):
    shift = mul(lead_hot(lead, seg_row), vec[0:LEADS, :].astype(bf16), 0, 0) + vec_row(vec, ROW_OB)
    total = p0[...].astype(f32) + p1[...].astype(f32) + p2[...].astype(f32) + p3[...].astype(f32)
    total = tok[...].astype(f32) + shift + total
    middle[...] = total
    normal, _ = row_stats(total)
    n2[...] = (normal * vec_row(vec, ROW_G2) + vec_row(vec, ROW_B2)).astype(bf16)


def down_copies(mover, first, ff, w_down):
    copies = [mover.start(first.at[:, c, 1], w_down.at[c, :, 0]) for c in range(2)]
    return copies + [mover.start(ff.at[:, c, PLANE:], w_down.at[c, :, 1:]) for c in range(2)]


def ffn_kernel(mover, pos, up_b, n0, n1, n2, n3, d_outs, first, ff, act, d_hid, p0, p1, p2, p3, d_up_b, w_up, w_down, hid):
    yx = pos[1]
    rows, d = n0.shape
    for_up = [mover.start(ff.at[:, c, 0:PLANE], w_up.at[:, :, c]) for c in range(2)]
    for_down = down_copies(mover, first, ff, w_down)
    mover.wait(for_up)
    normed = jnp.concatenate([n0[...], n1[...], n2[...], n3[...]], 0)
    up = w_up[...].reshape(d, -1)
    hid[...] = mul(normed, up, 1, 0) + up_b[...].astype(f32)
    mover.wait(for_down)
    down = w_down[...].reshape(-1, d)
    sums = jnp.zeros(d_up_b.shape, f32)
    for j in range(PLANE):
        here = slice(j * rows, (j + 1) * rows)
        hidden = hid[here, :]
        phi = 0.5 * (1.0 + lax.erf(hidden * 0.7071067811865476))
        act[here, :] = (hidden * phi).astype(bf16)
        slope = phi + hidden * (jnp.exp(-0.5 * hidden * hidden) * 0.3989422804014327)
        d_act = mul(d_outs[yx ^ j], down, 1, 1)
        low = (d_act * slope).astype(bf16)
        d_hid[here, :] = low
        sums = sums + jnp.sum(low.astype(f32), 0, keepdims=True)
    d_up_b[...] = sums
    back = mul(d_hid[...], up, 1, 1)
    for j, out in enumerate((p0, p1, p2, p3)):
        out[...] = back[j * rows : (j + 1) * rows, :].astype(out.dtype)


def ffn_grad_kernel(mover, pos, act, d_hid, n0, n1, n2, n3, first, ff, d_outs, grads, outs, up_grad, down_grad, w_down):
    yx = pos[1]
    rows, d = outs.shape[1:]
    pending = down_copies(mover, first, ff, w_down)
    normed = jnp.concatenate([n0[...], n1[...], n2[...], n3[...]], 0)
    up_grad[...] = mul(normed, d_hid[...], 0, 0).astype(bf16).reshape(up_grad.shape)
    for c in range(2):
        mover.start(up_grad.at[:, :, c], grads.at[:, c, 0:PLANE])
    d_down = jnp.zeros((act.shape[1], d), f32)
    for j in range(PLANE):
        d_down = d_down + mul(act[j * rows : (j + 1) * rows, :], d_outs[yx ^ j], 0, 0)
    down_grad[...] = d_down.astype(bf16).reshape(down_grad.shape)
    for c in range(2):
        mover.start(down_grad.at[c], grads.at[:, c, PLANE : 2 * PLANE])
    mover.wait(pending)
    found = mul(act[...], w_down[...].reshape(-1, d), 1, 0)
    for j in range(PLANE):
        outs[yx ^ j] = found[j * rows : (j + 1) * rows, :].astype(bf16)


def ffn_last_kernel(mover, shard, ups, down, out_rows):
    ups[...] = shard[0:PLANE]
    down[...] = shard[PLANE : 2 * PLANE].astype(f32).reshape(down.shape)
    out_rows[...] = shard[2 * PLANE].astype(f32)


def branch_kernel(mover, vec, middle, d_out, p0, p1, p2, p3, d_mid, d_branch, d_vec):
    dy = p0[...].astype(f32) + p1[...].astype(f32) + p2[...].astype(f32) + p3[...].astype(f32)
    normal, inv = row_stats(middle[...])
    d_rows = d_out[...].astype(f32)
    total = d_rows + norm_back(dy * vec_row(vec, ROW_G2), normal, inv)
    d_mid[...] = total
    low = total.astype(bf16)
    d_branch[...] = low
    sums = [jnp.sum(v, 0, keepdims=True) for v in (dy * normal, dy, d_rows, low.astype(f32))]
    d_vec[...] = jnp.concatenate(sums + [jnp.zeros((4, dy.shape[1]), f32)], 0)


def out_back_kernel(mover, pos, att, w_out, b0, b1, b2, b3, others, o0, o1, o2, o3, grads, d_att, grad):
    z = pos[0]
    head = o0.shape[0]
    branch = jnp.concatenate([b0[...], b1[...], b2[...], b3[...]], 0)
    d = branch.shape[1]
    d_att[...] = mul(w_out[...].reshape(-1, d), branch, 1, 1).astype(bf16).reshape(d_att.shape)
    for u, out in enumerate((o0, o1, o2, o3)):
        out[...] = d_att[z ^ u]
    grad[...] = mul(att[...], branch, 1, 0).astype(bf16).reshape(grad.shape)
    mover.start(grad, grads.at[:, :, 2 * PLANE])


def attend_back_kernel(count, mover, seg_row, b0, b1, b2, b3, c0, c1, c2, c3, lse,
                       o0, o1, o2, o3, qa, ka, vt, vn, dot, dq, dk, dv, kt):
    fill_heads(seg_row, count, (b0, b1, b2, b3), qa, ka, vt)
    span = b0.shape[1]
    rows = seg_row.shape[1]
    head = vt.shape[0]
    for k, block in enumerate((b0, b1, b2, b3)):
        cols = slice(k * span, (k + 1) * span)
        vn[cols, :] = vt[:, cols].T
        kt[:, cols] = block[head : 2 * head, :]
        for s, block in enumerate((c0, c1, c2, c3)):
            dot[:, k * span + s * rows : k * span + (s + 1) * rows] = block[:, k * rows : (k + 1) * rows]
    dk[...] = jnp.zeros_like(dk)
    dv[...] = jnp.zeros_like(dv)
    logs = lse

    def step(i, carry):
        for k in (2 * i, 2 * i + 1):
            at = pl.ds(pl.multiple_of(k * span, span), span)
            scores = mul(ka[...], qa[:, at], 1, 0)
            soft = jnp.exp(scores - logs[0:1, at])
            d_out = dot[:, at]
            d_soft = mul(vn[...], d_out, 1, 0)
            delta = jnp.sum(soft * d_soft, 0, keepdims=True)
            d_scores = (soft * (d_soft - delta)).astype(bf16)
            dv[...] += mul(d_out, soft.astype(bf16), 1, 1)
            dk[...] += mul(qa[0:head, at], d_scores, 1, 1)
            dq[:, at] = (mul(kt[...], d_scores, 1, 0) * score_scale).astype(bf16)
        return carry

    lax.fori_loop(0, PLANE // 2, step, 0)
    for k, out in enumerate((o0, o1, o2, o3)):
        cols = slice(k * span, (k + 1) * span)
        out[0:head, :] = dq[:, cols]
        out[head : 2 * head, :] = dk[:, cols].astype(bf16)
        out[2 * head :, :] = dv[:, cols].astype(bf16)


def join_heads(yx, blocks, joined):
    head = blocks[0].shape[0] // 3
    for k, block in enumerate(blocks):
        for part in range(3):
            joined[part * PLANE + (yx ^ k)] = block[part * head : (part + 1) * head, :]
    return joined[...].reshape(3 * PLANE * head, -1)


def qkv_back_kernel(mover, pos, lead, seg_row, vec, toks, n1, w, g0, g1, g2, g3, d_mid, d_mid_vec, d_up_b,
                    r0, r1, r2, r3, mine, o0, o1, joined, d_vec, both):
    z, yx, core = pos[0], pos[1], pos[2]
    rows, d = r0.shape
    width = d // DEPTH
    head = width // PLANE
    rw = mine.shape[2]
    cols = 3 * width
    fr = mine.shape[3] - cols
    for k, block in enumerate((g0, g1, g2, g3)):
        for part in range(3):
            joined[part * PLANE + (yx ^ k)] = block[part * head : (part + 1) * head, :]
    grads = joined[...].reshape(cols, DEPTH * rows)
    grad = mul(n1[...], grads, 0, 1).astype(bf16)
    back = mul(grads, w[...].reshape(d, cols), 0, 1)
    hot = lead_hot(lead, seg_row)
    shift = mul(hot, vec[0:LEADS, :].astype(bf16), 0, 0)
    gain = vec_row(vec, ROW_G1)
    d_gain = jnp.zeros((1, d), f32)
    d_bias = jnp.zeros((1, d), f32)
    d_emb = d_mid[...]
    for s, out in enumerate((r0, r1, r2, r3)):
        piece = back[s * rows : (s + 1) * rows, :]
        out[...] = piece.astype(out.dtype)
        normal, inv = row_stats(toks[z ^ s].astype(f32) + shift)
        d_gain = d_gain + jnp.sum(piece * normal, 0, keepdims=True)
        d_bias = d_bias + jnp.sum(piece, 0, keepdims=True)
        d_emb = d_emb + norm_back(piece * gain, normal, inv)
    high = d_emb.astype(bf16)
    low = (d_emb - high.astype(f32)).astype(bf16)
    d_vec[...] = jnp.zeros_like(d_vec)
    d_vec[0:LEADS, :] = mul(hot, high, 1, 0) + mul(hot, low, 1, 0)
    sums = mul(jnp.ones((8, DEPTH * rows), bf16), grads, 1, 1)
    d_vec[ROW_G1 : ROW_G1 + 1, :] = d_gain
    d_vec[ROW_B1 : ROW_B1 + 1, :] = d_bias
    at = pl.ds(pl.multiple_of(z * width, width), width)
    d_vec[ROW_QB : ROW_QB + 1, at] = sums[0:1, 0:width]
    d_vec[ROW_VB : ROW_VB + 1, at] = sums[0:1, 2 * width :]
    for i, row in enumerate((ROW_G2, ROW_B2, ROW_DB, ROW_OB)):
        d_vec[row : row + 1, :] = d_mid_vec[i : i + 1, :]
    small = d_vec[...]
    mark = lax.broadcasted_iota(jnp.int32, (rw, fr), 0) == VEC_ROWS
    for zz in range(DEPTH):
        for k in range(PLANE):
            for c in range(2):
                i = (zz * PLANE + k) * 2 + c
                side = jnp.concatenate([small[:, i * rw : (i + 1) * rw], jnp.zeros((rw, fr - rw), f32)], 1)
                start = (c * DEPTH + zz) * fr
                last = jnp.where(yx == k, d_up_b[:, start : start + fr], 0.0)
                side = jnp.where(mark, last, side).astype(bf16)
                both[zz, k, c] = jnp.concatenate([grad[i * rw : (i + 1) * rw, :], side], 1)
    mover.start(both.at[0:2, :, 1 - core], o0)
    mover.start(both.at[2:4, :, 1 - core], o1)
    mover.start(both.at[:, :, core], mine)


def first_back_kernel(mover, lead, seg_row, vec, tok, d_mid, r0, r1, r2, r3, out):
    shift = mul(lead_hot(lead, seg_row), vec[0:LEADS, :].astype(bf16), 0, 0)
    normal, inv = row_stats(tok[...].astype(f32) + shift)
    dy = r0[...].astype(f32) + r1[...].astype(f32) + r2[...].astype(f32) + r3[...].astype(f32)
    out[...] = d_mid[...] + norm_back(dy * vec_row(vec, ROW_G1), normal, inv)


def layer_out_kernel(mover, vec, middle, blocks, out):
    total = middle[...] + vec_row(vec, ROW_DB)
    for k in range(PLANE):
        total = total + blocks[k].astype(f32)
    out[...] = total.astype(bf16)


def pair_kernel(mover, mine, o0, o1, out):
    for k in range(PLANE):
        out[k, 0:2] = (mine[0:2, k].astype(f32) + o0[:, k].astype(f32)).astype(bf16)
        out[k, 2:4] = (mine[2:4, k].astype(f32) + o1[:, k].astype(f32)).astype(bf16)


def quad_kernel(mover, pos, blocks, o0, o1, o2, o3, total):
    found = blocks[0].astype(f32)
    for k in range(1, PLANE):
        found = found + blocks[k].astype(f32)
    total[...] = found.astype(bf16)
    for u, out in enumerate((o0, o1, o2, o3)):
        out[...] = total[pos[0] ^ u]


def qkv_join_kernel(mover, pos, b0, b1, b2, b3, out, table, *rest):
    z = pos[0]
    rw = out.shape[0]
    width = out.shape[1] // (3 * DEPTH)
    side = jnp.zeros((rw, b0.shape[1] - 3 * width), f32)
    for s, block in enumerate((b0, b1, b2, b3)):
        for part in range(3):
            start = pl.multiple_of((part * DEPTH + (z ^ s)) * width, width)
            out[:, pl.ds(start, width)] = block[:, part * width : (part + 1) * width].astype(f32)
        side = side + block[:, 3 * width :].astype(f32)
    table[...] = side[0:LEADS, 0:rw]
    for i, row in enumerate(rest[:-1]):
        row[...] = side[LEADS + i : LEADS + i + 1, 0:rw].reshape(rw)
    rest[-1][...] = side[VEC_ROWS : VEC_ROWS + 1, :].reshape(-1)


def up_join_kernel(mover, blocks, out):
    fr = blocks.shape[2] // (2 * DEPTH)
    for k in range(PLANE):
        for c in range(2):
            for zz in range(DEPTH):
                src = (c * DEPTH + zz) * fr
                dst = ((zz * PLANE + k) * 2 + c) * fr
                out[:, dst : dst + fr] = blocks[k, :, src : src + fr].astype(f32)


COSTS = {
    "q_prep_kernel": (1, 4), "q_stack_kernel": (1, 4), "up_prep_kernel": (1, 4), "shard_kernel": (1, 4), "first_shard_kernel": (1, 4), "qkv_kernel": (5, 20),
    "attend_kernel": (9, 24), "out_kernel": (2, 12), "norm_kernel": (2, 8), "ffn_kernel": (8, 32), "ffn_grad_kernel": (8, 32),
    "branch_kernel": (2, 12), "out_back_kernel": (3, 12), "attend_back_kernel": (15, 32),
    "qkv_back_kernel": (10, 28), "first_back_kernel": (2, 8), "layer_out_kernel": (1, 8),
    "pair_kernel": (2, 8), "quad_kernel": (1, 8), "qkv_join_kernel": (1, 4), "up_join_kernel": (2, 8), "ffn_last_kernel": (1, 8),
}
PLANE_AXES = ("y", "x")


def trade(blocks, axes):
    return lax.all_to_all(blocks, axes, split_axis=0, concat_axis=0, tiled=True)


ALL = ("z", "y", "x", "g")


def across(blocks):
    swap = [(0, 1), (1, 0)]
    return (
        blocks[0],
        lax.ppermute(blocks[1], "x", swap),
        lax.ppermute(blocks[2], "y", swap),
        lax.ppermute(blocks[3], ("y", "x"), [(i, i ^ 3) for i in range(PLANE)]),
    )


def to_depth(block, step):
    return lax.ppermute(block, "z", [(i, i ^ step) for i in range(DEPTH)])


def along(blocks):
    return (blocks[0],) + tuple(to_depth(blocks[u], u) for u in range(1, DEPTH))


def core_swap(block):
    return lax.ppermute(block, "g", [(0, 1), (1, 0)])


def far(blocks):
    return [Far(block) for block in blocks]


def raw(blocks):
    return [Raw(block) for block in blocks]


def fast_local(
    tokens, segment_ids, lead_index, lead_table, ln1_gain, ln1_bias, qkv_weight, q_bias, v_bias,
    out_weight, out_bias, ln2_gain, ln2_bias, up_weight, up_bias, down_weight, down_bias, d_out,
):
    z = lax.axis_index("z")
    yx = lax.axis_index("y") * 2 + lax.axis_index("x")
    c = lax.axis_index("g")
    pos = jnp.stack([z, yx, c]).astype(jnp.int32)
    tok, d_rows = tokens[0], d_out[0]
    rows, d = tok.shape
    head = d // HEADS
    span = DEPTH * rows
    group = PLANE * span
    rw = qkv_weight.shape[0]
    fr = down_weight.shape[0]
    ff = 2 * DEPTH * fr
    lead = lead_index[0]
    count = lead.shape[0]
    width = 3 * d // DEPTH
    seg_row = segment_ids
    up_shape, down_shape = (DEPTH, PLANE, 2, rw, ff), (2, DEPTH, PLANE, rw, d)

    order = []
    call = functools.partial(run, order)
    side = width + -(-max(rw, fr) // 128) * 128

    q_rows = along(
        call(
            q_prep_kernel,
            [((rw, side), bf16)] * 4,
            [pos]
            + far((qkv_weight, lead_table, ln1_gain, ln1_bias, q_bias, v_bias, out_bias, ln2_gain, ln2_bias, down_bias, up_bias)),
        )
    )
    toks = lax.all_gather(tok, "z", axis=0)
    (first_shard,) = call(first_shard_kernel, [((2, rw, d), bf16, "far")], [out_weight, down_weight])
    first = lax.all_gather(first_shard, ("z", "g"), axis=0).reshape(DEPTH, 2, 2, rw, d)
    (up_cols,) = call(up_prep_kernel, [((PLANE, rw, ff), bf16)], [up_weight])
    up_cols = trade(up_cols, PLANE_AXES)
    (q_stack,) = call(q_stack_kernel, [((DEPTH, rw, side), bf16)], [pos, *q_rows], after=[up_cols])
    q_plane = across((q_stack,) * PLANE)
    q_other = [core_swap(block) for block in q_plane]
    n1, w_qkv, vec, up_b, *blocks = call(
        qkv_kernel,
        [((span, d), bf16, "far"), ((DEPTH, PLANE, 2, rw, width), bf16, "raw"), ((VEC_ROWS, d), f32), ((1, ff), f32)]
        + [((3 * head, span), bf16)] * 4,
        [pos, lead, seg_row, Far(toks), *q_plane, *q_other],
        [((DEPTH, PLANE, 2, rw, side), bf16), ((3 * PLANE, head, span), bf16)],
    )
    (ff_shard,) = call(shard_kernel, [((2 * PLANE - 1, rw, d), bf16, "far")], [up_cols, down_weight])
    ff_all = lax.all_gather(ff_shard, ("z", "g"), axis=0).reshape(DEPTH, 2, 2 * PLANE - 1, rw, d)
    blocks = across(blocks)

    d_outs = trade(jnp.broadcast_to(d_rows[None], (PLANE, rows, d)), PLANE_AXES)
    *att_parts, lse = call(
        functools.partial(attend_kernel, count),
        [((head, PLANE * rows), bf16)] * 4 + [((8, group), f32)],
        [seg_row, *blocks],
        [((128, group), bf16), ((group, 128), bf16), ((head, group), bf16)],
    )
    att_parts = along(att_parts)
    *parts, att, w_out = call(
        out_kernel,
        [((rows, d), f32)] + [((rows, d), bf16)] * 3 + [((DEPTH * head, span), bf16), ((DEPTH, 2, rw, d), bf16)],
        [pos, *att_parts, Raw(first)],
        after=[d_outs],
    )
    parts = across(parts)
    middle, n2 = call(norm_kernel, [((rows, d), f32, "far"), ((rows, d), bf16)], [lead, seg_row, vec, Far(tok), *parts])
    n2_plane = across((n2,) * PLANE)

    act, d_hid, p0, p1, p2, p3, d_up_b = call(
        ffn_kernel,
        [((span, ff), bf16), ((span, ff), bf16), ((rows, d), f32)] + [((rows, d), bf16)] * 3 + [((1, ff), f32)],
        [pos, up_b, *n2_plane, Far(d_outs), Raw(first), Raw(ff_all)],
        [(up_shape, bf16), (down_shape, bf16), ((span, ff), f32)],
    )
    parts = across((p0, p1, p2, p3))
    ff_grad, outs = call(
        ffn_grad_kernel,
        [((DEPTH, 2, 2 * PLANE + 1, rw, d), bf16, "raw"), ((PLANE, rows, d), bf16, "far")],
        [pos, act, d_hid, *n2_plane, Raw(first), Raw(ff_all), Far(d_outs)],
        [(up_shape, bf16), (down_shape, bf16), (down_shape, bf16)],
    )
    d_mid, d_branch, d_mid_vec = call(
        branch_kernel,
        [((rows, d), f32, "far"), ((rows, d), bf16), ((8, d), f32)],
        [vec, Far(middle), Far(d_rows), *parts],
    )
    branch_plane = across((d_branch,) * PLANE)
    *d_att, ff_grad = call(
        out_back_kernel,
        [((head, span), bf16)] * 4 + [(ff_grad.shape, bf16, "raw")],
        [pos, att, w_out, *branch_plane, Raw(ff_grad)],
        [((DEPTH, head, span), bf16), ((DEPTH, 2, rw, d), bf16)],
        alias=(7, 4),
    )
    d_att = along(d_att)
    ff_grad = lax.psum_scatter(
        ff_grad.reshape(2 * DEPTH, 2 * PLANE + 1, rw, d), ("z", "g"), scatter_dimension=0, tiled=True
    )[0]
    outs = trade(outs, PLANE_AXES)

    d_blocks = call(
        functools.partial(attend_back_kernel, count),
        [((3 * head, span), bf16)] * 4,
        [seg_row, *blocks, *d_att, lse],
        [((128, group), bf16), ((group, 128), bf16), ((head, group), bf16), ((group, head), bf16),
         ((head, group), bf16), ((head, group), bf16), ((head, group), f32), ((head, group), f32), ((head, group), bf16)],
    )
    d_blocks = across(d_blocks)
    (layer_out,) = call(layer_out_kernel, [((rows, d), bf16)], [vec, Far(middle), outs])
    r0, r1, r2, r3, mine, o0, o1 = call(
        qkv_back_kernel,
        [((rows, d), f32)] + [((rows, d), bf16)] * 3
        + [((DEPTH, PLANE, rw, side), bf16)] + [((DEPTH // 2, PLANE, rw, side), bf16)] * 2,
        [pos, lead, seg_row, vec, Far(toks), Far(n1), Far(w_qkv), *d_blocks, Far(d_mid), d_mid_vec, d_up_b],
        [((3 * PLANE, head, span), bf16), ((rw, d), f32), ((DEPTH, PLANE, 2, rw, side), bf16)],
    )
    returned = along((r0, r1, r2, r3))
    (quads,) = call(
        pair_kernel, [((PLANE, DEPTH, rw, side), bf16)], [mine, core_swap(o0), core_swap(o1)]
    )
    quads = trade(quads, PLANE_AXES)
    cols = along(call(quad_kernel, [((rw, side), bf16)] * 4, [pos, quads], [((DEPTH, rw, side), bf16)]))
    ups, d_down, d_out_weight = call(
        ffn_last_kernel, [((PLANE, rw, ff), bf16), ((fr, d), f32), ((rw, d), f32)], [ff_grad]
    )
    ups = trade(ups, PLANE_AXES)
    (d_tokens,) = call(
        first_back_kernel, [((rows, d), f32)], [lead, seg_row, vec, Far(tok), Far(d_mid), *returned]
    )
    d_qkv, table, d_g1, d_b1, d_qb, d_vb, d_ob, d_g2, d_b2, d_db, d_ub = call(
        qkv_join_kernel,
        [((rw, 3 * d), f32), ((LEADS, rw), f32)] + [((rw,), f32)] * 8 + [((fr,), f32)],
        [pos, *cols],
    )
    (d_up,) = call(up_join_kernel, [((rw, PLANE * ff), f32)], [ups])
    return (
        layer_out[None], d_tokens[None], table, d_g1, d_b1, d_qkv, d_qb, d_vb, d_out_weight, d_ob,
        d_g2, d_b2, d_up, d_ub, d_down, d_db,
    )


def specs(band, grp):
    every = band + grp
    rows = P(grp, band, None)
    in_specs = (
        rows, P(grp, band), P(grp, None), P(None, every), P(every), P(every), P(every, None), P(every), P(every),
        P(every, None), P(every), P(every), P(every), P(every, None), P(every), P(every, None), P(every), rows,
    )
    out_specs = (
        rows, rows, P(None, every), P(every), P(every), P(every, None), P(every), P(every), P(every, None), P(every),
        P(every), P(every), P(every, None), P(every), P(every, None), P(every),
    )
    return in_specs, out_specs


def solution(mesh):
    band, grp = mesh.shape["band"], mesh.shape["grp"]
    if band == HEADS and grp == 2:
        mesh = Mesh(mesh.devices.reshape(DEPTH, 2, 2, grp), ("z", "y", "x", "g"))
        in_specs, out_specs = specs(("z", "y", "x"), ("g",))
        return jax.shard_map(fast_local, mesh=mesh, in_specs=in_specs, out_specs=out_specs, check_vma=False)
    in_specs, out_specs = specs(("band",), ("grp",))
    return jax.shard_map(local, mesh=mesh, in_specs=in_specs, out_specs=out_specs, check_vma=False)
```

```python
import functools
import math

import jax
import jax.numpy as jnp
from jax import lax
from jax.experimental import pallas as pl
from jax.experimental.pallas import tpu as pltpu
from jax.sharding import Mesh
from jax.sharding import PartitionSpec as P

bf16, f32 = jnp.bfloat16, jnp.float32

HEADS = 16


epsilon = 1e-05
score_scale = 0.125
masked_score = -1e30


def norm_rows(values, norm_gain, norm_bias):
    row_mean = jnp.mean(values, -1, keepdims=True)
    centred = values - row_mean
    row_var = jnp.mean(centred * centred, -1, keepdims=True)
    return centred * lax.rsqrt(row_var + epsilon) * norm_gain + norm_bias


def gelu_exact(values):
    return jax.nn.gelu(values, approximate=False)


def split_blocks(values, block_rows):
    return values.reshape((values.shape[0] // block_rows, block_rows) + values.shape[1:])


def block_scores(query_heads, key_heads, allowed):
    raw_scores = (
        jnp.einsum("qhd,khd->hqk", query_heads, key_heads, preferred_element_type=jnp.float32)
        * score_scale
    )
    return jnp.where(allowed[None], raw_scores, masked_score)


def softmax_rows(query_heads, key_heads, allowed, log_total):
    scores = block_scores(query_heads, key_heads, allowed)
    return jnp.where(allowed[None], jnp.exp(scores - log_total[:, :, None]), 0.0)


def score_grads(query_heads, key_heads, value_heads, d_heads, allowed, log_total, row_delta):
    soft_rows = softmax_rows(query_heads, key_heads, allowed, log_total)
    d_soft = jnp.einsum("qhd,khd->hqk", d_heads, value_heads, preferred_element_type=jnp.float32)
    d_scores = (soft_rows * (d_soft - row_delta[:, :, None])).astype(jnp.bfloat16)
    return (soft_rows.astype(jnp.bfloat16), d_scores)


def local(
    tokens,
    segment_ids,
    lead_index,
    lead_table,
    ln1_gain,
    ln1_bias,
    qkv_weight,
    q_bias,
    v_bias,
    out_weight,
    out_bias,
    ln2_gain,
    ln2_bias,
    up_weight,
    up_bias,
    down_weight,
    down_bias,
    d_out,
):
    (
        table_full,
        first_gain,
        first_shift,
        project_full,
        query_shift,
        value_shift,
        out_full,
        out_shift,
        second_gain,
        second_shift,
        up_full,
        up_shift,
        down_full,
        down_shift,
    ) = (
        lax.all_gather(lead_table, ("band", "grp"), axis=1, tiled=True),
        lax.all_gather(ln1_gain, ("band", "grp"), axis=0, tiled=True),
        lax.all_gather(ln1_bias, ("band", "grp"), axis=0, tiled=True),
        lax.all_gather(qkv_weight, ("band", "grp"), axis=0, tiled=True),
        lax.all_gather(q_bias, ("band", "grp"), axis=0, tiled=True),
        lax.all_gather(v_bias, ("band", "grp"), axis=0, tiled=True),
        lax.all_gather(out_weight, ("band", "grp"), axis=0, tiled=True),
        lax.all_gather(out_bias, ("band", "grp"), axis=0, tiled=True),
        lax.all_gather(ln2_gain, ("band", "grp"), axis=0, tiled=True),
        lax.all_gather(ln2_bias, ("band", "grp"), axis=0, tiled=True),
        lax.all_gather(up_weight, ("band", "grp"), axis=0, tiled=True),
        lax.all_gather(up_bias, ("band", "grp"), axis=0, tiled=True),
        lax.all_gather(down_weight, ("band", "grp"), axis=0, tiled=True),
        lax.all_gather(down_bias, ("band", "grp"), axis=0, tiled=True),
    )
    tok_rows = tokens.shape[1]
    features = tokens.shape[2]
    head_dim = features // HEADS
    band_count = lax.axis_size("band")
    group_rows = tok_rows * band_count
    block_rows = math.gcd(group_rows, 1024)
    own_segments = segment_ids[0]
    group_segments = jnp.tile(own_segments, band_count)
    sample_count = lead_index.shape[1]
    lead_count = lead_table.shape[0]
    sample_hot = (
        own_segments[:, None] == jnp.arange(sample_count, dtype=jnp.int32)[None, :]
    ).astype(jnp.float32)
    lead_hot = (lead_index[0][:, None] == jnp.arange(lead_count, dtype=jnp.int32)[None, :]).astype(
        jnp.float32
    )
    lead_pick = jnp.dot(sample_hot, lead_hot, precision=lax.Precision.HIGHEST)
    embedded = tokens[0].astype(jnp.float32) + jnp.dot(
        lead_pick.astype(jnp.bfloat16), table_full, preferred_element_type=jnp.float32
    )
    normed_first = norm_rows(
        embedded, first_gain.astype(jnp.float32), first_shift.astype(jnp.float32)
    ).astype(jnp.bfloat16)
    projected = jnp.dot(normed_first, project_full, preferred_element_type=jnp.float32)
    query_rows = (projected[:, :features] + query_shift.astype(jnp.float32)).astype(jnp.bfloat16)
    key_rows = projected[:, features : 2 * features].astype(jnp.bfloat16)
    value_rows = (projected[:, 2 * features :] + value_shift.astype(jnp.float32)).astype(
        jnp.bfloat16
    )
    key_all, value_all = (
        lax.all_gather(key_rows, "band", axis=0, tiled=True),
        lax.all_gather(value_rows, "band", axis=0, tiled=True),
    )
    query_heads = query_rows.reshape(tok_rows, HEADS, head_dim)
    key_blocks = split_blocks(key_all.reshape(group_rows, HEADS, head_dim), block_rows)
    value_blocks = split_blocks(value_all.reshape(group_rows, HEADS, head_dim), block_rows)
    segment_blocks = split_blocks(group_segments, block_rows)

    def stats_step(running, block_data):
        running_max, running_sum = running
        key_block, key_segments = block_data
        allowed = own_segments[:, None] == key_segments[None, :]
        scores = block_scores(query_heads, key_block, allowed)
        new_max = jnp.maximum(running_max, jnp.max(scores, -1))
        block_sum = jnp.sum(
            jnp.where(allowed[None], jnp.exp(scores - new_max[:, :, None]), 0.0), -1
        )
        return ((new_max, running_sum * jnp.exp(running_max - new_max) + block_sum), None)

    start_max = jnp.full((HEADS, tok_rows), masked_score, jnp.float32)
    start_sum = jnp.zeros((HEADS, tok_rows), jnp.float32)
    (final_max, final_sum), unused_out = lax.scan(
        stats_step, (start_max, start_sum), (key_blocks, segment_blocks)
    )
    log_total = final_max + jnp.log(final_sum)

    def output_step(running, block_data):
        high_part, low_part = running
        key_block, value_block, key_segments = block_data
        allowed = own_segments[:, None] == key_segments[None, :]
        soft_rows = softmax_rows(query_heads, key_block, allowed, log_total)
        soft_low = soft_rows.astype(jnp.bfloat16)
        soft_rest = (soft_rows - soft_low.astype(jnp.float32)).astype(jnp.bfloat16)
        high_part = high_part + jnp.einsum(
            "hqk,khd->qhd", soft_low, value_block, preferred_element_type=jnp.float32
        )
        low_part = low_part + jnp.einsum(
            "hqk,khd->qhd", soft_rest, value_block, preferred_element_type=jnp.float32
        )
        return ((high_part, low_part), None)

    empty_heads = jnp.zeros((tok_rows, HEADS, head_dim), jnp.float32)
    (attn_high, attn_low), unused_out = lax.scan(
        output_step, (empty_heads, empty_heads), (key_blocks, value_blocks, segment_blocks)
    )
    attended = attn_high.reshape(tok_rows, features).astype(jnp.bfloat16)
    middle = (
        embedded
        + jnp.dot(attended, out_full, preferred_element_type=jnp.float32)
        + out_shift.astype(jnp.float32)
    )
    normed_second = norm_rows(
        middle, second_gain.astype(jnp.float32), second_shift.astype(jnp.float32)
    ).astype(jnp.bfloat16)
    hidden = jnp.dot(normed_second, up_full, preferred_element_type=jnp.float32) + up_shift.astype(
        jnp.float32
    )
    activated = gelu_exact(hidden).astype(jnp.bfloat16)
    result = (
        middle
        + jnp.dot(activated, down_full, preferred_element_type=jnp.float32)
        + down_shift.astype(jnp.float32)
    )
    layer_out = result.astype(jnp.bfloat16)[None]
    first_gain_back, project_back, out_back, second_gain_back, up_back, down_back = (
        lax.all_gather(ln1_gain, ("band", "grp"), axis=0, tiled=True),
        lax.all_gather(qkv_weight, ("band", "grp"), axis=0, tiled=True),
        lax.all_gather(out_weight, ("band", "grp"), axis=0, tiled=True),
        lax.all_gather(ln2_gain, ("band", "grp"), axis=0, tiled=True),
        lax.all_gather(up_weight, ("band", "grp"), axis=0, tiled=True),
        lax.all_gather(down_weight, ("band", "grp"), axis=0, tiled=True),
    )
    d_rows = d_out[0]
    d_down_shift = jnp.sum(d_rows.astype(jnp.float32), 0)
    d_down = jnp.einsum("tf,td->fd", activated, d_rows, preferred_element_type=jnp.float32)
    d_act = jnp.einsum("td,fd->tf", d_rows, down_back, preferred_element_type=jnp.float32)
    unused_gelu, gelu_back = jax.vjp(gelu_exact, hidden)
    d_hidden = gelu_back(d_act)[0].astype(jnp.bfloat16)
    d_up_shift = jnp.sum(d_hidden.astype(jnp.float32), 0)
    d_up = jnp.einsum("td,tf->df", normed_second, d_hidden, preferred_element_type=jnp.float32)
    d_normed_second = jnp.einsum("tf,df->td", d_hidden, up_back, preferred_element_type=jnp.float32)
    unused_second, second_back = jax.vjp(
        norm_rows, middle, second_gain_back.astype(jnp.float32), second_shift.astype(jnp.float32)
    )
    d_middle_part, d_gain_second, d_shift_second = second_back(d_normed_second)
    d_middle = d_rows.astype(jnp.float32) + d_middle_part
    d_branch = d_middle.astype(jnp.bfloat16)
    d_out_shift = jnp.sum(d_branch.astype(jnp.float32), 0)
    d_out_full = jnp.einsum("ti,to->io", attended, d_branch, preferred_element_type=jnp.float32)
    d_attended = jnp.einsum(
        "to,io->ti", d_branch, out_back, preferred_element_type=jnp.float32
    ).astype(jnp.bfloat16)
    d_heads = d_attended.reshape(tok_rows, HEADS, head_dim)
    row_delta = jnp.sum(d_heads.astype(jnp.float32) * (attn_high + attn_low), -1).T

    def query_grad(d_query_acc, key_block, value_block, key_segments):
        allowed = own_segments[:, None] == key_segments[None, :]
        soft_low, d_scores = score_grads(
            query_heads, key_block, value_block, d_heads, allowed, log_total, row_delta
        )
        d_query_acc = d_query_acc + jnp.einsum(
            "hqk,khd->qhd", d_scores, key_block, preferred_element_type=jnp.float32
        )
        return (d_query_acc, soft_low, d_scores)

    def owner_step(d_query_acc, block_data):
        key_block, value_block, key_segments = block_data
        d_query_acc, soft_low, d_scores = query_grad(
            d_query_acc, key_block, value_block, key_segments
        )
        d_key_block = (
            jnp.einsum("hqk,qhd->khd", d_scores, query_heads, preferred_element_type=jnp.float32)
            * score_scale
        )
        d_value_block = jnp.einsum(
            "hqk,qhd->khd", soft_low, d_heads, preferred_element_type=jnp.float32
        )
        return (d_query_acc, (d_key_block, d_value_block))

    d_query_sum, (d_key_parts, d_value_parts) = lax.scan(
        owner_step, empty_heads, (key_blocks, value_blocks, segment_blocks)
    )
    d_key_sum, d_value_sum = (
        lax.psum_scatter(
            d_key_parts.reshape(group_rows, features).astype(jnp.bfloat16),
            "band",
            scatter_dimension=0,
            tiled=True,
        ).astype(jnp.float32),
        lax.psum_scatter(
            d_value_parts.reshape(group_rows, features).astype(jnp.bfloat16),
            "band",
            scatter_dimension=0,
            tiled=True,
        ).astype(jnp.float32),
    )
    d_query = (d_query_sum.reshape(tok_rows, features) * score_scale).astype(jnp.bfloat16)
    d_key = d_key_sum.astype(jnp.bfloat16)
    d_value = d_value_sum.astype(jnp.bfloat16)
    d_query_shift = jnp.sum(d_query.astype(jnp.float32), 0)
    d_value_shift = jnp.sum(d_value.astype(jnp.float32), 0)
    d_project_rows = jnp.concatenate([d_query, d_key, d_value], 1)
    d_project = jnp.einsum(
        "ti,to->io", normed_first, d_project_rows, preferred_element_type=jnp.float32
    )
    d_normed_first = jnp.einsum(
        "to,io->ti", d_project_rows, project_back, preferred_element_type=jnp.float32
    )
    unused_first, first_back = jax.vjp(
        norm_rows, embedded, first_gain_back.astype(jnp.float32), first_shift.astype(jnp.float32)
    )
    d_embed_part, d_gain_first, d_shift_first = first_back(d_normed_first)
    d_embedded = d_middle + d_embed_part
    d_table = jnp.einsum("tl,td->ld", lead_pick, d_embedded, precision=lax.Precision.HIGHEST)
    shards = (
        lax.psum_scatter(d_table, ("band", "grp"), scatter_dimension=1, tiled=True),
        lax.psum_scatter(d_gain_first, ("band", "grp"), scatter_dimension=0, tiled=True),
        lax.psum_scatter(d_shift_first, ("band", "grp"), scatter_dimension=0, tiled=True),
        lax.psum_scatter(d_project, ("band", "grp"), scatter_dimension=0, tiled=True),
        lax.psum_scatter(d_query_shift, ("band", "grp"), scatter_dimension=0, tiled=True),
        lax.psum_scatter(d_value_shift, ("band", "grp"), scatter_dimension=0, tiled=True),
        lax.psum_scatter(d_out_full, ("band", "grp"), scatter_dimension=0, tiled=True),
        lax.psum_scatter(d_out_shift, ("band", "grp"), scatter_dimension=0, tiled=True),
        lax.psum_scatter(d_gain_second, ("band", "grp"), scatter_dimension=0, tiled=True),
        lax.psum_scatter(d_shift_second, ("band", "grp"), scatter_dimension=0, tiled=True),
        lax.psum_scatter(d_up, ("band", "grp"), scatter_dimension=0, tiled=True),
        lax.psum_scatter(d_up_shift, ("band", "grp"), scatter_dimension=0, tiled=True),
        lax.psum_scatter(d_down, ("band", "grp"), scatter_dimension=0, tiled=True),
        lax.psum_scatter(d_down_shift, ("band", "grp"), scatter_dimension=0, tiled=True),
    )
    return (layer_out, d_embedded[None]) + tuple(shards)


DEPTH = 4
PLANE = 4
BIG = 1e30
HBM = pltpu.MemorySpace.HBM
VMEM = pltpu.MemorySpace.VMEM
SMEM = pltpu.MemorySpace.SMEM
LEADS = 16
ROW_G1, ROW_B1, ROW_QB, ROW_VB, ROW_OB, ROW_G2, ROW_B2, ROW_DB = range(16, 24)
VEC_ROWS = 24


def mul(left, right, over_left, over_right):
    return lax.dot_general(
        left, right, (((over_left,), (over_right,)), ((), ())), preferred_element_type=jnp.float32
    )


class Mover:
    def __init__(self, sems):
        self.sems, self.used, self.open = sems, 0, []

    def start(self, source, target):
        copy = pltpu.make_async_copy(source, target, self.sems.at[self.used])
        self.used += 1
        copy.start()
        self.open.append(copy)
        return copy

    def wait(self, copies=None):
        for copy in list(self.open if copies is None else copies):
            copy.wait()
            self.open = [other for other in self.open if other is not copy]


class Far:
    def __init__(self, value):
        self.value = value


class Raw(Far):
    pass


class Given:
    def __init__(self, ref, held, mover):
        self.ref, self.mover, self.copy = held, mover, mover.start(ref, held)
        self.shape, self.dtype = ref.shape, ref.dtype

    def ready(self):
        if self.copy is not None:
            self.mover.wait([self.copy])
            self.copy = None
        return self.ref

    def __getitem__(self, at):
        return self.ready()[at]


def run(order, kernel, outs, ins, scratch=(), after=(), alias=None):
    after = list(after) + order
    kinds = [type(a) if isinstance(a, Far) else None for a in ins]
    ins = [a.value if kind else a for a, kind in zip(ins, kinds)]
    staged = [pltpu.VMEM(a.shape, a.dtype) for a, kind in zip(ins, kinds) if kind is Far]
    outs = [o if len(o) == 3 else o + ("",) for o in outs]
    staged += [pltpu.VMEM(o[0], o[1]) for o in outs if o[2] == "far"]
    n_in, n_after, n_out, n_staged = len(ins), len(after), len(outs), len(staged)
    name = getattr(kernel, "func", kernel).__name__
    micros, room = COSTS[name]
    cost = pl.CostEstimate(flops=micros * 1_100_000_000, bytes_accessed=micros * 3_600_000, transcendentals=0)

    def body(*refs):
        mover = Mover(refs[-1])
        held = list(refs[len(refs) - 1 - n_staged : -1])
        given = [
            Given(ref, held.pop(0), mover) if kind is Far else ref for ref, kind in zip(refs[:n_in], kinds)
        ]
        refs = refs[n_in + n_after : len(refs) - 1 - n_staged]
        made = [held.pop(0) if o[2] == "far" else ref for ref, o in zip(refs, outs)]
        kernel(mover, *given, *made, *refs[n_out + 1 :])
        for ref, written, o in zip(refs, made, outs):
            if o[2] == "far":
                mover.start(written, ref)
        for operand in given:
            if isinstance(operand, Given):
                operand.ready()
        refs[n_out][...] = jnp.zeros_like(refs[n_out])
        mover.wait()

    spaces = [pl.ANY if kind else SMEM if a.dtype == jnp.int32 and a.ndim == 1 else VMEM for a, kind in zip(ins, kinds)]
    results = pl.pallas_call(
        body,
        name=name,
        out_shape=[HBM(o[0], o[1]) if o[2] else jax.ShapeDtypeStruct(o[0], o[1]) for o in outs]
        + [jax.ShapeDtypeStruct((8, 128), f32)],
        in_specs=[pl.BlockSpec(memory_space=space) for space in spaces + [pl.ANY] * n_after],
        out_specs=[pl.BlockSpec(memory_space=pl.ANY if o[2] else VMEM) for o in outs] + [pl.BlockSpec(memory_space=VMEM)],
        scratch_shapes=[pltpu.VMEM(s, d) for s, d in scratch] + staged + [pltpu.SemaphoreType.DMA((64,))],
        compiler_params=pltpu.CompilerParams(vmem_limit_bytes=room << 20),
        cost_estimate=cost,
        input_output_aliases=dict([alias] if alias else []),
    )(
        *[pltpu.with_memory_space_constraint(a, HBM) if kind else a for a, kind in zip(ins, kinds)],
        *[pltpu.with_memory_space_constraint(a, HBM) if a.size > 4096 else a for a in after],
    )
    order[:] = results[n_out:]
    return results[:n_out]


def row_stats(values):
    mean = jnp.mean(values, -1, keepdims=True)
    centred = values - mean
    inv = lax.rsqrt(jnp.mean(centred * centred, -1, keepdims=True) + epsilon)
    return centred * inv, inv


def norm_back(d_normal, normal, inv):
    first = jnp.mean(d_normal, -1, keepdims=True)
    second = jnp.mean(d_normal * normal, -1, keepdims=True)
    return inv * (d_normal - first - normal * second)


def lead_hot(lead, seg_row):
    seg = seg_row[...]
    found = jnp.zeros_like(seg)
    for slot in range(lead.shape[0]):
        found = jnp.where(seg == slot, lead[slot], found)
    slots = lax.broadcasted_iota(jnp.int32, (LEADS, seg.shape[1]), 0)
    return jnp.where(slots == found, 1.0, 0.0).astype(bf16)


def vec_row(vec, row):
    return vec[row : row + 1, :].astype(f32)


def q_prep_kernel(mover, pos, qkv, table, g1, b1, qb, vb, ob, g2, b2, db, ub, up, out_rows, down, o0, o1, o2, o3, cols, first):
    outs = (o0, o1, o2, o3)
    z = pos[0]
    rw = qkv.shape[0]
    d = qkv.shape[1] // 3
    width = d // DEPTH
    side = outs[0].shape[1] - 3 * width

    def wide(values):
        values = values.astype(f32)
        return jnp.concatenate([values, jnp.zeros((values.shape[0], side - values.shape[1]), f32)], 1)

    rows = [wide(table[...])] + [wide(v[...].reshape(1, -1)) for v in (g1, b1, qb, vb, ob, g2, b2, db)]
    rows += [ub[...].reshape(1, -1).astype(f32), jnp.zeros((rw - VEC_ROWS - 1, side), f32)]
    small = jnp.concatenate(rows, 0).astype(bf16)
    for u, out in enumerate(outs):
        for part in range(3):
            start = pl.multiple_of(part * d + (z ^ u) * width, width)
            out[:, part * width : (part + 1) * width] = qkv[:, pl.ds(start, width)]
        out[:, 3 * width :] = small
    fr = up.shape[1] // (DEPTH * PLANE * 2)
    for k in range(PLANE):
        for c in range(2):
            for zz in range(DEPTH):
                src = ((zz * PLANE + k) * 2 + c) * fr
                dst = (c * DEPTH + zz) * fr
                cols[k, :, dst : dst + fr] = up[:, src : src + fr]
    first[0] = out_rows[...]
    first[1] = down[0:rw, :]


def q_stack_kernel(mover, pos, b0, b1, b2, b3, out):
    for u, block in enumerate((b0, b1, b2, b3)):
        mover.start(block, out.at[pos[0] ^ u])


def shard_kernel(mover, ups, down, out):
    out[0:PLANE] = ups[...]
    out[PLANE:] = down[out.shape[1] :, :].reshape(PLANE - 1, -1, down.shape[1])


def qkv_kernel(mover, pos, lead, seg_row, toks, *refs):
    z, yx, c = pos[0], pos[1], pos[2]
    qa, qc, (n1, w_out, vec, up_b, o0, o1, o2, o3, w, proj) = refs[:4], refs[4:8], refs[8:]
    rows, d = toks.shape[1:]
    width = d // DEPTH
    head = width // PLANE
    rw = w.shape[3]
    fr = w.shape[4] - 3 * width
    pending = [mover.start(qa[k], w.at[:, yx ^ k, c]) for k in range(PLANE)]
    pending += [mover.start(qc[k], w.at[:, yx ^ k, 1 - c]) for k in range(PLANE)]
    mover.wait(pending)
    mover.start(w.at[:, :, :, :, 0 : 3 * width], w_out)
    for zz in range(DEPTH):
        for k in range(PLANE):
            for core in range(2):
                i = (zz * PLANE + k) * 2 + core
                side = w[zz, k, core, :, 3 * width :].astype(f32)
                vec[:, i * rw : (i + 1) * rw] = side[0:VEC_ROWS, 0:rw]
        for core in range(2):
            side = w[zz, yx, core, :, 3 * width :].astype(f32)
            start = (core * DEPTH + zz) * fr
            up_b[:, start : start + fr] = side[VEC_ROWS : VEC_ROWS + 1, :]
    shift = mul(lead_hot(lead, seg_row), vec[0:LEADS, :].astype(bf16), 0, 0)
    gain, bias = vec_row(vec, ROW_G1), vec_row(vec, ROW_B1)
    for s in range(DEPTH):
        normal, _ = row_stats(toks[z ^ s].astype(f32) + shift)
        n1[s * rows : (s + 1) * rows, :] = (normal * gain + bias).astype(bf16)
    at = pl.ds(pl.multiple_of(z * width, width), width)
    biases = jnp.concatenate(
        [vec[ROW_QB : ROW_QB + 1, at], jnp.zeros((1, width), f32), vec[ROW_VB : ROW_VB + 1, at]], 1
    )
    first = lax.broadcasted_iota(jnp.int32, (8, 3 * width), 0) == 0
    biases = jnp.where(first, biases, 0.0).astype(bf16)
    ones = jnp.ones((8, DEPTH * rows), bf16)
    weight = w[:, :, :, :, 0 : 3 * width].reshape(d, 3 * width)
    found = mul(weight, n1[...], 0, 1) + mul(biases, ones, 0, 0)
    proj[...] = found.astype(bf16).reshape(proj.shape)
    for k, out in enumerate((o0, o1, o2, o3)):
        for part in range(3):
            mover.start(proj.at[part * PLANE + (yx ^ k)], out.at[part * head : (part + 1) * head])


def fill_heads(seg_row, count, blocks, qa, ka, vt):
    head = blocks[0].shape[0] // 3
    span = blocks[0].shape[1]
    seg = jnp.concatenate([seg_row[...]] * (span // seg_row.shape[1]), 1)
    slots = lax.broadcasted_iota(jnp.int32, (16, span), 0)
    hot, real = jnp.where(slots == seg, 1.0, 0.0), slots < count
    q_mark = jnp.where(real, (hot - 1.0) * BIG, 0.0).astype(bf16)
    k_mark = jnp.where(real, hot, 0.0).astype(bf16)
    rest = qa.shape[0] - head - 16
    for k, block in enumerate(blocks):
        cols = slice(k * span, (k + 1) * span)
        qa[0:head, cols] = block[0:head, :] * jnp.asarray(score_scale, bf16)
        qa[head : head + 16, cols] = q_mark
        qa[head + 16 :, cols] = jnp.zeros((rest, span), bf16)
        keys = jnp.concatenate([block[head : 2 * head, :], k_mark, jnp.zeros((rest, span), bf16)], 0)
        ka[cols, :] = keys.T
        vt[:, cols] = block[2 * head :, :]


def attend_kernel(count, mover, seg_row, b0, b1, b2, b3, o0, o1, o2, o3, lse, qa, ka, vt):
    fill_heads(seg_row, count, (b0, b1, b2, b3), qa, ka, vt)
    span = b0.shape[1]
    rows = seg_row.shape[1]
    outs = (o0, o1, o2, o3)

    def step(k, carry):
        for half in range(DEPTH // 2):
            at = pl.ds(pl.multiple_of(k * span + half * 2 * rows, 2 * rows), 2 * rows)
            scores = mul(ka[...], qa[:, at], 1, 0)
            top = jnp.max(scores, 0, keepdims=True)
            soft = jnp.exp(scores - top)
            total = jnp.sum(soft, 0, keepdims=True)
            found = mul(vt[...], soft.astype(bf16), 1, 0) / total
            lse[:, at] = jnp.broadcast_to(top + jnp.log(total), (8, 2 * rows))
            for i in range(2):
                outs[half * 2 + i][:, pl.ds(pl.multiple_of(k * rows, rows), rows)] = found[
                    :, i * rows : (i + 1) * rows
                ].astype(bf16)
        return carry

    lax.fori_loop(0, PLANE, step, 0)


def out_kernel(mover, pos, a0, a1, a2, a3, first, p0, p1, p2, p3, att, w_out):
    z = pos[0]
    head = a0.shape[0]
    rows, d = p0.shape
    pending = [mover.start(first.at[:, :, 0], w_out)]
    for u, block in enumerate((a0, a1, a2, a3)):
        att[pl.ds(pl.multiple_of((z ^ u) * head, head), head), :] = block[...]
    mover.wait(pending)
    found = mul(att[...], w_out[...].reshape(-1, d), 0, 0)
    for j, out in enumerate((p0, p1, p2, p3)):
        out[...] = found[j * rows : (j + 1) * rows, :].astype(out.dtype)


def norm_kernel(mover, lead, seg_row, vec, tok, p0, p1, p2, p3, middle, n2):
    shift = mul(lead_hot(lead, seg_row), vec[0:LEADS, :].astype(bf16), 0, 0) + vec_row(vec, ROW_OB)
    total = p0[...].astype(f32) + p1[...].astype(f32) + p2[...].astype(f32) + p3[...].astype(f32)
    total = tok[...].astype(f32) + shift + total
    middle[...] = total
    normal, _ = row_stats(total)
    n2[...] = (normal * vec_row(vec, ROW_G2) + vec_row(vec, ROW_B2)).astype(bf16)


def down_copies(mover, first, ff, w_down):
    copies = [mover.start(first.at[:, c, 1], w_down.at[c, :, 0]) for c in range(2)]
    return copies + [mover.start(ff.at[:, c, PLANE:], w_down.at[c, :, 1:]) for c in range(2)]


def ffn_kernel(mover, pos, up_b, n0, n1, n2, n3, d_outs, first, ff, act, d_hid, p0, p1, p2, p3, d_up_b, w_up, w_down, hid):
    yx = pos[1]
    rows, d = n0.shape
    for_up = [mover.start(ff.at[:, c, 0:PLANE], w_up.at[:, :, c]) for c in range(2)]
    for_down = down_copies(mover, first, ff, w_down)
    mover.wait(for_up)
    normed = jnp.concatenate([n0[...], n1[...], n2[...], n3[...]], 0)
    up = w_up[...].reshape(d, -1)
    hid[...] = mul(normed, up, 1, 0) + up_b[...].astype(f32)
    mover.wait(for_down)
    down = w_down[...].reshape(-1, d)
    sums = jnp.zeros(d_up_b.shape, f32)
    for j in range(PLANE):
        here = slice(j * rows, (j + 1) * rows)
        hidden = hid[here, :]
        phi = 0.5 * (1.0 + lax.erf(hidden * 0.7071067811865476))
        act[here, :] = (hidden * phi).astype(bf16)
        slope = phi + hidden * (jnp.exp(-0.5 * hidden * hidden) * 0.3989422804014327)
        d_act = mul(d_outs[yx ^ j], down, 1, 1)
        low = (d_act * slope).astype(bf16)
        d_hid[here, :] = low
        sums = sums + jnp.sum(low.astype(f32), 0, keepdims=True)
    d_up_b[...] = sums
    back = mul(d_hid[...], up, 1, 1)
    for j, out in enumerate((p0, p1, p2, p3)):
        out[...] = back[j * rows : (j + 1) * rows, :].astype(out.dtype)


def ffn_grad_kernel(mover, pos, act, d_hid, n0, n1, n2, n3, first, ff, d_outs, grads, outs, up_grad, down_grad, w_down):
    yx = pos[1]
    rows, d = outs.shape[1:]
    pending = down_copies(mover, first, ff, w_down)
    normed = jnp.concatenate([n0[...], n1[...], n2[...], n3[...]], 0)
    up_grad[...] = mul(normed, d_hid[...], 0, 0).astype(bf16).reshape(up_grad.shape)
    for c in range(2):
        mover.start(up_grad.at[:, :, c], grads.at[:, c, 0:PLANE])
    d_down = jnp.zeros((act.shape[1], d), f32)
    for j in range(PLANE):
        d_down = d_down + mul(act[j * rows : (j + 1) * rows, :], d_outs[yx ^ j], 0, 0)
    down_grad[...] = d_down.astype(bf16).reshape(down_grad.shape)
    for c in range(2):
        mover.start(down_grad.at[c], grads.at[:, c, PLANE : 2 * PLANE])
    mover.wait(pending)
    found = mul(act[...], w_down[...].reshape(-1, d), 1, 0)
    for j in range(PLANE):
        outs[yx ^ j] = found[j * rows : (j + 1) * rows, :].astype(bf16)


def ffn_last_kernel(mover, shard, ups, down, out_rows):
    ups[...] = shard[0:PLANE]
    down[...] = shard[PLANE : 2 * PLANE].astype(f32).reshape(down.shape)
    out_rows[...] = shard[2 * PLANE].astype(f32)


def branch_kernel(mover, vec, middle, d_out, p0, p1, p2, p3, d_mid, d_branch, d_vec):
    dy = p0[...].astype(f32) + p1[...].astype(f32) + p2[...].astype(f32) + p3[...].astype(f32)
    normal, inv = row_stats(middle[...])
    d_rows = d_out[...].astype(f32)
    total = d_rows + norm_back(dy * vec_row(vec, ROW_G2), normal, inv)
    d_mid[...] = total
    low = total.astype(bf16)
    d_branch[...] = low
    sums = [jnp.sum(v, 0, keepdims=True) for v in (dy * normal, dy, d_rows, low.astype(f32))]
    d_vec[...] = jnp.concatenate(sums + [jnp.zeros((4, dy.shape[1]), f32)], 0)


def out_back_kernel(mover, pos, att, w_out, b0, b1, b2, b3, others, o0, o1, o2, o3, grads, d_att, grad):
    z = pos[0]
    head = o0.shape[0]
    branch = jnp.concatenate([b0[...], b1[...], b2[...], b3[...]], 0)
    d = branch.shape[1]
    d_att[...] = mul(w_out[...].reshape(-1, d), branch, 1, 1).astype(bf16).reshape(d_att.shape)
    for u, out in enumerate((o0, o1, o2, o3)):
        out[...] = d_att[z ^ u]
    grad[...] = mul(att[...], branch, 1, 0).astype(bf16).reshape(grad.shape)
    mover.start(grad, grads.at[:, :, 2 * PLANE])


def attend_back_kernel(count, mover, seg_row, b0, b1, b2, b3, c0, c1, c2, c3, lse,
                       o0, o1, o2, o3, qa, ka, vt, vn, dot, dq, dk, dv, kt):
    fill_heads(seg_row, count, (b0, b1, b2, b3), qa, ka, vt)
    span = b0.shape[1]
    rows = seg_row.shape[1]
    head = vt.shape[0]
    for k, block in enumerate((b0, b1, b2, b3)):
        cols = slice(k * span, (k + 1) * span)
        vn[cols, :] = vt[:, cols].T
        kt[:, cols] = block[head : 2 * head, :]
        for s, block in enumerate((c0, c1, c2, c3)):
            dot[:, k * span + s * rows : k * span + (s + 1) * rows] = block[:, k * rows : (k + 1) * rows]
    dk[...] = jnp.zeros_like(dk)
    dv[...] = jnp.zeros_like(dv)
    logs = lse

    def step(i, carry):
        for k in (2 * i, 2 * i + 1):
            at = pl.ds(pl.multiple_of(k * span, span), span)
            scores = mul(ka[...], qa[:, at], 1, 0)
            soft = jnp.exp(scores - logs[0:1, at])
            d_out = dot[:, at]
            d_soft = mul(vn[...], d_out, 1, 0)
            delta = jnp.sum(soft * d_soft, 0, keepdims=True)
            d_scores = (soft * (d_soft - delta)).astype(bf16)
            dv[...] += mul(d_out, soft.astype(bf16), 1, 1)
            dk[...] += mul(qa[0:head, at], d_scores, 1, 1)
            dq[:, at] = (mul(kt[...], d_scores, 1, 0) * score_scale).astype(bf16)
        return carry

    lax.fori_loop(0, PLANE // 2, step, 0)
    for k, out in enumerate((o0, o1, o2, o3)):
        cols = slice(k * span, (k + 1) * span)
        out[0:head, :] = dq[:, cols]
        out[head : 2 * head, :] = dk[:, cols].astype(bf16)
        out[2 * head :, :] = dv[:, cols].astype(bf16)


def join_heads(yx, blocks, joined):
    head = blocks[0].shape[0] // 3
    for k, block in enumerate(blocks):
        for part in range(3):
            joined[part * PLANE + (yx ^ k)] = block[part * head : (part + 1) * head, :]
    return joined[...].reshape(3 * PLANE * head, -1)


def qkv_back_kernel(mover, pos, lead, seg_row, vec, toks, n1, w, g0, g1, g2, g3, d_mid, d_mid_vec, d_up_b,
                    r0, r1, r2, r3, mine, o0, o1, joined, d_vec, both):
    z, yx, core = pos[0], pos[1], pos[2]
    rows, d = r0.shape
    width = d // DEPTH
    head = width // PLANE
    rw = mine.shape[2]
    cols = 3 * width
    fr = mine.shape[3] - cols
    for k, block in enumerate((g0, g1, g2, g3)):
        for part in range(3):
            joined[part * PLANE + (yx ^ k)] = block[part * head : (part + 1) * head, :]
    grads = joined[...].reshape(cols, DEPTH * rows)
    grad = mul(n1[...], grads, 0, 1).astype(bf16)
    back = mul(grads, w[...].reshape(d, cols), 0, 1)
    hot = lead_hot(lead, seg_row)
    shift = mul(hot, vec[0:LEADS, :].astype(bf16), 0, 0)
    gain = vec_row(vec, ROW_G1)
    d_gain = jnp.zeros((1, d), f32)
    d_bias = jnp.zeros((1, d), f32)
    d_emb = d_mid[...]
    for s, out in enumerate((r0, r1, r2, r3)):
        piece = back[s * rows : (s + 1) * rows, :]
        out[...] = piece.astype(out.dtype)
        normal, inv = row_stats(toks[z ^ s].astype(f32) + shift)
        d_gain = d_gain + jnp.sum(piece * normal, 0, keepdims=True)
        d_bias = d_bias + jnp.sum(piece, 0, keepdims=True)
        d_emb = d_emb + norm_back(piece * gain, normal, inv)
    high = d_emb.astype(bf16)
    low = (d_emb - high.astype(f32)).astype(bf16)
    d_vec[...] = jnp.zeros_like(d_vec)
    d_vec[0:LEADS, :] = mul(hot, high, 1, 0) + mul(hot, low, 1, 0)
    sums = mul(jnp.ones((8, DEPTH * rows), bf16), grads, 1, 1)
    d_vec[ROW_G1 : ROW_G1 + 1, :] = d_gain
    d_vec[ROW_B1 : ROW_B1 + 1, :] = d_bias
    at = pl.ds(pl.multiple_of(z * width, width), width)
    d_vec[ROW_QB : ROW_QB + 1, at] = sums[0:1, 0:width]
    d_vec[ROW_VB : ROW_VB + 1, at] = sums[0:1, 2 * width :]
    for i, row in enumerate((ROW_G2, ROW_B2, ROW_DB, ROW_OB)):
        d_vec[row : row + 1, :] = d_mid_vec[i : i + 1, :]
    small = d_vec[...]
    mark = lax.broadcasted_iota(jnp.int32, (rw, fr), 0) == VEC_ROWS
    for zz in range(DEPTH):
        for k in range(PLANE):
            for c in range(2):
                i = (zz * PLANE + k) * 2 + c
                side = jnp.concatenate([small[:, i * rw : (i + 1) * rw], jnp.zeros((rw, fr - rw), f32)], 1)
                start = (c * DEPTH + zz) * fr
                last = jnp.where(yx == k, d_up_b[:, start : start + fr], 0.0)
                side = jnp.where(mark, last, side).astype(bf16)
                both[zz, k, c] = jnp.concatenate([grad[i * rw : (i + 1) * rw, :], side], 1)
    mover.start(both.at[0:2, :, 1 - core], o0)
    mover.start(both.at[2:4, :, 1 - core], o1)
    mover.start(both.at[:, :, core], mine)


def first_back_kernel(mover, lead, seg_row, vec, tok, d_mid, r0, r1, r2, r3, out):
    shift = mul(lead_hot(lead, seg_row), vec[0:LEADS, :].astype(bf16), 0, 0)
    normal, inv = row_stats(tok[...].astype(f32) + shift)
    dy = r0[...].astype(f32) + r1[...].astype(f32) + r2[...].astype(f32) + r3[...].astype(f32)
    out[...] = d_mid[...] + norm_back(dy * vec_row(vec, ROW_G1), normal, inv)


def layer_out_kernel(mover, vec, middle, blocks, out):
    total = middle[...] + vec_row(vec, ROW_DB)
    for k in range(PLANE):
        total = total + blocks[k].astype(f32)
    out[...] = total.astype(bf16)


def pair_kernel(mover, pos, mine, o0, o1, p0, p1, p2, p3, total):
    yx = pos[1]
    total[0:2] = (mine[0:2].astype(f32) + o0[...].astype(f32)).astype(bf16)
    total[2:4] = (mine[2:4].astype(f32) + o1[...].astype(f32)).astype(bf16)
    for k, out in enumerate((p0, p1, p2, p3)):
        mover.start(total.at[:, yx ^ k], out)


def quad_kernel(mover, pos, b0, b1, b2, b3, o0, o1, o2, o3, total):
    found = b0[...].astype(f32) + b1[...].astype(f32) + b2[...].astype(f32) + b3[...].astype(f32)
    total[...] = found.astype(bf16)
    for u, out in enumerate((o0, o1, o2, o3)):
        out[...] = total[pos[0] ^ u]


def qkv_join_kernel(mover, pos, b0, b1, b2, b3, out, table, *rest):
    z = pos[0]
    rw = out.shape[0]
    width = out.shape[1] // (3 * DEPTH)
    side = jnp.zeros((rw, b0.shape[1] - 3 * width), f32)
    for s, block in enumerate((b0, b1, b2, b3)):
        for part in range(3):
            start = pl.multiple_of((part * DEPTH + (z ^ s)) * width, width)
            out[:, pl.ds(start, width)] = block[:, part * width : (part + 1) * width].astype(f32)
        side = side + block[:, 3 * width :].astype(f32)
    table[...] = side[0:LEADS, 0:rw]
    for i, row in enumerate(rest[:-1]):
        row[...] = side[LEADS + i : LEADS + i + 1, 0:rw].reshape(rw)
    rest[-1][...] = side[VEC_ROWS : VEC_ROWS + 1, :].reshape(-1)


def up_join_kernel(mover, blocks, out):
    fr = blocks.shape[2] // (2 * DEPTH)
    for k in range(PLANE):
        for c in range(2):
            for zz in range(DEPTH):
                src = (c * DEPTH + zz) * fr
                dst = ((zz * PLANE + k) * 2 + c) * fr
                out[:, dst : dst + fr] = blocks[k, :, src : src + fr].astype(f32)


COSTS = {
    "q_prep_kernel": (3, 6), "q_stack_kernel": (1, 4), "up_prep_kernel": (1, 4), "shard_kernel": (1, 4), "first_shard_kernel": (1, 4), "qkv_kernel": (5, 20),
    "attend_kernel": (9, 24), "out_kernel": (2, 12), "norm_kernel": (2, 8), "ffn_kernel": (8, 32), "ffn_grad_kernel": (8, 32),
    "branch_kernel": (2, 12), "out_back_kernel": (3, 12), "attend_back_kernel": (15, 32),
    "qkv_back_kernel": (10, 28), "first_back_kernel": (2, 8), "layer_out_kernel": (1, 8),
    "pair_kernel": (2, 8), "quad_kernel": (1, 8), "qkv_join_kernel": (1, 4), "up_join_kernel": (2, 8), "ffn_last_kernel": (1, 8),
}
PLANE_AXES = ("y", "x")


def trade(blocks, axes):
    return lax.all_to_all(blocks, axes, split_axis=0, concat_axis=0, tiled=True)


ALL = ("z", "y", "x", "g")


def across(blocks):
    swap = [(0, 1), (1, 0)]
    return (
        blocks[0],
        lax.ppermute(blocks[1], "x", swap),
        lax.ppermute(blocks[2], "y", swap),
        lax.ppermute(blocks[3], ("y", "x"), [(i, i ^ 3) for i in range(PLANE)]),
    )


def to_depth(block, step):
    return lax.ppermute(block, "z", [(i, i ^ step) for i in range(DEPTH)])


def along(blocks):
    return (blocks[0],) + tuple(to_depth(blocks[u], u) for u in range(1, DEPTH))


def core_swap(block):
    return lax.ppermute(block, "g", [(0, 1), (1, 0)])


def far(blocks):
    return [Far(block) for block in blocks]


def raw(blocks):
    return [Raw(block) for block in blocks]


def fast_local(
    tokens, segment_ids, lead_index, lead_table, ln1_gain, ln1_bias, qkv_weight, q_bias, v_bias,
    out_weight, out_bias, ln2_gain, ln2_bias, up_weight, up_bias, down_weight, down_bias, d_out,
):
    z = lax.axis_index("z")
    yx = lax.axis_index("y") * 2 + lax.axis_index("x")
    c = lax.axis_index("g")
    pos = jnp.stack([z, yx, c]).astype(jnp.int32)
    tok, d_rows = tokens[0], d_out[0]
    rows, d = tok.shape
    head = d // HEADS
    span = DEPTH * rows
    group = PLANE * span
    rw = qkv_weight.shape[0]
    fr = down_weight.shape[0]
    ff = 2 * DEPTH * fr
    lead = lead_index[0]
    count = lead.shape[0]
    width = 3 * d // DEPTH
    seg_row = segment_ids
    up_shape, down_shape = (DEPTH, PLANE, 2, rw, ff), (2, DEPTH, PLANE, rw, d)

    order = []
    call = functools.partial(run, order)
    side = width + -(-max(rw, fr) // 128) * 128

    *q_rows, up_cols, first_shard = call(
        q_prep_kernel,
        [((rw, side), bf16)] * 4 + [((PLANE, rw, ff), bf16), ((2, rw, d), bf16, "far")],
        [pos]
        + far((qkv_weight, lead_table, ln1_gain, ln1_bias, q_bias, v_bias, out_bias, ln2_gain, ln2_bias, down_bias, up_bias))
        + far((up_weight, out_weight, down_weight)),
    )
    q_rows = along(q_rows)
    toks = lax.all_gather(tok, "z", axis=0)
    first = lax.all_gather(first_shard, ("z", "g"), axis=0).reshape(DEPTH, 2, 2, rw, d)
    up_cols = trade(up_cols, PLANE_AXES)
    (q_stack,) = call(q_stack_kernel, [((DEPTH, rw, side), bf16)], [pos, *q_rows], after=[up_cols])
    q_plane = across((q_stack,) * PLANE)
    q_other = [core_swap(block) for block in q_plane]
    n1, w_qkv, vec, up_b, *blocks = call(
        qkv_kernel,
        [((span, d), bf16, "far"), ((DEPTH, PLANE, 2, rw, width), bf16, "raw"), ((VEC_ROWS, d), f32), ((1, ff), f32)]
        + [((3 * head, span), bf16)] * 4,
        [pos, lead, seg_row, Far(toks), *q_plane, *q_other],
        [((DEPTH, PLANE, 2, rw, side), bf16), ((3 * PLANE, head, span), bf16)],
    )
    (ff_shard,) = call(shard_kernel, [((2 * PLANE - 1, rw, d), bf16, "far")], [up_cols, down_weight])
    ff_all = lax.all_gather(ff_shard, ("z", "g"), axis=0).reshape(DEPTH, 2, 2 * PLANE - 1, rw, d)
    blocks = across(blocks)

    d_outs = trade(jnp.broadcast_to(d_rows[None], (PLANE, rows, d)), PLANE_AXES)
    *att_parts, lse = call(
        functools.partial(attend_kernel, count),
        [((head, PLANE * rows), bf16)] * 4 + [((8, group), f32)],
        [seg_row, *blocks],
        [((128, group), bf16), ((group, 128), bf16), ((head, group), bf16)],
    )
    att_parts = along(att_parts)
    *parts, att, w_out = call(
        out_kernel,
        [((rows, d), f32)] + [((rows, d), bf16)] * 3 + [((DEPTH * head, span), bf16), ((DEPTH, 2, rw, d), bf16)],
        [pos, *att_parts, Raw(first)],
        after=[d_outs],
    )
    parts = across(parts)
    middle, n2 = call(norm_kernel, [((rows, d), f32, "far"), ((rows, d), bf16)], [lead, seg_row, vec, Far(tok), *parts])
    n2_plane = across((n2,) * PLANE)

    act, d_hid, p0, p1, p2, p3, d_up_b = call(
        ffn_kernel,
        [((span, ff), bf16), ((span, ff), bf16), ((rows, d), f32)] + [((rows, d), bf16)] * 3 + [((1, ff), f32)],
        [pos, up_b, *n2_plane, Far(d_outs), Raw(first), Raw(ff_all)],
        [(up_shape, bf16), (down_shape, bf16), ((span, ff), f32)],
    )
    parts = across((p0, p1, p2, p3))
    ff_grad, outs = call(
        ffn_grad_kernel,
        [((DEPTH, 2, 2 * PLANE + 1, rw, d), bf16, "raw"), ((PLANE, rows, d), bf16, "far")],
        [pos, act, d_hid, *n2_plane, Raw(first), Raw(ff_all), Far(d_outs)],
        [(up_shape, bf16), (down_shape, bf16), (down_shape, bf16)],
    )
    d_mid, d_branch, d_mid_vec = call(
        branch_kernel,
        [((rows, d), f32, "far"), ((rows, d), bf16), ((8, d), f32)],
        [vec, Far(middle), Far(d_rows), *parts],
    )
    branch_plane = across((d_branch,) * PLANE)
    *d_att, ff_grad = call(
        out_back_kernel,
        [((head, span), bf16)] * 4 + [(ff_grad.shape, bf16, "raw")],
        [pos, att, w_out, *branch_plane, Raw(ff_grad)],
        [((DEPTH, head, span), bf16), ((DEPTH, 2, rw, d), bf16)],
        alias=(7, 4),
    )
    d_att = along(d_att)
    ff_grad = lax.psum_scatter(
        ff_grad.reshape(2 * DEPTH, 2 * PLANE + 1, rw, d), ("z", "g"), scatter_dimension=0, tiled=True
    )[0]
    outs = trade(outs, PLANE_AXES)

    d_blocks = call(
        functools.partial(attend_back_kernel, count),
        [((3 * head, span), bf16)] * 4,
        [seg_row, *blocks, *d_att, lse],
        [((128, group), bf16), ((group, 128), bf16), ((head, group), bf16), ((group, head), bf16),
         ((head, group), bf16), ((head, group), bf16), ((head, group), f32), ((head, group), f32), ((head, group), bf16)],
    )
    d_blocks = across(d_blocks)
    (layer_out,) = call(layer_out_kernel, [((rows, d), bf16)], [vec, Far(middle), outs])
    r0, r1, r2, r3, mine, o0, o1 = call(
        qkv_back_kernel,
        [((rows, d), f32)] + [((rows, d), bf16)] * 3
        + [((DEPTH, PLANE, rw, side), bf16)] + [((DEPTH // 2, PLANE, rw, side), bf16)] * 2,
        [pos, lead, seg_row, vec, Far(toks), Far(n1), Far(w_qkv), *d_blocks, Far(d_mid), d_mid_vec, d_up_b],
        [((3 * PLANE, head, span), bf16), ((rw, d), f32), ((DEPTH, PLANE, 2, rw, side), bf16)],
    )
    returned = along((r0, r1, r2, r3))
    quads = across(
        call(
            pair_kernel,
            [((DEPTH, rw, side), bf16)] * 4,
            [pos, mine, core_swap(o0), core_swap(o1)],
            [((DEPTH, PLANE, rw, side), bf16)],
        )
    )
    cols = along(call(quad_kernel, [((rw, side), bf16)] * 4, [pos, *quads], [((DEPTH, rw, side), bf16)]))
    ups, d_down, d_out_weight = call(
        ffn_last_kernel, [((PLANE, rw, ff), bf16), ((fr, d), f32), ((rw, d), f32)], [ff_grad]
    )
    ups = trade(ups, PLANE_AXES)
    (d_tokens,) = call(
        first_back_kernel, [((rows, d), f32)], [lead, seg_row, vec, Far(tok), Far(d_mid), *returned]
    )
    d_qkv, table, d_g1, d_b1, d_qb, d_vb, d_ob, d_g2, d_b2, d_db, d_ub = call(
        qkv_join_kernel,
        [((rw, 3 * d), f32), ((LEADS, rw), f32)] + [((rw,), f32)] * 8 + [((fr,), f32)],
        [pos, *cols],
    )
    (d_up,) = call(up_join_kernel, [((rw, PLANE * ff), f32)], [ups])
    return (
        layer_out[None], d_tokens[None], table, d_g1, d_b1, d_qkv, d_qb, d_vb, d_out_weight, d_ob,
        d_g2, d_b2, d_up, d_ub, d_down, d_db,
    )


def specs(band, grp):
    every = band + grp
    rows = P(grp, band, None)
    in_specs = (
        rows, P(grp, band), P(grp, None), P(None, every), P(every), P(every), P(every, None), P(every), P(every),
        P(every, None), P(every), P(every), P(every), P(every, None), P(every), P(every, None), P(every), rows,
    )
    out_specs = (
        rows, rows, P(None, every), P(every), P(every), P(every, None), P(every), P(every), P(every, None), P(every),
        P(every), P(every), P(every, None), P(every), P(every, None), P(every),
    )
    return in_specs, out_specs


def solution(mesh):
    band, grp = mesh.shape["band"], mesh.shape["grp"]
    if band == HEADS and grp == 2:
        mesh = Mesh(mesh.devices.reshape(DEPTH, 2, 2, grp), ("z", "y", "x", "g"))
        in_specs, out_specs = specs(("z", "y", "x"), ("g",))
        return jax.shard_map(fast_local, mesh=mesh, in_specs=in_specs, out_specs=out_specs, check_vma=False)
    in_specs, out_specs = specs(("band",), ("grp",))
    return jax.shard_map(local, mesh=mesh, in_specs=in_specs, out_specs=out_specs, check_vma=False)
```

```python
import functools
import math

import jax
import jax.numpy as jnp
from jax import lax
from jax.experimental import pallas as pl
from jax.experimental.pallas import tpu as pltpu
from jax.sharding import Mesh
from jax.sharding import PartitionSpec as P

bf16, f32 = jnp.bfloat16, jnp.float32

HEADS = 16


epsilon = 1e-05
score_scale = 0.125
masked_score = -1e30


def norm_rows(values, norm_gain, norm_bias):
    row_mean = jnp.mean(values, -1, keepdims=True)
    centred = values - row_mean
    row_var = jnp.mean(centred * centred, -1, keepdims=True)
    return centred * lax.rsqrt(row_var + epsilon) * norm_gain + norm_bias


def gelu_exact(values):
    return jax.nn.gelu(values, approximate=False)


def split_blocks(values, block_rows):
    return values.reshape((values.shape[0] // block_rows, block_rows) + values.shape[1:])


def block_scores(query_heads, key_heads, allowed):
    raw_scores = (
        jnp.einsum("qhd,khd->hqk", query_heads, key_heads, preferred_element_type=jnp.float32)
        * score_scale
    )
    return jnp.where(allowed[None], raw_scores, masked_score)


def softmax_rows(query_heads, key_heads, allowed, log_total):
    scores = block_scores(query_heads, key_heads, allowed)
    return jnp.where(allowed[None], jnp.exp(scores - log_total[:, :, None]), 0.0)


def score_grads(query_heads, key_heads, value_heads, d_heads, allowed, log_total, row_delta):
    soft_rows = softmax_rows(query_heads, key_heads, allowed, log_total)
    d_soft = jnp.einsum("qhd,khd->hqk", d_heads, value_heads, preferred_element_type=jnp.float32)
    d_scores = (soft_rows * (d_soft - row_delta[:, :, None])).astype(jnp.bfloat16)
    return (soft_rows.astype(jnp.bfloat16), d_scores)


def local(
    tokens,
    segment_ids,
    lead_index,
    lead_table,
    ln1_gain,
    ln1_bias,
    qkv_weight,
    q_bias,
    v_bias,
    out_weight,
    out_bias,
    ln2_gain,
    ln2_bias,
    up_weight,
    up_bias,
    down_weight,
    down_bias,
    d_out,
):
    (
        table_full,
        first_gain,
        first_shift,
        project_full,
        query_shift,
        value_shift,
        out_full,
        out_shift,
        second_gain,
        second_shift,
        up_full,
        up_shift,
        down_full,
        down_shift,
    ) = (
        lax.all_gather(lead_table, ("band", "grp"), axis=1, tiled=True),
        lax.all_gather(ln1_gain, ("band", "grp"), axis=0, tiled=True),
        lax.all_gather(ln1_bias, ("band", "grp"), axis=0, tiled=True),
        lax.all_gather(qkv_weight, ("band", "grp"), axis=0, tiled=True),
        lax.all_gather(q_bias, ("band", "grp"), axis=0, tiled=True),
        lax.all_gather(v_bias, ("band", "grp"), axis=0, tiled=True),
        lax.all_gather(out_weight, ("band", "grp"), axis=0, tiled=True),
        lax.all_gather(out_bias, ("band", "grp"), axis=0, tiled=True),
        lax.all_gather(ln2_gain, ("band", "grp"), axis=0, tiled=True),
        lax.all_gather(ln2_bias, ("band", "grp"), axis=0, tiled=True),
        lax.all_gather(up_weight, ("band", "grp"), axis=0, tiled=True),
        lax.all_gather(up_bias, ("band", "grp"), axis=0, tiled=True),
        lax.all_gather(down_weight, ("band", "grp"), axis=0, tiled=True),
        lax.all_gather(down_bias, ("band", "grp"), axis=0, tiled=True),
    )
    tok_rows = tokens.shape[1]
    features = tokens.shape[2]
    head_dim = features // HEADS
    band_count = lax.axis_size("band")
    group_rows = tok_rows * band_count
    block_rows = math.gcd(group_rows, 1024)
    own_segments = segment_ids[0]
    group_segments = jnp.tile(own_segments, band_count)
    sample_count = lead_index.shape[1]
    lead_count = lead_table.shape[0]
    sample_hot = (
        own_segments[:, None] == jnp.arange(sample_count, dtype=jnp.int32)[None, :]
    ).astype(jnp.float32)
    lead_hot = (lead_index[0][:, None] == jnp.arange(lead_count, dtype=jnp.int32)[None, :]).astype(
        jnp.float32
    )
    lead_pick = jnp.dot(sample_hot, lead_hot, precision=lax.Precision.HIGHEST)
    embedded = tokens[0].astype(jnp.float32) + jnp.dot(
        lead_pick.astype(jnp.bfloat16), table_full, preferred_element_type=jnp.float32
    )
    normed_first = norm_rows(
        embedded, first_gain.astype(jnp.float32), first_shift.astype(jnp.float32)
    ).astype(jnp.bfloat16)
    projected = jnp.dot(normed_first, project_full, preferred_element_type=jnp.float32)
    query_rows = (projected[:, :features] + query_shift.astype(jnp.float32)).astype(jnp.bfloat16)
    key_rows = projected[:, features : 2 * features].astype(jnp.bfloat16)
    value_rows = (projected[:, 2 * features :] + value_shift.astype(jnp.float32)).astype(
        jnp.bfloat16
    )
    key_all, value_all = (
        lax.all_gather(key_rows, "band", axis=0, tiled=True),
        lax.all_gather(value_rows, "band", axis=0, tiled=True),
    )
    query_heads = query_rows.reshape(tok_rows, HEADS, head_dim)
    key_blocks = split_blocks(key_all.reshape(group_rows, HEADS, head_dim), block_rows)
    value_blocks = split_blocks(value_all.reshape(group_rows, HEADS, head_dim), block_rows)
    segment_blocks = split_blocks(group_segments, block_rows)

    def stats_step(running, block_data):
        running_max, running_sum = running
        key_block, key_segments = block_data
        allowed = own_segments[:, None] == key_segments[None, :]
        scores = block_scores(query_heads, key_block, allowed)
        new_max = jnp.maximum(running_max, jnp.max(scores, -1))
        block_sum = jnp.sum(
            jnp.where(allowed[None], jnp.exp(scores - new_max[:, :, None]), 0.0), -1
        )
        return ((new_max, running_sum * jnp.exp(running_max - new_max) + block_sum), None)

    start_max = jnp.full((HEADS, tok_rows), masked_score, jnp.float32)
    start_sum = jnp.zeros((HEADS, tok_rows), jnp.float32)
    (final_max, final_sum), unused_out = lax.scan(
        stats_step, (start_max, start_sum), (key_blocks, segment_blocks)
    )
    log_total = final_max + jnp.log(final_sum)

    def output_step(running, block_data):
        high_part, low_part = running
        key_block, value_block, key_segments = block_data
        allowed = own_segments[:, None] == key_segments[None, :]
        soft_rows = softmax_rows(query_heads, key_block, allowed, log_total)
        soft_low = soft_rows.astype(jnp.bfloat16)
        soft_rest = (soft_rows - soft_low.astype(jnp.float32)).astype(jnp.bfloat16)
        high_part = high_part + jnp.einsum(
            "hqk,khd->qhd", soft_low, value_block, preferred_element_type=jnp.float32
        )
        low_part = low_part + jnp.einsum(
            "hqk,khd->qhd", soft_rest, value_block, preferred_element_type=jnp.float32
        )
        return ((high_part, low_part), None)

    empty_heads = jnp.zeros((tok_rows, HEADS, head_dim), jnp.float32)
    (attn_high, attn_low), unused_out = lax.scan(
        output_step, (empty_heads, empty_heads), (key_blocks, value_blocks, segment_blocks)
    )
    attended = attn_high.reshape(tok_rows, features).astype(jnp.bfloat16)
    middle = (
        embedded
        + jnp.dot(attended, out_full, preferred_element_type=jnp.float32)
        + out_shift.astype(jnp.float32)
    )
    normed_second = norm_rows(
        middle, second_gain.astype(jnp.float32), second_shift.astype(jnp.float32)
    ).astype(jnp.bfloat16)
    hidden = jnp.dot(normed_second, up_full, preferred_element_type=jnp.float32) + up_shift.astype(
        jnp.float32
    )
    activated = gelu_exact(hidden).astype(jnp.bfloat16)
    result = (
        middle
        + jnp.dot(activated, down_full, preferred_element_type=jnp.float32)
        + down_shift.astype(jnp.float32)
    )
    layer_out = result.astype(jnp.bfloat16)[None]
    first_gain_back, project_back, out_back, second_gain_back, up_back, down_back = (
        lax.all_gather(ln1_gain, ("band", "grp"), axis=0, tiled=True),
        lax.all_gather(qkv_weight, ("band", "grp"), axis=0, tiled=True),
        lax.all_gather(out_weight, ("band", "grp"), axis=0, tiled=True),
        lax.all_gather(ln2_gain, ("band", "grp"), axis=0, tiled=True),
        lax.all_gather(up_weight, ("band", "grp"), axis=0, tiled=True),
        lax.all_gather(down_weight, ("band", "grp"), axis=0, tiled=True),
    )
    d_rows = d_out[0]
    d_down_shift = jnp.sum(d_rows.astype(jnp.float32), 0)
    d_down = jnp.einsum("tf,td->fd", activated, d_rows, preferred_element_type=jnp.float32)
    d_act = jnp.einsum("td,fd->tf", d_rows, down_back, preferred_element_type=jnp.float32)
    unused_gelu, gelu_back = jax.vjp(gelu_exact, hidden)
    d_hidden = gelu_back(d_act)[0].astype(jnp.bfloat16)
    d_up_shift = jnp.sum(d_hidden.astype(jnp.float32), 0)
    d_up = jnp.einsum("td,tf->df", normed_second, d_hidden, preferred_element_type=jnp.float32)
    d_normed_second = jnp.einsum("tf,df->td", d_hidden, up_back, preferred_element_type=jnp.float32)
    unused_second, second_back = jax.vjp(
        norm_rows, middle, second_gain_back.astype(jnp.float32), second_shift.astype(jnp.float32)
    )
    d_middle_part, d_gain_second, d_shift_second = second_back(d_normed_second)
    d_middle = d_rows.astype(jnp.float32) + d_middle_part
    d_branch = d_middle.astype(jnp.bfloat16)
    d_out_shift = jnp.sum(d_branch.astype(jnp.float32), 0)
    d_out_full = jnp.einsum("ti,to->io", attended, d_branch, preferred_element_type=jnp.float32)
    d_attended = jnp.einsum(
        "to,io->ti", d_branch, out_back, preferred_element_type=jnp.float32
    ).astype(jnp.bfloat16)
    d_heads = d_attended.reshape(tok_rows, HEADS, head_dim)
    row_delta = jnp.sum(d_heads.astype(jnp.float32) * (attn_high + attn_low), -1).T

    def query_grad(d_query_acc, key_block, value_block, key_segments):
        allowed = own_segments[:, None] == key_segments[None, :]
        soft_low, d_scores = score_grads(
            query_heads, key_block, value_block, d_heads, allowed, log_total, row_delta
        )
        d_query_acc = d_query_acc + jnp.einsum(
            "hqk,khd->qhd", d_scores, key_block, preferred_element_type=jnp.float32
        )
        return (d_query_acc, soft_low, d_scores)

    def owner_step(d_query_acc, block_data):
        key_block, value_block, key_segments = block_data
        d_query_acc, soft_low, d_scores = query_grad(
            d_query_acc, key_block, value_block, key_segments
        )
        d_key_block = (
            jnp.einsum("hqk,qhd->khd", d_scores, query_heads, preferred_element_type=jnp.float32)
            * score_scale
        )
        d_value_block = jnp.einsum(
            "hqk,qhd->khd", soft_low, d_heads, preferred_element_type=jnp.float32
        )
        return (d_query_acc, (d_key_block, d_value_block))

    d_query_sum, (d_key_parts, d_value_parts) = lax.scan(
        owner_step, empty_heads, (key_blocks, value_blocks, segment_blocks)
    )
    d_key_sum, d_value_sum = (
        lax.psum_scatter(
            d_key_parts.reshape(group_rows, features).astype(jnp.bfloat16),
            "band",
            scatter_dimension=0,
            tiled=True,
        ).astype(jnp.float32),
        lax.psum_scatter(
            d_value_parts.reshape(group_rows, features).astype(jnp.bfloat16),
            "band",
            scatter_dimension=0,
            tiled=True,
        ).astype(jnp.float32),
    )
    d_query = (d_query_sum.reshape(tok_rows, features) * score_scale).astype(jnp.bfloat16)
    d_key = d_key_sum.astype(jnp.bfloat16)
    d_value = d_value_sum.astype(jnp.bfloat16)
    d_query_shift = jnp.sum(d_query.astype(jnp.float32), 0)
    d_value_shift = jnp.sum(d_value.astype(jnp.float32), 0)
    d_project_rows = jnp.concatenate([d_query, d_key, d_value], 1)
    d_project = jnp.einsum(
        "ti,to->io", normed_first, d_project_rows, preferred_element_type=jnp.float32
    )
    d_normed_first = jnp.einsum(
        "to,io->ti", d_project_rows, project_back, preferred_element_type=jnp.float32
    )
    unused_first, first_back = jax.vjp(
        norm_rows, embedded, first_gain_back.astype(jnp.float32), first_shift.astype(jnp.float32)
    )
    d_embed_part, d_gain_first, d_shift_first = first_back(d_normed_first)
    d_embedded = d_middle + d_embed_part
    d_table = jnp.einsum("tl,td->ld", lead_pick, d_embedded, precision=lax.Precision.HIGHEST)
    shards = (
        lax.psum_scatter(d_table, ("band", "grp"), scatter_dimension=1, tiled=True),
        lax.psum_scatter(d_gain_first, ("band", "grp"), scatter_dimension=0, tiled=True),
        lax.psum_scatter(d_shift_first, ("band", "grp"), scatter_dimension=0, tiled=True),
        lax.psum_scatter(d_project, ("band", "grp"), scatter_dimension=0, tiled=True),
        lax.psum_scatter(d_query_shift, ("band", "grp"), scatter_dimension=0, tiled=True),
        lax.psum_scatter(d_value_shift, ("band", "grp"), scatter_dimension=0, tiled=True),
        lax.psum_scatter(d_out_full, ("band", "grp"), scatter_dimension=0, tiled=True),
        lax.psum_scatter(d_out_shift, ("band", "grp"), scatter_dimension=0, tiled=True),
        lax.psum_scatter(d_gain_second, ("band", "grp"), scatter_dimension=0, tiled=True),
        lax.psum_scatter(d_shift_second, ("band", "grp"), scatter_dimension=0, tiled=True),
        lax.psum_scatter(d_up, ("band", "grp"), scatter_dimension=0, tiled=True),
        lax.psum_scatter(d_up_shift, ("band", "grp"), scatter_dimension=0, tiled=True),
        lax.psum_scatter(d_down, ("band", "grp"), scatter_dimension=0, tiled=True),
        lax.psum_scatter(d_down_shift, ("band", "grp"), scatter_dimension=0, tiled=True),
    )
    return (layer_out, d_embedded[None]) + tuple(shards)


DEPTH = 4
PLANE = 4
BIG = 1e30
HBM = pltpu.MemorySpace.HBM
VMEM = pltpu.MemorySpace.VMEM
SMEM = pltpu.MemorySpace.SMEM
LEADS = 16
ROW_G1, ROW_B1, ROW_QB, ROW_VB, ROW_OB, ROW_G2, ROW_B2, ROW_DB = range(16, 24)
VEC_ROWS = 24


def mul(left, right, over_left, over_right):
    return lax.dot_general(
        left, right, (((over_left,), (over_right,)), ((), ())), preferred_element_type=jnp.float32
    )


class Mover:
    def __init__(self, sems):
        self.sems, self.used, self.open = sems, 0, []

    def start(self, source, target):
        copy = pltpu.make_async_copy(source, target, self.sems.at[self.used])
        self.used += 1
        copy.start()
        self.open.append(copy)
        return copy

    def wait(self, copies=None):
        for copy in list(self.open if copies is None else copies):
            copy.wait()
            self.open = [other for other in self.open if other is not copy]


class Far:
    def __init__(self, value):
        self.value = value


class Raw(Far):
    pass


class Given:
    def __init__(self, ref, held, mover):
        self.ref, self.mover, self.copy = held, mover, mover.start(ref, held)
        self.shape, self.dtype = ref.shape, ref.dtype

    def ready(self):
        if self.copy is not None:
            self.mover.wait([self.copy])
            self.copy = None
        return self.ref

    def __getitem__(self, at):
        return self.ready()[at]


def run(order, kernel, outs, ins, scratch=(), after=(), alias=None):
    after = list(after) + order
    kinds = [type(a) if isinstance(a, Far) else None for a in ins]
    ins = [a.value if kind else a for a, kind in zip(ins, kinds)]
    staged = [pltpu.VMEM(a.shape, a.dtype) for a, kind in zip(ins, kinds) if kind is Far]
    outs = [o if len(o) == 3 else o + ("",) for o in outs]
    staged += [pltpu.VMEM(o[0], o[1]) for o in outs if o[2] == "far"]
    n_in, n_after, n_out, n_staged = len(ins), len(after), len(outs), len(staged)
    name = getattr(kernel, "func", kernel).__name__
    micros, room = COSTS[name]
    cost = pl.CostEstimate(flops=micros * 1_100_000_000, bytes_accessed=micros * 3_600_000, transcendentals=0)

    def body(*refs):
        mover = Mover(refs[-1])
        held = list(refs[len(refs) - 1 - n_staged : -1])
        given = [
            Given(ref, held.pop(0), mover) if kind is Far else ref for ref, kind in zip(refs[:n_in], kinds)
        ]
        refs = refs[n_in + n_after : len(refs) - 1 - n_staged]
        made = [held.pop(0) if o[2] == "far" else ref for ref, o in zip(refs, outs)]
        kernel(mover, *given, *made, *refs[n_out + 1 :])
        for ref, written, o in zip(refs, made, outs):
            if o[2] == "far":
                mover.start(written, ref)
        for operand in given:
            if isinstance(operand, Given):
                operand.ready()
        refs[n_out][...] = jnp.zeros_like(refs[n_out])
        mover.wait()

    spaces = [pl.ANY if kind else SMEM if a.dtype == jnp.int32 and a.ndim == 1 else VMEM for a, kind in zip(ins, kinds)]
    results = pl.pallas_call(
        body,
        name=name,
        out_shape=[HBM(o[0], o[1]) if o[2] else jax.ShapeDtypeStruct(o[0], o[1]) for o in outs]
        + [jax.ShapeDtypeStruct((8, 128), f32)],
        in_specs=[pl.BlockSpec(memory_space=space) for space in spaces + [pl.ANY] * n_after],
        out_specs=[pl.BlockSpec(memory_space=pl.ANY if o[2] else VMEM) for o in outs] + [pl.BlockSpec(memory_space=VMEM)],
        scratch_shapes=[pltpu.VMEM(s, d) for s, d in scratch] + staged + [pltpu.SemaphoreType.DMA((64,))],
        compiler_params=pltpu.CompilerParams(vmem_limit_bytes=room << 20),
        cost_estimate=cost,
        input_output_aliases=dict([alias] if alias else []),
    )(
        *[pltpu.with_memory_space_constraint(a, HBM) if kind else a for a, kind in zip(ins, kinds)],
        *[pltpu.with_memory_space_constraint(a, HBM) if a.size > 4096 else a for a in after],
    )
    order[:] = results[n_out:]
    return results[:n_out]


def row_stats(values):
    mean = jnp.mean(values, -1, keepdims=True)
    centred = values - mean
    inv = lax.rsqrt(jnp.mean(centred * centred, -1, keepdims=True) + epsilon)
    return centred * inv, inv


def norm_back(d_normal, normal, inv):
    first = jnp.mean(d_normal, -1, keepdims=True)
    second = jnp.mean(d_normal * normal, -1, keepdims=True)
    return inv * (d_normal - first - normal * second)


def lead_hot(lead, seg_row):
    seg = seg_row[...]
    found = jnp.zeros_like(seg)
    for slot in range(lead.shape[0]):
        found = jnp.where(seg == slot, lead[slot], found)
    slots = lax.broadcasted_iota(jnp.int32, (LEADS, seg.shape[1]), 0)
    return jnp.where(slots == found, 1.0, 0.0).astype(bf16)


def vec_row(vec, row):
    return vec[row : row + 1, :].astype(f32)


def q_prep_kernel(mover, pos, qkv, table, g1, b1, qb, vb, ob, g2, b2, db, ub, up, out_rows, down, o0, o1, o2, o3, cols, first):
    outs = (o0, o1, o2, o3)
    z = pos[0]
    rw = qkv.shape[0]
    d = qkv.shape[1] // 3
    width = d // DEPTH
    side = outs[0].shape[1] - 3 * width

    def wide(values):
        values = values.astype(f32)
        return jnp.concatenate([values, jnp.zeros((values.shape[0], side - values.shape[1]), f32)], 1)

    rows = [wide(table[...])] + [wide(v[...].reshape(1, -1)) for v in (g1, b1, qb, vb, ob, g2, b2, db)]
    rows += [ub[...].reshape(1, -1).astype(f32), jnp.zeros((rw - VEC_ROWS - 1, side), f32)]
    small = jnp.concatenate(rows, 0).astype(bf16)
    for u, out in enumerate(outs):
        for part in range(3):
            start = pl.multiple_of(part * d + (z ^ u) * width, width)
            out[:, part * width : (part + 1) * width] = qkv[:, pl.ds(start, width)]
        out[:, 3 * width :] = small
    fr = up.shape[1] // (DEPTH * PLANE * 2)
    for k in range(PLANE):
        for c in range(2):
            for zz in range(DEPTH):
                src = ((zz * PLANE + k) * 2 + c) * fr
                dst = (c * DEPTH + zz) * fr
                cols[k, :, dst : dst + fr] = up[:, src : src + fr]
    first[0] = out_rows[...]
    first[1] = down[0:rw, :]


def q_stack_kernel(mover, pos, b0, b1, b2, b3, out):
    for u, block in enumerate((b0, b1, b2, b3)):
        mover.start(block, out.at[pos[0] ^ u])


def qkv_kernel(mover, pos, lead, seg_row, toks, *refs):
    z, yx, c = pos[0], pos[1], pos[2]
    qa, qc, (ups, down, shard, n1, w_out, vec, up_b, o0, o1, o2, o3, w, proj) = refs[:4], refs[4:8], refs[8:]
    rows, d = toks.shape[1:]
    width = d // DEPTH
    head = width // PLANE
    rw = w.shape[3]
    fr = w.shape[4] - 3 * width
    pending = [mover.start(qa[k], w.at[:, yx ^ k, c]) for k in range(PLANE)]
    pending += [mover.start(qc[k], w.at[:, yx ^ k, 1 - c]) for k in range(PLANE)]
    shard[0:PLANE] = ups[...]
    shard[PLANE:] = down[shard.shape[1] :, :].reshape(PLANE - 1, -1, down.shape[1])
    mover.wait(pending)
    mover.start(w.at[:, :, :, :, 0 : 3 * width], w_out)
    for zz in range(DEPTH):
        for k in range(PLANE):
            for core in range(2):
                i = (zz * PLANE + k) * 2 + core
                side = w[zz, k, core, :, 3 * width :].astype(f32)
                vec[:, i * rw : (i + 1) * rw] = side[0:VEC_ROWS, 0:rw]
        for core in range(2):
            side = w[zz, yx, core, :, 3 * width :].astype(f32)
            start = (core * DEPTH + zz) * fr
            up_b[:, start : start + fr] = side[VEC_ROWS : VEC_ROWS + 1, :]
    shift = mul(lead_hot(lead, seg_row), vec[0:LEADS, :].astype(bf16), 0, 0)
    gain, bias = vec_row(vec, ROW_G1), vec_row(vec, ROW_B1)
    for s in range(DEPTH):
        normal, _ = row_stats(toks[z ^ s].astype(f32) + shift)
        n1[s * rows : (s + 1) * rows, :] = (normal * gain + bias).astype(bf16)
    at = pl.ds(pl.multiple_of(z * width, width), width)
    biases = jnp.concatenate(
        [vec[ROW_QB : ROW_QB + 1, at], jnp.zeros((1, width), f32), vec[ROW_VB : ROW_VB + 1, at]], 1
    )
    first = lax.broadcasted_iota(jnp.int32, (8, 3 * width), 0) == 0
    biases = jnp.where(first, biases, 0.0).astype(bf16)
    ones = jnp.ones((8, DEPTH * rows), bf16)
    weight = w[:, :, :, :, 0 : 3 * width].reshape(d, 3 * width)
    found = mul(weight, n1[...], 0, 1) + mul(biases, ones, 0, 0)
    proj[...] = found.astype(bf16).reshape(proj.shape)
    for k, out in enumerate((o0, o1, o2, o3)):
        for part in range(3):
            mover.start(proj.at[part * PLANE + (yx ^ k)], out.at[part * head : (part + 1) * head])


def fill_heads(seg_row, count, blocks, qa, ka, vt):
    head = blocks[0].shape[0] // 3
    span = blocks[0].shape[1]
    seg = jnp.concatenate([seg_row[...]] * (span // seg_row.shape[1]), 1)
    slots = lax.broadcasted_iota(jnp.int32, (16, span), 0)
    hot, real = jnp.where(slots == seg, 1.0, 0.0), slots < count
    q_mark = jnp.where(real, (hot - 1.0) * BIG, 0.0).astype(bf16)
    k_mark = jnp.where(real, hot, 0.0).astype(bf16)
    rest = qa.shape[0] - head - 16
    for k, block in enumerate(blocks):
        cols = slice(k * span, (k + 1) * span)
        qa[0:head, cols] = block[0:head, :] * jnp.asarray(score_scale, bf16)
        qa[head : head + 16, cols] = q_mark
        qa[head + 16 :, cols] = jnp.zeros((rest, span), bf16)
        keys = jnp.concatenate([block[head : 2 * head, :], k_mark, jnp.zeros((rest, span), bf16)], 0)
        ka[cols, :] = keys.T
        vt[:, cols] = block[2 * head :, :]


def attend_kernel(count, mover, seg_row, b0, b1, b2, b3, o0, o1, o2, o3, lse, qa, ka, vt):
    fill_heads(seg_row, count, (b0, b1, b2, b3), qa, ka, vt)
    span = b0.shape[1]
    rows = seg_row.shape[1]
    outs = (o0, o1, o2, o3)

    def step(k, carry):
        for half in range(DEPTH // 2):
            at = pl.ds(pl.multiple_of(k * span + half * 2 * rows, 2 * rows), 2 * rows)
            scores = mul(ka[...], qa[:, at], 1, 0)
            top = jnp.max(scores, 0, keepdims=True)
            soft = jnp.exp(scores - top)
            total = jnp.sum(soft, 0, keepdims=True)
            found = mul(vt[...], soft.astype(bf16), 1, 0) / total
            lse[:, at] = jnp.broadcast_to(top + jnp.log(total), (8, 2 * rows))
            for i in range(2):
                outs[half * 2 + i][:, pl.ds(pl.multiple_of(k * rows, rows), rows)] = found[
                    :, i * rows : (i + 1) * rows
                ].astype(bf16)
        return carry

    lax.fori_loop(0, PLANE, step, 0)


def out_kernel(mover, pos, a0, a1, a2, a3, first, p0, p1, p2, p3, att, w_out):
    z = pos[0]
    head = a0.shape[0]
    rows, d = p0.shape
    pending = [mover.start(first.at[:, :, 0], w_out)]
    for u, block in enumerate((a0, a1, a2, a3)):
        att[pl.ds(pl.multiple_of((z ^ u) * head, head), head), :] = block[...]
    mover.wait(pending)
    found = mul(att[...], w_out[...].reshape(-1, d), 0, 0)
    for j, out in enumerate((p0, p1, p2, p3)):
        out[...] = found[j * rows : (j + 1) * rows, :].astype(out.dtype)


def norm_kernel(mover, lead, seg_row, vec, tok, p0, p1, p2, p3, middle, n2):
    shift = mul(lead_hot(lead, seg_row), vec[0:LEADS, :].astype(bf16), 0, 0) + vec_row(vec, ROW_OB)
    total = p0[...].astype(f32) + p1[...].astype(f32) + p2[...].astype(f32) + p3[...].astype(f32)
    total = tok[...].astype(f32) + shift + total
    middle[...] = total
    normal, _ = row_stats(total)
    n2[...] = (normal * vec_row(vec, ROW_G2) + vec_row(vec, ROW_B2)).astype(bf16)


def down_copies(mover, first, ff, w_down):
    copies = [mover.start(first.at[:, c, 1], w_down.at[c, :, 0]) for c in range(2)]
    return copies + [mover.start(ff.at[:, c, PLANE:], w_down.at[c, :, 1:]) for c in range(2)]


def ffn_kernel(mover, pos, up_b, n0, n1, n2, n3, d_outs, first, ff, act, d_hid, p0, p1, p2, p3, d_up_b, w_up, w_down, hid):
    yx = pos[1]
    rows, d = n0.shape
    for_up = [mover.start(ff.at[:, c, 0:PLANE], w_up.at[:, :, c]) for c in range(2)]
    for_down = down_copies(mover, first, ff, w_down)
    mover.wait(for_up)
    normed = jnp.concatenate([n0[...], n1[...], n2[...], n3[...]], 0)
    up = w_up[...].reshape(d, -1)
    hid[...] = mul(normed, up, 1, 0) + up_b[...].astype(f32)
    mover.wait(for_down)
    down = w_down[...].reshape(-1, d)
    sums = jnp.zeros(d_up_b.shape, f32)
    for j in range(PLANE):
        here = slice(j * rows, (j + 1) * rows)
        hidden = hid[here, :]
        phi = 0.5 * (1.0 + lax.erf(hidden * 0.7071067811865476))
        act[here, :] = (hidden * phi).astype(bf16)
        slope = phi + hidden * (jnp.exp(-0.5 * hidden * hidden) * 0.3989422804014327)
        d_act = mul(d_outs[yx ^ j], down, 1, 1)
        low = (d_act * slope).astype(bf16)
        d_hid[here, :] = low
        sums = sums + jnp.sum(low.astype(f32), 0, keepdims=True)
    d_up_b[...] = sums
    back = mul(d_hid[...], up, 1, 1)
    for j, out in enumerate((p0, p1, p2, p3)):
        out[...] = back[j * rows : (j + 1) * rows, :].astype(out.dtype)


def ffn_grad_kernel(mover, pos, act, d_hid, n0, n1, n2, n3, first, ff, d_outs, grads, outs, up_grad, down_grad, w_down):
    yx = pos[1]
    rows, d = outs.shape[1:]
    pending = down_copies(mover, first, ff, w_down)
    normed = jnp.concatenate([n0[...], n1[...], n2[...], n3[...]], 0)
    up_grad[...] = mul(normed, d_hid[...], 0, 0).astype(bf16).reshape(up_grad.shape)
    for c in range(2):
        mover.start(up_grad.at[:, :, c], grads.at[:, c, 0:PLANE])
    d_down = jnp.zeros((act.shape[1], d), f32)
    for j in range(PLANE):
        d_down = d_down + mul(act[j * rows : (j + 1) * rows, :], d_outs[yx ^ j], 0, 0)
    down_grad[...] = d_down.astype(bf16).reshape(down_grad.shape)
    for c in range(2):
        mover.start(down_grad.at[c], grads.at[:, c, PLANE : 2 * PLANE])
    mover.wait(pending)
    found = mul(act[...], w_down[...].reshape(-1, d), 1, 0)
    for j in range(PLANE):
        outs[yx ^ j] = found[j * rows : (j + 1) * rows, :].astype(bf16)


def ffn_last_kernel(mover, shard, ups, down, out_rows):
    ups[...] = shard[0:PLANE]
    down[...] = shard[PLANE : 2 * PLANE].astype(f32).reshape(down.shape)
    out_rows[...] = shard[2 * PLANE].astype(f32)


def branch_kernel(mover, vec, middle, d_out, p0, p1, p2, p3, d_mid, d_branch, d_vec):
    dy = p0[...].astype(f32) + p1[...].astype(f32) + p2[...].astype(f32) + p3[...].astype(f32)
    normal, inv = row_stats(middle[...])
    d_rows = d_out[...].astype(f32)
    total = d_rows + norm_back(dy * vec_row(vec, ROW_G2), normal, inv)
    d_mid[...] = total
    low = total.astype(bf16)
    d_branch[...] = low
    sums = [jnp.sum(v, 0, keepdims=True) for v in (dy * normal, dy, d_rows, low.astype(f32))]
    d_vec[...] = jnp.concatenate(sums + [jnp.zeros((4, dy.shape[1]), f32)], 0)


def out_back_kernel(mover, pos, att, w_out, b0, b1, b2, b3, others, o0, o1, o2, o3, grads, d_att, grad):
    z = pos[0]
    head = o0.shape[0]
    branch = jnp.concatenate([b0[...], b1[...], b2[...], b3[...]], 0)
    d = branch.shape[1]
    d_att[...] = mul(w_out[...].reshape(-1, d), branch, 1, 1).astype(bf16).reshape(d_att.shape)
    for u, out in enumerate((o0, o1, o2, o3)):
        out[...] = d_att[z ^ u]
    grad[...] = mul(att[...], branch, 1, 0).astype(bf16).reshape(grad.shape)
    mover.start(grad, grads.at[:, :, 2 * PLANE])


def attend_back_kernel(count, mover, seg_row, b0, b1, b2, b3, c0, c1, c2, c3, lse,
                       o0, o1, o2, o3, qa, ka, vt, vn, dot, dq, dk, dv, kt):
    fill_heads(seg_row, count, (b0, b1, b2, b3), qa, ka, vt)
    span = b0.shape[1]
    rows = seg_row.shape[1]
    head = vt.shape[0]
    for k, block in enumerate((b0, b1, b2, b3)):
        cols = slice(k * span, (k + 1) * span)
        vn[cols, :] = vt[:, cols].T
        kt[:, cols] = block[head : 2 * head, :]
        for s, block in enumerate((c0, c1, c2, c3)):
            dot[:, k * span + s * rows : k * span + (s + 1) * rows] = block[:, k * rows : (k + 1) * rows]
    dk[...] = jnp.zeros_like(dk)
    dv[...] = jnp.zeros_like(dv)
    logs = lse

    def step(i, carry):
        for k in (2 * i, 2 * i + 1):
            at = pl.ds(pl.multiple_of(k * span, span), span)
            scores = mul(ka[...], qa[:, at], 1, 0)
            soft = jnp.exp(scores - logs[0:1, at])
            d_out = dot[:, at]
            d_soft = mul(vn[...], d_out, 1, 0)
            delta = jnp.sum(soft * d_soft, 0, keepdims=True)
            d_scores = (soft * (d_soft - delta)).astype(bf16)
            dv[...] += mul(d_out, soft.astype(bf16), 1, 1)
            dk[...] += mul(qa[0:head, at], d_scores, 1, 1)
            dq[:, at] = (mul(kt[...], d_scores, 1, 0) * score_scale).astype(bf16)
        return carry

    lax.fori_loop(0, PLANE // 2, step, 0)
    for k, out in enumerate((o0, o1, o2, o3)):
        cols = slice(k * span, (k + 1) * span)
        out[0:head, :] = dq[:, cols]
        out[head : 2 * head, :] = dk[:, cols].astype(bf16)
        out[2 * head :, :] = dv[:, cols].astype(bf16)


def join_heads(yx, blocks, joined):
    head = blocks[0].shape[0] // 3
    for k, block in enumerate(blocks):
        for part in range(3):
            joined[part * PLANE + (yx ^ k)] = block[part * head : (part + 1) * head, :]
    return joined[...].reshape(3 * PLANE * head, -1)


def qkv_back_kernel(mover, pos, lead, seg_row, vec, toks, n1, w, g0, g1, g2, g3, d_mid, d_mid_vec, d_up_b,
                    r0, r1, r2, r3, mine, o0, o1, joined, d_vec, both):
    z, yx, core = pos[0], pos[1], pos[2]
    rows, d = r0.shape
    width = d // DEPTH
    head = width // PLANE
    rw = mine.shape[2]
    cols = 3 * width
    fr = mine.shape[3] - cols
    for k, block in enumerate((g0, g1, g2, g3)):
        for part in range(3):
            joined[part * PLANE + (yx ^ k)] = block[part * head : (part + 1) * head, :]
    grads = joined[...].reshape(cols, DEPTH * rows)
    grad = mul(n1[...], grads, 0, 1).astype(bf16)
    back = mul(grads, w[...].reshape(d, cols), 0, 1)
    hot = lead_hot(lead, seg_row)
    shift = mul(hot, vec[0:LEADS, :].astype(bf16), 0, 0)
    gain = vec_row(vec, ROW_G1)
    d_gain = jnp.zeros((1, d), f32)
    d_bias = jnp.zeros((1, d), f32)
    d_emb = d_mid[...]
    for s, out in enumerate((r0, r1, r2, r3)):
        piece = back[s * rows : (s + 1) * rows, :]
        out[...] = piece.astype(out.dtype)
        normal, inv = row_stats(toks[z ^ s].astype(f32) + shift)
        d_gain = d_gain + jnp.sum(piece * normal, 0, keepdims=True)
        d_bias = d_bias + jnp.sum(piece, 0, keepdims=True)
        d_emb = d_emb + norm_back(piece * gain, normal, inv)
    high = d_emb.astype(bf16)
    low = (d_emb - high.astype(f32)).astype(bf16)
    d_vec[...] = jnp.zeros_like(d_vec)
    d_vec[0:LEADS, :] = mul(hot, high, 1, 0) + mul(hot, low, 1, 0)
    sums = mul(jnp.ones((8, DEPTH * rows), bf16), grads, 1, 1)
    d_vec[ROW_G1 : ROW_G1 + 1, :] = d_gain
    d_vec[ROW_B1 : ROW_B1 + 1, :] = d_bias
    at = pl.ds(pl.multiple_of(z * width, width), width)
    d_vec[ROW_QB : ROW_QB + 1, at] = sums[0:1, 0:width]
    d_vec[ROW_VB : ROW_VB + 1, at] = sums[0:1, 2 * width :]
    for i, row in enumerate((ROW_G2, ROW_B2, ROW_DB, ROW_OB)):
        d_vec[row : row + 1, :] = d_mid_vec[i : i + 1, :]
    small = d_vec[...]
    mark = lax.broadcasted_iota(jnp.int32, (rw, fr), 0) == VEC_ROWS
    for zz in range(DEPTH):
        for k in range(PLANE):
            for c in range(2):
                i = (zz * PLANE + k) * 2 + c
                side = jnp.concatenate([small[:, i * rw : (i + 1) * rw], jnp.zeros((rw, fr - rw), f32)], 1)
                start = (c * DEPTH + zz) * fr
                last = jnp.where(yx == k, d_up_b[:, start : start + fr], 0.0)
                side = jnp.where(mark, last, side).astype(bf16)
                both[zz, k, c] = jnp.concatenate([grad[i * rw : (i + 1) * rw, :], side], 1)
    mover.start(both.at[0:2, :, 1 - core], o0)
    mover.start(both.at[2:4, :, 1 - core], o1)
    mover.start(both.at[:, :, core], mine)


def first_back_kernel(mover, lead, seg_row, vec, tok, d_mid, r0, r1, r2, r3, out):
    shift = mul(lead_hot(lead, seg_row), vec[0:LEADS, :].astype(bf16), 0, 0)
    normal, inv = row_stats(tok[...].astype(f32) + shift)
    dy = r0[...].astype(f32) + r1[...].astype(f32) + r2[...].astype(f32) + r3[...].astype(f32)
    out[...] = d_mid[...] + norm_back(dy * vec_row(vec, ROW_G1), normal, inv)


def layer_out_kernel(mover, vec, middle, blocks, out):
    total = middle[...] + vec_row(vec, ROW_DB)
    for k in range(PLANE):
        total = total + blocks[k].astype(f32)
    out[...] = total.astype(bf16)


def pair_kernel(mover, pos, mine, o0, o1, p0, p1, p2, p3, total):
    yx = pos[1]
    total[0:2] = (mine[0:2].astype(f32) + o0[...].astype(f32)).astype(bf16)
    total[2:4] = (mine[2:4].astype(f32) + o1[...].astype(f32)).astype(bf16)
    for k, out in enumerate((p0, p1, p2, p3)):
        mover.start(total.at[:, yx ^ k], out)


def quad_kernel(mover, pos, b0, b1, b2, b3, o0, o1, o2, o3, total):
    found = b0[...].astype(f32) + b1[...].astype(f32) + b2[...].astype(f32) + b3[...].astype(f32)
    total[...] = found.astype(bf16)
    for u, out in enumerate((o0, o1, o2, o3)):
        out[...] = total[pos[0] ^ u]


def qkv_join_kernel(mover, pos, b0, b1, b2, b3, out, table, *rest):
    z = pos[0]
    rw = out.shape[0]
    width = out.shape[1] // (3 * DEPTH)
    side = jnp.zeros((rw, b0.shape[1] - 3 * width), f32)
    for s, block in enumerate((b0, b1, b2, b3)):
        for part in range(3):
            start = pl.multiple_of((part * DEPTH + (z ^ s)) * width, width)
            out[:, pl.ds(start, width)] = block[:, part * width : (part + 1) * width].astype(f32)
        side = side + block[:, 3 * width :].astype(f32)
    table[...] = side[0:LEADS, 0:rw]
    for i, row in enumerate(rest[:-1]):
        row[...] = side[LEADS + i : LEADS + i + 1, 0:rw].reshape(rw)
    rest[-1][...] = side[VEC_ROWS : VEC_ROWS + 1, :].reshape(-1)


def up_join_kernel(mover, blocks, out):
    fr = blocks.shape[2] // (2 * DEPTH)
    for k in range(PLANE):
        for c in range(2):
            for zz in range(DEPTH):
                src = (c * DEPTH + zz) * fr
                dst = ((zz * PLANE + k) * 2 + c) * fr
                out[:, dst : dst + fr] = blocks[k, :, src : src + fr].astype(f32)


COSTS = {
    "q_prep_kernel": (3, 6), "q_stack_kernel": (1, 4), "up_prep_kernel": (1, 4),  "first_shard_kernel": (1, 4), "qkv_kernel": (5, 20),
    "attend_kernel": (9, 24), "out_kernel": (2, 12), "norm_kernel": (2, 8), "ffn_kernel": (8, 32), "ffn_grad_kernel": (8, 32),
    "branch_kernel": (2, 12), "out_back_kernel": (3, 12), "attend_back_kernel": (15, 32),
    "qkv_back_kernel": (10, 28), "first_back_kernel": (2, 8), "layer_out_kernel": (1, 8),
    "pair_kernel": (2, 8), "quad_kernel": (1, 8), "qkv_join_kernel": (1, 4), "up_join_kernel": (2, 8), "ffn_last_kernel": (1, 8),
}
PLANE_AXES = ("y", "x")


def trade(blocks, axes):
    return lax.all_to_all(blocks, axes, split_axis=0, concat_axis=0, tiled=True)


ALL = ("z", "y", "x", "g")


def across(blocks):
    swap = [(0, 1), (1, 0)]
    return (
        blocks[0],
        lax.ppermute(blocks[1], "x", swap),
        lax.ppermute(blocks[2], "y", swap),
        lax.ppermute(blocks[3], ("y", "x"), [(i, i ^ 3) for i in range(PLANE)]),
    )


def to_depth(block, step):
    return lax.ppermute(block, "z", [(i, i ^ step) for i in range(DEPTH)])


def along(blocks):
    return (blocks[0],) + tuple(to_depth(blocks[u], u) for u in range(1, DEPTH))


def core_swap(block):
    return lax.ppermute(block, "g", [(0, 1), (1, 0)])


def far(blocks):
    return [Far(block) for block in blocks]


def raw(blocks):
    return [Raw(block) for block in blocks]


def fast_local(
    tokens, segment_ids, lead_index, lead_table, ln1_gain, ln1_bias, qkv_weight, q_bias, v_bias,
    out_weight, out_bias, ln2_gain, ln2_bias, up_weight, up_bias, down_weight, down_bias, d_out,
):
    z = lax.axis_index("z")
    yx = lax.axis_index("y") * 2 + lax.axis_index("x")
    c = lax.axis_index("g")
    pos = jnp.stack([z, yx, c]).astype(jnp.int32)
    tok, d_rows = tokens[0], d_out[0]
    rows, d = tok.shape
    head = d // HEADS
    span = DEPTH * rows
    group = PLANE * span
    rw = qkv_weight.shape[0]
    fr = down_weight.shape[0]
    ff = 2 * DEPTH * fr
    lead = lead_index[0]
    count = lead.shape[0]
    width = 3 * d // DEPTH
    seg_row = segment_ids
    up_shape, down_shape = (DEPTH, PLANE, 2, rw, ff), (2, DEPTH, PLANE, rw, d)

    order = []
    call = functools.partial(run, order)
    side = width + -(-max(rw, fr) // 128) * 128

    *q_rows, up_cols, first_shard = call(
        q_prep_kernel,
        [((rw, side), bf16)] * 4 + [((PLANE, rw, ff), bf16), ((2, rw, d), bf16, "far")],
        [pos]
        + far((qkv_weight, lead_table, ln1_gain, ln1_bias, q_bias, v_bias, out_bias, ln2_gain, ln2_bias, down_bias, up_bias))
        + far((up_weight, out_weight, down_weight)),
    )
    q_rows = along(q_rows)
    toks = lax.all_gather(tok, "z", axis=0)
    first = lax.all_gather(first_shard, ("z", "g"), axis=0).reshape(DEPTH, 2, 2, rw, d)
    up_cols = trade(up_cols, PLANE_AXES)
    (q_stack,) = call(q_stack_kernel, [((DEPTH, rw, side), bf16)], [pos, *q_rows], after=[up_cols])
    q_plane = across((q_stack,) * PLANE)
    q_other = [core_swap(block) for block in q_plane]
    ff_shard, n1, w_qkv, vec, up_b, *blocks = call(
        qkv_kernel,
        [((2 * PLANE - 1, rw, d), bf16, "far"), ((span, d), bf16, "far"), ((DEPTH, PLANE, 2, rw, width), bf16, "raw"), ((VEC_ROWS, d), f32), ((1, ff), f32)]
        + [((3 * head, span), bf16)] * 4,
        [pos, lead, seg_row, Far(toks), *q_plane, *q_other, up_cols, Far(down_weight)],
        [((DEPTH, PLANE, 2, rw, side), bf16), ((3 * PLANE, head, span), bf16)],
    )
    ff_all = lax.all_gather(ff_shard, ("z", "g"), axis=0).reshape(DEPTH, 2, 2 * PLANE - 1, rw, d)
    blocks = across(blocks)

    d_outs = trade(jnp.broadcast_to(d_rows[None], (PLANE, rows, d)), PLANE_AXES)
    *att_parts, lse = call(
        functools.partial(attend_kernel, count),
        [((head, PLANE * rows), bf16)] * 4 + [((8, group), f32)],
        [seg_row, *blocks],
        [((128, group), bf16), ((group, 128), bf16), ((head, group), bf16)],
    )
    att_parts = along(att_parts)
    *parts, att, w_out = call(
        out_kernel,
        [((rows, d), f32)] + [((rows, d), bf16)] * 3 + [((DEPTH * head, span), bf16), ((DEPTH, 2, rw, d), bf16)],
        [pos, *att_parts, Raw(first)],
        after=[d_outs],
    )
    parts = across(parts)
    middle, n2 = call(norm_kernel, [((rows, d), f32, "far"), ((rows, d), bf16)], [lead, seg_row, vec, Far(tok), *parts])
    n2_plane = across((n2,) * PLANE)

    act, d_hid, p0, p1, p2, p3, d_up_b = call(
        ffn_kernel,
        [((span, ff), bf16), ((span, ff), bf16), ((rows, d), f32)] + [((rows, d), bf16)] * 3 + [((1, ff), f32)],
        [pos, up_b, *n2_plane, Far(d_outs), Raw(first), Raw(ff_all)],
        [(up_shape, bf16), (down_shape, bf16), ((span, ff), f32)],
    )
    parts = across((p0, p1, p2, p3))
    ff_grad, outs = call(
        ffn_grad_kernel,
        [((DEPTH, 2, 2 * PLANE + 1, rw, d), bf16, "raw"), ((PLANE, rows, d), bf16, "far")],
        [pos, act, d_hid, *n2_plane, Raw(first), Raw(ff_all), Far(d_outs)],
        [(up_shape, bf16), (down_shape, bf16), (down_shape, bf16)],
    )
    d_mid, d_branch, d_mid_vec = call(
        branch_kernel,
        [((rows, d), f32, "far"), ((rows, d), bf16), ((8, d), f32)],
        [vec, Far(middle), Far(d_rows), *parts],
    )
    branch_plane = across((d_branch,) * PLANE)
    *d_att, ff_grad = call(
        out_back_kernel,
        [((head, span), bf16)] * 4 + [(ff_grad.shape, bf16, "raw")],
        [pos, att, w_out, *branch_plane, Raw(ff_grad)],
        [((DEPTH, head, span), bf16), ((DEPTH, 2, rw, d), bf16)],
        alias=(7, 4),
    )
    d_att = along(d_att)
    ff_grad = lax.psum_scatter(
        ff_grad.reshape(2 * DEPTH, 2 * PLANE + 1, rw, d), ("z", "g"), scatter_dimension=0, tiled=True
    )[0]
    outs = trade(outs, PLANE_AXES)

    d_blocks = call(
        functools.partial(attend_back_kernel, count),
        [((3 * head, span), bf16)] * 4,
        [seg_row, *blocks, *d_att, lse],
        [((128, group), bf16), ((group, 128), bf16), ((head, group), bf16), ((group, head), bf16),
         ((head, group), bf16), ((head, group), bf16), ((head, group), f32), ((head, group), f32), ((head, group), bf16)],
    )
    d_blocks = across(d_blocks)
    (layer_out,) = call(layer_out_kernel, [((rows, d), bf16)], [vec, Far(middle), outs])
    r0, r1, r2, r3, mine, o0, o1 = call(
        qkv_back_kernel,
        [((rows, d), f32)] + [((rows, d), bf16)] * 3
        + [((DEPTH, PLANE, rw, side), bf16)] + [((DEPTH // 2, PLANE, rw, side), bf16)] * 2,
        [pos, lead, seg_row, vec, Far(toks), Far(n1), Far(w_qkv), *d_blocks, Far(d_mid), d_mid_vec, d_up_b],
        [((3 * PLANE, head, span), bf16), ((rw, d), f32), ((DEPTH, PLANE, 2, rw, side), bf16)],
    )
    returned = along((r0, r1, r2, r3))
    quads = across(
        call(
            pair_kernel,
            [((DEPTH, rw, side), bf16)] * 4,
            [pos, mine, core_swap(o0), core_swap(o1)],
            [((DEPTH, PLANE, rw, side), bf16)],
        )
    )
    cols = along(call(quad_kernel, [((rw, side), bf16)] * 4, [pos, *quads], [((DEPTH, rw, side), bf16)]))
    ups, d_down, d_out_weight = call(
        ffn_last_kernel, [((PLANE, rw, ff), bf16), ((fr, d), f32), ((rw, d), f32)], [ff_grad]
    )
    ups = trade(ups, PLANE_AXES)
    (d_tokens,) = call(
        first_back_kernel, [((rows, d), f32)], [lead, seg_row, vec, Far(tok), Far(d_mid), *returned]
    )
    d_qkv, table, d_g1, d_b1, d_qb, d_vb, d_ob, d_g2, d_b2, d_db, d_ub = call(
        qkv_join_kernel,
        [((rw, 3 * d), f32), ((LEADS, rw), f32)] + [((rw,), f32)] * 8 + [((fr,), f32)],
        [pos, *cols],
    )
    (d_up,) = call(up_join_kernel, [((rw, PLANE * ff), f32)], [ups])
    return (
        layer_out[None], d_tokens[None], table, d_g1, d_b1, d_qkv, d_qb, d_vb, d_out_weight, d_ob,
        d_g2, d_b2, d_up, d_ub, d_down, d_db,
    )


def specs(band, grp):
    every = band + grp
    rows = P(grp, band, None)
    in_specs = (
        rows, P(grp, band), P(grp, None), P(None, every), P(every), P(every), P(every, None), P(every), P(every),
        P(every, None), P(every), P(every), P(every), P(every, None), P(every), P(every, None), P(every), rows,
    )
    out_specs = (
        rows, rows, P(None, every), P(every), P(every), P(every, None), P(every), P(every), P(every, None), P(every),
        P(every), P(every), P(every, None), P(every), P(every, None), P(every),
    )
    return in_specs, out_specs


def solution(mesh):
    band, grp = mesh.shape["band"], mesh.shape["grp"]
    if band == HEADS and grp == 2:
        mesh = Mesh(mesh.devices.reshape(DEPTH, 2, 2, grp), ("z", "y", "x", "g"))
        in_specs, out_specs = specs(("z", "y", "x"), ("g",))
        return jax.shard_map(fast_local, mesh=mesh, in_specs=in_specs, out_specs=out_specs, check_vma=False)
    in_specs, out_specs = specs(("band",), ("grp",))
    return jax.shard_map(local, mesh=mesh, in_specs=in_specs, out_specs=out_specs, check_vma=False)
```
